32 devices in a mesh: grp: 2 (over x), wave: 16 (over z, y, core).
Axes of the slice: x: 2, y: 2, z: 4, core: 2. Of those that a mesh axis runs over, the one named last changes fastest.
Arguments:
- wave_pairs: int32 [640], P('wave'), may hold values from 0 to 639, each once
- band_owner: int32 [32], P('wave'), may hold values from 0 to 31, each once
- spectra_even: bfloat16 [640, 641, 256], P('wave', None, 'grp'), parts along dimension 2, may hold values from -0.15625 to 0.15625
- spectra_odd: bfloat16 [640, 640, 256], P('wave', None, 'grp'), parts along dimension 2, may hold values from -0.15625 to 0.15625
- legendre_even: bfloat16 [640, 32, 641], P('wave'), may hold values from -0.25 to 0.25
- legendre_odd: bfloat16 [640, 32, 640], P('wave'), may hold values from -0.25 to 0.25
Outputs:
- grid_values: bfloat16 [32, 2, 128, 2688], P('wave', None, 'grp'), parts along dimension 2
The draws below stay inside these ranges and needn't reach their ends.
There are 2 independent parts, one for each index of `grp`. The reference program is written for one: setup_inputs(seed, part) draws one part's arguments, and reference() takes and returns one part's arrays. A program takes and returns all parts, laid end to end along the dimension named above; an argument that names none is the same for every part. Nothing has to cross between parts.
Inputs may be any that keep to these rules, and one draw needn't show every extreme that they name: `wave_pairs`: each lower wavenumber 0 to 639 stands in exactly one slot. `band_owner`: each latitude pair stands in exactly one slot.
All inputs are finite; a program needn't handle non-finite values.
Results may differ from the reference program's by a relative error of at most 0.0055.
Values may be sent and summed in bfloat16 or wider, within the bound.
No kernel may reach another device: no remote copies, remote signals or barrier semaphores. Data moves between devices by JAX's collectives and lax.ppermute only.
A program may use at most 64 MiB of HBM per device.

```python
import math
import jax
import jax.numpy as jnp
from jax import lax

M = 1280
NLON = 2688
F = 64
NPAIR = 640
HE = 641
HO = 640
LATN = 32


def steps_of(stream_key, extent, pieces, least, top_value):
    loudness = 1.0
    for position, parts in pieces:
        heights = jax.random.uniform(jax.random.fold_in(jax.random.fold_in(stream_key, 6), position), (parts,), jnp.float32, least / len(pieces), top_value / len(pieces))
        loudness = loudness * jnp.repeat(jnp.exp(heights), extent[position] // parts).reshape((-1,) + (1,) * (len(extent) - 1 - position))
    return loudness


def normal_values(rng, extent, spread, reach, pieces=(), kind=jnp.bfloat16):
    loudness = steps_of(rng, extent, pieces, -0.22, 0.18) if pieces else 1.0
    array = jax.random.normal(rng, extent, jnp.float32) * spread * loudness
    return jnp.minimum(jnp.maximum(array, -reach), reach).astype(kind)


def setup_inputs(seed: int = 0, part: int = 0) -> dict:
    keys = jax.random.split(jax.random.key(seed), 7)
    own_keys = jax.random.split(jax.random.fold_in(keys[6], part), 7)
    wave_pairs = jax.random.permutation(keys[0], NPAIR).astype(jnp.int32)
    band_owner = jax.random.permutation(keys[1], LATN).astype(jnp.int32)
    spectra_even = normal_values(own_keys[2], (NPAIR, HE, 2 * F), M ** -0.5, 0.15625, ((0, 16),))
    spectra_odd = normal_values(own_keys[3], (NPAIR, HO, 2 * F), M ** -0.5, 0.15625, ((0, 16),))
    legendre_even = normal_values(keys[4], (NPAIR, LATN, HE), HE ** -0.5, 0.25, ((0, 16),))
    legendre_odd = normal_values(keys[5], (NPAIR, LATN, HO), HO ** -0.5, 0.25, ((0, 16),))
    return {"wave_pairs": wave_pairs, "band_owner": band_owner, "spectra_even": spectra_even, "spectra_odd": spectra_odd, "legendre_even": legendre_even, "legendre_odd": legendre_odd}


def parity_half(panel, spectra, limit_count):
    column_ids = jnp.arange(spectra.shape[0], dtype=jnp.int32)[:, None]
    in_lower = column_ids < limit_count
    zeroed = jnp.zeros_like(spectra)
    masked = jnp.concatenate([jnp.where(in_lower, spectra, zeroed), jnp.where(in_lower, zeroed, spectra)], axis=1)
    return jnp.dot(panel, masked, preferred_element_type=jnp.float32)


def legendre_pair(operands):
    low_wave, panel_even, panel_odd, spectra_even, spectra_odd = operands
    symmetric = parity_half(panel_even, spectra_even, (M - low_wave + 1) // 2)
    antisym = parity_half(panel_odd, spectra_odd, (M - low_wave) // 2)
    north_rows = (symmetric + antisym).astype(jnp.bfloat16)
    south_rows = (symmetric - antisym).astype(jnp.bfloat16)
    return jnp.stack([north_rows, south_rows], axis=1)


def wave_tables(low_wave):
    wavenumbers = jnp.stack([low_wave, M - 1 - low_wave], axis=-1).astype(jnp.int32)
    longitude = jnp.arange(NLON, dtype=jnp.int32)
    residue = (wavenumbers[..., None] * longitude) % NLON
    angles = residue.astype(jnp.float32) * (2.0 * math.pi / NLON)
    factor = jnp.where(wavenumbers == 0, 1.0, 2.0).astype(jnp.float32)[..., None]
    cosine = (factor * jnp.cos(angles)).astype(jnp.bfloat16)
    sine = (-factor * jnp.sin(angles)).astype(jnp.bfloat16)
    return jnp.stack([cosine, sine], axis=-2)


def reference(wave_pairs, band_owner, spectra_even, spectra_odd, legendre_even, legendre_odd):
    fourier_rows = lax.map(legendre_pair, (wave_pairs, legendre_even, legendre_odd, spectra_even, spectra_odd))
    fourier_rows = jnp.take(fourier_rows, band_owner, axis=1)
    pairs_total = fourier_rows.shape[0]
    slots = fourier_rows.shape[1]
    fields = spectra_even.shape[2] // 2
    shaped = fourier_rows.reshape(pairs_total, slots, 2, 2, 2, fields).astype(jnp.float32)
    tables = wave_tables(wave_pairs).astype(jnp.float32)
    summed = jnp.einsum("qshwrf,qwrn->shfn", shaped, tables, precision=lax.Precision.HIGHEST)
    return summed.astype(jnp.bfloat16)
```

```python
import functools
import math

import jax
import jax.numpy as jnp
from jax import lax
from jax.experimental import pallas as pl
from jax.experimental.pallas import tpu as pltpu
from jax.sharding import PartitionSpec as P

M = 1280
NLON = 2688
HALF = NLON // 2
ROWS = 8
LANES = 128


def round_up(value, unit):
    return -(-value // unit) * unit


def legendre_kernel(waves_ref, se_ref, so_ref, le_ref, lo_ref, out_ref, columns_ref, rows_ref):
    lats = le_ref.shape[1]
    he, ho = le_ref.shape[2], lo_ref.shape[2]
    columns_ref[...] = se_ref[...].astype(jnp.float32).reshape(columns_ref.shape)
    base = pl.program_id(0) * ROWS
    ids_e = lax.broadcasted_iota(jnp.int32, (lats, he), 1)
    ids_o = lax.broadcasted_iota(jnp.int32, (lats, ho), 1)
    for p in range(ROWS):
        low = waves_ref[base + p]
        low_is_even = low % 2 == 0

        def split(panel, ids, count):
            in_low = ids < count
            zero = jnp.zeros_like(panel)
            lower = jnp.where(in_low, panel, zero)
            upper = jnp.where(in_low, zero, panel)
            return jnp.concatenate([lower, upper], axis=0)

        even = split(le_ref[p], ids_e, (M - low + 1) // 2)
        odd = split(lo_ref[p], ids_o, (M - low) // 2)
        xe = columns_ref[pl.ds(p, he, stride=ROWS), :].astype(jnp.bfloat16)
        sym = jnp.dot(even, xe, preferred_element_type=jnp.float32)
        anti = jnp.dot(odd, so_ref[p], preferred_element_type=jnp.float32)
        first = jnp.where(low_is_even, 0, lats) + p * 2 * lats
        second = jnp.where(low_is_even, lats, 0) + p * 2 * lats
        north, south = sym + anti, sym - anti
        rows_ref[0, pl.ds(pl.multiple_of(first, ROWS), lats), :] = north[:lats]
        rows_ref[0, pl.ds(pl.multiple_of(second, ROWS), lats), :] = north[lats:]
        rows_ref[1, pl.ds(pl.multiple_of(first, ROWS), lats), :] = south[:lats]
        rows_ref[1, pl.ds(pl.multiple_of(second, ROWS), lats), :] = south[lats:]

    def emit(lat, carry):
        for h in range(2):
            for w in range(2):
                picked = rows_ref[h, pl.ds(w * lats + lat, ROWS, stride=2 * lats), :]
                out_ref[lat, h, w] = picked.astype(jnp.bfloat16)
        return carry

    lax.fori_loop(0, lats, emit, 0, unroll=8)


def legendre_stage(waves, spectra_even, spectra_odd, legendre_even, legendre_odd):
    pairs, he, width = spectra_even.shape
    ho = spectra_odd.shape[1]
    lats = legendre_even.shape[1]
    by_column = jnp.transpose(spectra_even, (1, 0, 2))
    return pl.pallas_call(
        legendre_kernel,
        out_shape=jax.ShapeDtypeStruct((lats, 2, 2, pairs, width), jnp.bfloat16),
        grid_spec=pltpu.PrefetchScalarGridSpec(
            num_scalar_prefetch=1,
            grid=(pairs // ROWS,),
            in_specs=[
                pl.BlockSpec((he, ROWS, width), lambda i, w: (0, i, 0)),
                pl.BlockSpec((ROWS, ho, width), lambda i, w: (i, 0, 0)),
                pl.BlockSpec((ROWS, lats, he), lambda i, w: (i, 0, 0)),
                pl.BlockSpec((ROWS, lats, ho), lambda i, w: (i, 0, 0)),
            ],
            out_specs=pl.BlockSpec((lats, 2, 2, ROWS, width), lambda i, w: (0, 0, 0, i, 0)),
            scratch_shapes=[
                pltpu.VMEM((he * ROWS, width), jnp.float32),
                pltpu.VMEM((2, ROWS * 2 * lats, width), jnp.float32),
            ],
        ),
        compiler_params=pltpu.CompilerParams(vmem_limit_bytes=40 * 1024 * 1024),
        cost_estimate=pl.CostEstimate(
            flops=4 * pairs * lats * 2 * (he + ho) * width,
            bytes_accessed=2 * pairs * (he + ho) * (width + lats),
            transcendentals=0,
        ),
        name="legendre",
    )(waves, by_column, spectra_odd, legendre_even, legendre_odd)


def pick_kernel(bands_ref, rows_ref, out_ref, sems):
    lats = rows_ref.shape[0]

    def copy(slot):
        return pltpu.make_async_copy(rows_ref.at[bands_ref[slot]], out_ref.at[slot], sems.at[slot])

    @pl.loop(0, lats)
    def _(slot):
        copy(slot).start()

    @pl.loop(0, lats)
    def _(slot):
        copy(slot).wait()


def pick_latitudes(bands, rows):
    return pl.pallas_call(
        pick_kernel,
        out_shape=jax.ShapeDtypeStruct(rows.shape, rows.dtype),
        grid_spec=pltpu.PrefetchScalarGridSpec(
            num_scalar_prefetch=1,
            grid=(),
            in_specs=[pl.BlockSpec(memory_space=pl.ANY)],
            out_specs=pl.BlockSpec(memory_space=pl.ANY),
            scratch_shapes=[pltpu.SemaphoreType.DMA((rows.shape[0],))],
        ),
        name="pick",
    )(bands, rows)


def table_kernel(waves_ref, out_ref):
    low = waves_ref[...]
    rows = low.shape[0]
    even = jnp.where(low % 2 == 0, low, M - 1 - low)
    odd = M - 1 - even
    lane = lax.broadcasted_iota(jnp.int32, (rows, LANES), 1).astype(jnp.float32)
    unit = 2.0 * math.pi / NLON

    def angle(product):
        turns = jnp.floor(product * (1.0 / NLON))
        return (product - turns * NLON) * unit

    for w, wave in enumerate((even, odd)):
        number = wave.astype(jnp.float32)
        factor = jnp.where(wave == 0, 1.0, 2.0)
        start = angle(number * lane)
        step = angle(number * LANES)
        c, s = factor * jnp.cos(start), -factor * jnp.sin(start)
        dc, ds = jnp.cos(step), jnp.sin(step)
        for b in range(0, HALF, LANES):
            size = min(LANES, HALF - b)
            out_ref[w, 0, :, b : b + size] = c[:, :size].astype(jnp.bfloat16)
            out_ref[w, 1, :, b : b + size] = s[:, :size].astype(jnp.bfloat16)
            c, s = c * dc + s * ds, s * dc - c * ds


def wave_tables(waves):
    total = waves.shape[0]
    rows = 64
    return pl.pallas_call(
        table_kernel,
        out_shape=jax.ShapeDtypeStruct((2, 2, total, HALF), jnp.bfloat16),
        grid=(total // rows,),
        in_specs=[pl.BlockSpec((rows, LANES), lambda i: (i, 0))],
        out_specs=pl.BlockSpec((2, 2, rows, HALF), lambda i: (0, 0, i, 0)),
        compiler_params=pltpu.CompilerParams(vmem_limit_bytes=32 * 1024 * 1024),
        cost_estimate=pl.CostEstimate(
            flops=4 * 4 * total * HALF, bytes_accessed=8 * total * HALF, transcendentals=8 * total * LANES
        ),
        name="tables",
    )(jnp.broadcast_to(waves[:, None], (total, LANES)))


def fourier_kernel(arrived_ref, table_ref, out_ref, left_ref):
    devices, slots, _, _, pairs, width = arrived_ref.shape
    fields = width // 2
    total = devices * pairs
    for w in range(2):
        for s in range(slots):
            for h in range(2):
                x = jnp.concatenate([arrived_ref[d, s, h, w] for d in range(devices)], axis=0)
                xt = x.T
                r = (s * 2 + h) * fields
                left_ref[w, r : r + fields, :total] = xt[:fields]
                left_ref[w, r : r + fields, total:] = xt[fields:]
    chunk = 256
    ends = list(range(0, HALF, chunk)) + [HALF]
    for lo, hi in zip(ends[:-1], ends[1:]):
        sums = []
        for w in range(2):
            cos, sin = table_ref[w, 0, :, lo:hi], table_ref[w, 1, :, lo:hi]
            sums.append(
                jnp.dot(left_ref[w], jnp.concatenate([cos, sin], axis=0), preferred_element_type=jnp.float32)
            )
        plus = (sums[0] + sums[1]).astype(jnp.bfloat16)
        minus = (sums[0] - sums[1]).astype(jnp.bfloat16)
        out_ref[:, lo:hi] = plus
        out_ref[:, HALF + lo : HALF + hi] = minus


def fourier_stage(arrived, table):
    devices, slots, _, _, pairs, width = arrived.shape
    fields = width // 2
    total = devices * pairs
    out = pl.pallas_call(
        fourier_kernel,
        out_shape=jax.ShapeDtypeStruct((slots * 2 * fields, NLON), jnp.bfloat16),
        in_specs=[pl.BlockSpec(memory_space=pltpu.VMEM)] * 2,
        out_specs=pl.BlockSpec(memory_space=pltpu.VMEM),
        scratch_shapes=[pltpu.VMEM((2, slots * 2 * fields, 2 * total), jnp.bfloat16)],
        compiler_params=pltpu.CompilerParams(vmem_limit_bytes=40 * 1024 * 1024),
        name="fourier",
    )(arrived, table)
    return out.reshape(slots, 2, fields, NLON)


def on_device(wave_pairs, band_owner, spectra_even, spectra_odd, legendre_even, legendre_odd):
    devices = lax.axis_size("wave")
    pairs = round_up(wave_pairs.shape[0], ROWS)
    extra = pairs - wave_pairs.shape[0]
    slots = band_owner.shape[0]
    width = spectra_even.shape[2]
    if extra:
        wave_pairs = jnp.pad(wave_pairs, (0, extra))
        spectra_even, spectra_odd, legendre_even, legendre_odd = (
            jnp.pad(a, ((0, extra), (0, 0), (0, 0)))
            for a in (spectra_even, spectra_odd, legendre_even, legendre_odd)
        )

    own = jnp.pad(jnp.concatenate([wave_pairs, band_owner]), (0, round_up(pairs + slots, LANES) - pairs - slots))
    index = lax.all_to_all(jnp.broadcast_to(own, (devices,) + own.shape), "wave", 0, 0, tiled=True)
    all_pairs = index[:, :pairs].reshape(-1)
    all_bands = index[:, pairs : pairs + slots].reshape(-1)

    rows = legendre_stage(wave_pairs, spectra_even, spectra_odd, legendre_even, legendre_odd)
    picked = pick_latitudes(all_bands, rows).reshape(devices, slots, 2, 2, pairs, width)
    arrived = lax.all_to_all(picked, "wave", 0, 0, tiled=True)
    table = wave_tables(all_pairs)
    return fourier_stage(arrived, table)


def solution(mesh):
    return jax.shard_map(
        on_device,
        mesh=mesh,
        in_specs=(
            P("wave"),
            P("wave"),
            P("wave", None, "grp"),
            P("wave", None, "grp"),
            P("wave", None, None),
            P("wave", None, None),
        ),
        out_specs=P("wave", None, "grp", None),
        check_vma=False,
    )
```

```python
import functools
import math

import jax
import jax.numpy as jnp
from jax import lax
from jax.experimental import pallas as pl
from jax.experimental.pallas import tpu as pltpu
from jax.sharding import PartitionSpec as P

M = 1280
NLON = 2688
HALF = NLON // 2
ROWS = 8
LANES = 128


def round_up(value, unit):
    return -(-value // unit) * unit


def legendre_kernel(
    waves_ref, se_hbm, so_hbm, le_hbm, lo_hbm, out_ref, se_ref, so_ref, le_ref, lo_ref, columns_ref, sems
):
    pairs, lats, he = le_ref.shape
    ho = lo_ref.shape[2]
    groups = pairs // ROWS

    def copies(g):
        at = pl.ds(pl.multiple_of(g * ROWS, ROWS), ROWS)
        return (
            pltpu.make_async_copy(lo_hbm.at[at], lo_ref.at[at], sems.at[0, g]),
            pltpu.make_async_copy(so_hbm.at[at], so_ref.at[at], sems.at[1, g]),
            pltpu.make_async_copy(le_hbm.at[at], le_ref.at[at], sems.at[2, g]),
            pltpu.make_async_copy(se_hbm.at[:, at], se_ref.at[:, at], sems.at[3, g]),
        )

    for g in range(groups):
        for copy in copies(g):
            copy.start()

    ids_e = lax.broadcasted_iota(jnp.int32, (lats, he), 1)
    ids_o = lax.broadcasted_iota(jnp.int32, (lats, ho), 1)

    def split(panel, ids, count):
        in_low = ids < count
        zero = jnp.zeros_like(panel)
        lower = jnp.where(in_low, panel, zero)
        upper = jnp.where(in_low, zero, panel)
        return jnp.concatenate([lower, upper], axis=0)

    @pl.loop(0, groups)
    def _(g):
        for copy in copies(g):
            copy.wait()
        base = pl.multiple_of(g * ROWS, ROWS)
        columns_ref[...] = se_ref[:, pl.ds(base, ROWS), :].astype(jnp.float32).reshape(columns_ref.shape)
        for p in range(ROWS):
            low = waves_ref[base + p]
            parity = low % 2
            even = split(le_ref[base + p], ids_e, (M - low + 1) // 2)
            odd = split(lo_ref[base + p], ids_o, (M - low) // 2)
            xe = columns_ref[pl.ds(p, he, stride=ROWS), :].astype(jnp.bfloat16)
            sym = jnp.dot(even, xe, preferred_element_type=jnp.float32)
            anti = jnp.dot(odd, so_ref[base + p], preferred_element_type=jnp.float32)
            for h, rows in enumerate((sym + anti, sym - anti)):
                for w in range(2):
                    start = (parity ^ w) * (lats * pairs) + base + p
                    out_ref[h, pl.ds(start, lats, stride=pairs), :] = rows[w * lats : (w + 1) * lats]


def in_hbm(x):
    return pltpu.with_memory_space_constraint(x, pltpu.HBM)


def in_vmem(x):
    return pltpu.with_memory_space_constraint(x, pltpu.VMEM)


def legendre_stage(waves, spectra_even, spectra_odd, legendre_even, legendre_odd):
    pairs, he, width = spectra_even.shape
    ho = spectra_odd.shape[1]
    lats = legendre_even.shape[1]
    by_column = jnp.transpose(spectra_even, (1, 0, 2))
    return pl.pallas_call(
        legendre_kernel,
        out_shape=pltpu.VMEM((2, 2 * lats * pairs, width), jnp.float32),
        grid_spec=pltpu.PrefetchScalarGridSpec(
            num_scalar_prefetch=1,
            grid=(),
            in_specs=[pl.BlockSpec(memory_space=pl.ANY)] * 4,
            out_specs=pl.BlockSpec(memory_space=pltpu.VMEM),
            scratch_shapes=[
                pltpu.VMEM((he, pairs, width), jnp.bfloat16),
                pltpu.VMEM((pairs, ho, width), jnp.bfloat16),
                pltpu.VMEM((pairs, lats, he), jnp.bfloat16),
                pltpu.VMEM((pairs, lats, ho), jnp.bfloat16),
                pltpu.VMEM((he * ROWS, width), jnp.float32),
                pltpu.SemaphoreType.DMA((4, pairs // ROWS)),
            ],
        ),
        compiler_params=pltpu.CompilerParams(vmem_limit_bytes=40 * 1024 * 1024),
        cost_estimate=pl.CostEstimate(
            flops=4 * pairs * lats * 2 * (he + ho) * width,
            bytes_accessed=2 * pairs * (he + ho) * (width + lats),
            transcendentals=0,
        ),
        name="legendre",
    )(waves, in_hbm(by_column), in_hbm(spectra_odd), in_hbm(legendre_even), in_hbm(legendre_odd))


def pick_kernel(bands_ref, rows_ref, out_ref):
    lats, _, _, pairs, _ = out_ref.shape

    def emit(slot, carry):
        band = bands_ref[slot]
        for h in range(2):
            for w in range(2):
                start = pl.multiple_of((w * lats + band) * pairs, ROWS)
                out_ref[slot, h, w] = rows_ref[h, pl.ds(start, pairs), :].astype(jnp.bfloat16)
        return carry

    lax.fori_loop(0, lats, emit, 0, unroll=8)


def pick_latitudes(bands, rows, pairs):
    lats = bands.shape[0]
    width = rows.shape[2]
    return pl.pallas_call(
        pick_kernel,
        out_shape=jax.ShapeDtypeStruct((lats, 2, 2, pairs, width), jnp.bfloat16),
        grid_spec=pltpu.PrefetchScalarGridSpec(
            num_scalar_prefetch=1,
            grid=(),
            in_specs=[pl.BlockSpec(memory_space=pltpu.VMEM)],
            out_specs=pl.BlockSpec(memory_space=pltpu.VMEM),
        ),
        compiler_params=pltpu.CompilerParams(vmem_limit_bytes=16 * 1024 * 1024),
        name="pick",
    )(bands, in_vmem(rows))


def table_kernel(waves_ref, out_ref):
    unit = 2.0 * math.pi / NLON
    block = 64

    def angle(product):
        turns = jnp.floor(product * (1.0 / NLON))
        return (product - turns * NLON) * unit

    @pl.loop(0, waves_ref.shape[0] // block)
    def _(i):
        at = pl.ds(pl.multiple_of(i * block, block), block)
        low = waves_ref[at, :]
        even = jnp.where(low % 2 == 0, low, M - 1 - low)
        odd = M - 1 - even
        lane = lax.broadcasted_iota(jnp.int32, low.shape, 1).astype(jnp.float32)
        for w, wave in enumerate((even, odd)):
            number = wave.astype(jnp.float32)
            factor = jnp.where(wave == 0, 1.0, 2.0)
            start = angle(number * lane)
            step = angle(number * LANES)
            c, s = factor * jnp.cos(start), -factor * jnp.sin(start)
            dc, ds = jnp.cos(step), jnp.sin(step)
            for b in range(0, HALF, LANES):
                size = min(LANES, HALF - b)
                out_ref[w, 0, at, b : b + size] = c[:, :size].astype(jnp.bfloat16)
                out_ref[w, 1, at, b : b + size] = s[:, :size].astype(jnp.bfloat16)
                c, s = c * dc + s * ds, s * dc - c * ds


def wave_tables(waves):
    total = waves.shape[0]
    return pl.pallas_call(
        table_kernel,
        out_shape=pltpu.VMEM((2, 2, total, HALF), jnp.bfloat16),
        in_specs=[pl.BlockSpec(memory_space=pltpu.VMEM)],
        out_specs=pl.BlockSpec(memory_space=pltpu.VMEM),
        compiler_params=pltpu.CompilerParams(vmem_limit_bytes=16 * 1024 * 1024),
        cost_estimate=pl.CostEstimate(
            flops=4 * 4 * total * HALF, bytes_accessed=8 * total * HALF, transcendentals=8 * total * LANES
        ),
        name="tables",
    )(jnp.broadcast_to(waves[:, None], (total, LANES)))


def fourier_kernel(arrived_ref, table_ref, out_ref, left_ref):
    devices, slots, _, _, pairs, width = arrived_ref.shape
    fields = width // 2
    total = devices * pairs
    for w in range(2):
        for s in range(slots):
            for h in range(2):
                x = jnp.concatenate([arrived_ref[d, s, h, w] for d in range(devices)], axis=0)
                xt = x.T
                r = (s * 2 + h) * fields
                left_ref[w, r : r + fields, :total] = xt[:fields]
                left_ref[w, r : r + fields, total:] = xt[fields:]
    chunk = 256
    ends = list(range(0, HALF, chunk)) + [HALF]
    for lo, hi in zip(ends[:-1], ends[1:]):
        sums = []
        for w in range(2):
            cos, sin = table_ref[w, 0, :, lo:hi], table_ref[w, 1, :, lo:hi]
            sums.append(
                jnp.dot(left_ref[w], jnp.concatenate([cos, sin], axis=0), preferred_element_type=jnp.float32)
            )
        plus = (sums[0] + sums[1]).astype(jnp.bfloat16)
        minus = (sums[0] - sums[1]).astype(jnp.bfloat16)
        out_ref[:, lo:hi] = plus
        out_ref[:, HALF + lo : HALF + hi] = minus


def fourier_stage(arrived, table):
    devices, slots, _, _, pairs, width = arrived.shape
    fields = width // 2
    total = devices * pairs
    out = pl.pallas_call(
        fourier_kernel,
        out_shape=jax.ShapeDtypeStruct((slots * 2 * fields, NLON), jnp.bfloat16),
        in_specs=[pl.BlockSpec(memory_space=pltpu.VMEM)] * 2,
        out_specs=pl.BlockSpec(memory_space=pltpu.VMEM),
        scratch_shapes=[pltpu.VMEM((2, slots * 2 * fields, 2 * total), jnp.bfloat16)],
        compiler_params=pltpu.CompilerParams(vmem_limit_bytes=24 * 1024 * 1024),
        name="fourier",
    )(arrived, in_vmem(table))
    return out.reshape(slots, 2, fields, NLON)


def on_device(wave_pairs, band_owner, spectra_even, spectra_odd, legendre_even, legendre_odd):
    devices = lax.axis_size("wave")
    pairs = round_up(wave_pairs.shape[0], ROWS)
    extra = pairs - wave_pairs.shape[0]
    slots = band_owner.shape[0]
    width = spectra_even.shape[2]
    if extra:
        wave_pairs = jnp.pad(wave_pairs, (0, extra))
        spectra_even, spectra_odd, legendre_even, legendre_odd = (
            jnp.pad(a, ((0, extra), (0, 0), (0, 0)))
            for a in (spectra_even, spectra_odd, legendre_even, legendre_odd)
        )

    own = jnp.pad(jnp.concatenate([wave_pairs, band_owner]), (0, round_up(pairs + slots, LANES) - pairs - slots))
    index = lax.all_gather(own, "wave", axis=0)
    all_pairs = index[:, :pairs].reshape(-1)
    all_bands = index[:, pairs : pairs + slots].reshape(-1)

    rows = legendre_stage(wave_pairs, spectra_even, spectra_odd, legendre_even, legendre_odd)
    picked = pick_latitudes(all_bands, rows, pairs).reshape(devices, slots, 2, 2, pairs, width)
    arrived = lax.all_to_all(picked, "wave", 0, 0, tiled=True)
    table = wave_tables(all_pairs)
    return fourier_stage(arrived, table)


def solution(mesh):
    return jax.shard_map(
        on_device,
        mesh=mesh,
        in_specs=(
            P("wave"),
            P("wave"),
            P("wave", None, "grp"),
            P("wave", None, "grp"),
            P("wave", None, None),
            P("wave", None, None),
        ),
        out_specs=P("wave", None, "grp", None),
        check_vma=False,
    )
```

```python
import functools
import math

import jax
import jax.numpy as jnp
from jax import lax
from jax.experimental import pallas as pl
from jax.experimental.pallas import tpu as pltpu
from jax.sharding import PartitionSpec as P

M = 1280
NLON = 2688
HALF = NLON // 2
ROWS = 8
LANES = 128


def round_up(value, unit):
    return -(-value // unit) * unit


def legendre_kernel(
    first, waves_ref, se_hbm, so_hbm, le_hbm, lo_hbm, out_ref, se_ref, so_ref, le_ref, lo_ref, columns_ref, sems
):
    pairs, lats, he = le_ref.shape
    ho = lo_ref.shape[2]
    groups = pairs // ROWS

    def copies(g):
        at = pl.ds(pl.multiple_of(g * ROWS, ROWS), ROWS)
        source = pl.ds(pl.multiple_of(first + g * ROWS, ROWS), ROWS)
        return (
            pltpu.make_async_copy(lo_hbm.at[source], lo_ref.at[at], sems.at[0, g]),
            pltpu.make_async_copy(so_hbm.at[source], so_ref.at[at], sems.at[1, g]),
            pltpu.make_async_copy(le_hbm.at[source], le_ref.at[at], sems.at[2, g]),
            pltpu.make_async_copy(se_hbm.at[:, source], se_ref.at[g], sems.at[3, g]),
        )

    for g in range(groups):
        for copy in copies(g):
            copy.start()

    ids_e = lax.broadcasted_iota(jnp.int32, (lats, he), 1)
    ids_o = lax.broadcasted_iota(jnp.int32, (lats, ho), 1)

    def split(panel, ids, count):
        in_low = ids < count
        zero = jnp.zeros_like(panel)
        lower = jnp.where(in_low, panel, zero)
        upper = jnp.where(in_low, zero, panel)
        return jnp.concatenate([lower, upper], axis=0)

    @pl.loop(0, groups)
    def _(g):
        for copy in copies(g):
            copy.wait()
        base = pl.multiple_of(g * ROWS, ROWS)
        columns_ref[...] = se_ref[g].astype(jnp.float32).reshape(columns_ref.shape)
        for p in range(ROWS):
            low = waves_ref[first + base + p]
            parity = low % 2
            even = split(le_ref[base + p], ids_e, (M - low + 1) // 2)
            odd = split(lo_ref[base + p], ids_o, (M - low) // 2)
            xe = columns_ref[pl.ds(p, he, stride=ROWS), :].astype(jnp.bfloat16)
            sym = jnp.dot(even, xe, preferred_element_type=jnp.float32)
            anti = jnp.dot(odd, so_ref[base + p], preferred_element_type=jnp.float32)
            for h, rows in enumerate((sym + anti, sym - anti)):
                for w in range(2):
                    start = (parity ^ w) * (lats * pairs) + base + p
                    out_ref[h, pl.ds(start, lats, stride=pairs), :] = rows[w * lats : (w + 1) * lats]


def in_hbm(x):
    return pltpu.with_memory_space_constraint(x, pltpu.HBM)


def in_vmem(x):
    return pltpu.with_memory_space_constraint(x, pltpu.VMEM)


def legendre_stage(first, pairs, waves, spectra_even, spectra_odd, legendre_even, legendre_odd):
    _, he, width = spectra_even.shape
    ho = spectra_odd.shape[1]
    lats = legendre_even.shape[1]
    by_column = jnp.transpose(spectra_even, (1, 0, 2))
    return pl.pallas_call(
        functools.partial(legendre_kernel, first),
        out_shape=pltpu.VMEM((2, 2 * lats * pairs, width), jnp.float32),
        grid_spec=pltpu.PrefetchScalarGridSpec(
            num_scalar_prefetch=1,
            grid=(),
            in_specs=[pl.BlockSpec(memory_space=pl.ANY)] * 4,
            out_specs=pl.BlockSpec(memory_space=pltpu.VMEM),
            scratch_shapes=[
                pltpu.VMEM((pairs // ROWS, he, ROWS, width), jnp.bfloat16),
                pltpu.VMEM((pairs, ho, width), jnp.bfloat16),
                pltpu.VMEM((pairs, lats, he), jnp.bfloat16),
                pltpu.VMEM((pairs, lats, ho), jnp.bfloat16),
                pltpu.VMEM((he * ROWS, width), jnp.float32),
                pltpu.SemaphoreType.DMA((4, pairs // ROWS)),
            ],
        ),
        compiler_params=pltpu.CompilerParams(vmem_limit_bytes=40 * 1024 * 1024),
        cost_estimate=pl.CostEstimate(
            flops=4 * pairs * lats * 2 * (he + ho) * width,
            bytes_accessed=2 * pairs * (he + ho) * (width + lats),
            transcendentals=0,
        ),
        name=f"legendre_{first}",
    )(in_hbm(waves), in_hbm(by_column), in_hbm(spectra_odd), in_hbm(legendre_even), in_hbm(legendre_odd))


def pick_kernel(bands_ref, rows_ref, out_ref):
    lats, _, _, pairs, _ = out_ref.shape

    def emit(slot, carry):
        band = bands_ref[slot]
        for h in range(2):
            for w in range(2):
                start = pl.multiple_of((w * lats + band) * pairs, ROWS)
                out_ref[slot, h, w] = rows_ref[h, pl.ds(start, pairs), :].astype(jnp.bfloat16)
        return carry

    lax.fori_loop(0, lats, emit, 0, unroll=8)


def pick_latitudes(bands, rows, pairs):
    lats = bands.shape[0]
    width = rows.shape[2]
    return pl.pallas_call(
        pick_kernel,
        out_shape=jax.ShapeDtypeStruct((lats, 2, 2, pairs, width), jnp.bfloat16),
        grid_spec=pltpu.PrefetchScalarGridSpec(
            num_scalar_prefetch=1,
            grid=(),
            in_specs=[pl.BlockSpec(memory_space=pltpu.VMEM)],
            out_specs=pl.BlockSpec(memory_space=pltpu.VMEM),
        ),
        compiler_params=pltpu.CompilerParams(vmem_limit_bytes=16 * 1024 * 1024),
        name=f"pick_{pairs}",
    )(bands, in_vmem(rows))


def table_kernel(waves_ref, out_ref):
    low = waves_ref[...]
    even = jnp.where(low % 2 == 0, low, M - 1 - low)
    odd = M - 1 - even
    lane = lax.broadcasted_iota(jnp.int32, low.shape, 1).astype(jnp.float32)
    unit = 2.0 * math.pi / NLON

    def angle(product):
        turns = jnp.floor(product * (1.0 / NLON))
        return (product - turns * NLON) * unit

    for w, wave in enumerate((even, odd)):
        number = wave.astype(jnp.float32)
        factor = jnp.where(wave == 0, 1.0, 2.0)
        start = angle(number * lane)
        step = angle(number * LANES)
        c, s = factor * jnp.cos(start), -factor * jnp.sin(start)
        dc, ds = jnp.cos(step), jnp.sin(step)
        for b in range(0, HALF, LANES):
            size = min(LANES, HALF - b)
            out_ref[w, 0, :, b : b + size] = c[:, :size].astype(jnp.bfloat16)
            out_ref[w, 1, :, b : b + size] = s[:, :size].astype(jnp.bfloat16)
            c, s = c * dc + s * ds, s * dc - c * ds


def wave_tables(waves):
    total = waves.shape[0]
    rows = 64
    return pl.pallas_call(
        table_kernel,
        out_shape=pltpu.HBM((2, 2, total, HALF), jnp.bfloat16),
        grid=(total // rows,),
        in_specs=[pl.BlockSpec((rows, LANES), lambda i: (i, 0))],
        out_specs=pl.BlockSpec((2, 2, rows, HALF), lambda i: (0, 0, i, 0)),
        compiler_params=pltpu.CompilerParams(vmem_limit_bytes=32 * 1024 * 1024),
        cost_estimate=pl.CostEstimate(
            flops=4 * 4 * total * HALF, bytes_accessed=8 * total * HALF, transcendentals=8 * total * LANES
        ),
        name="tables",
    )(jnp.broadcast_to(waves[:, None], (total, LANES)))


def index_kernel(waves_ref, bands_ref, out_ref):
    waves, bands = waves_ref[...], bands_ref[...]
    lanes = out_ref.shape[2]
    rest = jnp.zeros((1, lanes - waves.shape[1] - bands.shape[1]), jnp.int32)
    row = jnp.concatenate([waves, bands, rest], axis=1)
    out_ref[...] = jnp.broadcast_to(row[None], out_ref.shape)


def index_rows(devices, waves, bands):
    lanes = round_up(waves.shape[0] + bands.shape[0], LANES)
    return pl.pallas_call(
        index_kernel,
        out_shape=pltpu.VMEM((devices, 1, lanes), jnp.int32),
        in_specs=[pl.BlockSpec(memory_space=pltpu.VMEM)] * 2,
        out_specs=pl.BlockSpec(memory_space=pltpu.VMEM),
        name="index",
    )(waves[None], bands[None])


def fourier_kernel(start, last, arrived_ref, table_hbm, before_hbm, out_hbm, left_ref, table_ref, sums_ref, row_ref, sems, out_sems):
    devices, slots, _, _, pairs, width = arrived_ref.shape
    fields = width // 2
    total = devices * pairs
    chunk = 256
    ends = list(range(0, HALF, chunk)) + [HALF]
    spans = list(zip(ends[:-1], ends[1:]))

    def loads(i):
        lo, hi = spans[i]
        at = table_hbm.at[:, :, start : start + total, lo:hi]
        copies = [pltpu.make_async_copy(at, table_ref.at[:, :, :, lo:hi], sems.at[0, i])]
        if before_hbm is not None:
            copies.append(
                pltpu.make_async_copy(before_hbm.at[:, :, lo:hi], sums_ref.at[:, :, lo:hi], sems.at[1, i])
            )
        return copies

    for i in range(len(spans)):
        for copy in loads(i):
            copy.start()

    for w in range(2):
        for s in range(slots):
            for h in range(2):
                x = jnp.concatenate([arrived_ref[d, s, h, w] for d in range(devices)], axis=0)
                xt = x.T
                r = (s * 2 + h) * fields
                left_ref[w, r : r + fields, :total] = xt[:fields]
                left_ref[w, r : r + fields, total:] = xt[fields:]

    stores = []
    sent = [0, round_up(HALF, LANES)]
    for i, (lo, hi) in enumerate(spans):
        for copy in loads(i):
            copy.wait()
        e, o = [
            jnp.dot(
                left_ref[w],
                jnp.concatenate([table_ref[w, 0, :, lo:hi], table_ref[w, 1, :, lo:hi]], axis=0),
                preferred_element_type=jnp.float32,
            )
            for w in range(2)
        ]
        plus, minus = e + o, e - o
        if before_hbm is not None:
            plus += sums_ref[0, :, lo:hi]
            minus += sums_ref[1, :, lo:hi]
        if not last:
            sums_ref[0, :, lo:hi] = plus
            sums_ref[1, :, lo:hi] = minus
            copy = pltpu.make_async_copy(sums_ref.at[:, :, lo:hi], out_hbm.at[:, :, lo:hi], out_sems.at[0, i])
            copy.start()
            stores.append(copy)
            continue
        row_ref[:, lo:hi] = plus.astype(jnp.bfloat16)
        row_ref[:, HALF + lo : HALF + hi] = minus.astype(jnp.bfloat16)
        done = hi == HALF
        reach = (round_up(HALF, LANES) if done else hi, NLON if done else (HALF + hi) // LANES * LANES)
        for part in range(2):
            at = slice(sent[part], reach[part])
            copy = pltpu.make_async_copy(row_ref.at[:, at], out_hbm.at[:, at], out_sems.at[part, i])
            copy.start()
            stores.append(copy)
            sent[part] = reach[part]
    for copy in stores:
        copy.wait()


def fourier_stage(arrived, table, start, before, last):
    devices, slots, _, _, pairs, width = arrived.shape
    fields = width // 2
    total = devices * pairs
    rows = slots * 2 * fields
    spans = pl.cdiv(HALF, 256)
    kernel = functools.partial(fourier_kernel, start, last)
    operands = [arrived, in_hbm(table)]
    if before is not None:
        operands.append(before)
    else:
        kernel = lambda a, t, *rest: fourier_kernel(start, last, a, t, None, *rest)
    shape = jax.ShapeDtypeStruct((rows, NLON), jnp.bfloat16) if last else jax.ShapeDtypeStruct((2, rows, HALF), jnp.float32)
    return pl.pallas_call(
        kernel,
        out_shape=shape,
        in_specs=[pl.BlockSpec(memory_space=pltpu.VMEM)] + [pl.BlockSpec(memory_space=pl.ANY)] * (len(operands) - 1),
        out_specs=pl.BlockSpec(memory_space=pl.ANY),
        scratch_shapes=[
            pltpu.VMEM((2, rows, 2 * total), jnp.bfloat16),
            pltpu.VMEM((2, 2, total, HALF), jnp.bfloat16),
            pltpu.VMEM((2, rows, HALF), jnp.float32),
            pltpu.VMEM((rows, NLON), jnp.bfloat16),
            pltpu.SemaphoreType.DMA((2, spans)),
            pltpu.SemaphoreType.DMA((2, spans)),
        ],
        compiler_params=pltpu.CompilerParams(vmem_limit_bytes=40 * 1024 * 1024),
        cost_estimate=pl.CostEstimate(
            flops=8 * rows * total * HALF, bytes_accessed=8 * total * HALF, transcendentals=0
        ),
        name=f"fourier_{start}",
    )(*operands)


def on_device(wave_pairs, band_owner, spectra_even, spectra_odd, legendre_even, legendre_odd):
    devices = lax.axis_size("wave")
    pairs = round_up(wave_pairs.shape[0], ROWS)
    extra = pairs - wave_pairs.shape[0]
    slots = band_owner.shape[0]
    width = spectra_even.shape[2]
    if extra:
        wave_pairs = jnp.pad(wave_pairs, (0, extra))
        spectra_even, spectra_odd, legendre_even, legendre_odd = (
            jnp.pad(a, ((0, extra), (0, 0), (0, 0)))
            for a in (spectra_even, spectra_odd, legendre_even, legendre_odd)
        )
    groups = pairs // ROWS
    cut = groups * 2 // 5 * ROWS
    ranges = [(lo, hi) for lo, hi in ((0, cut), (cut, pairs)) if hi > lo]

    index = lax.all_to_all(index_rows(devices, wave_pairs, band_owner), "wave", 0, 0, tiled=True)[:, 0]
    all_bands = index[:, pairs : pairs + slots].reshape(-1)
    all_pairs = jnp.concatenate([index[:, lo:hi].reshape(-1) for lo, hi in ranges])

    arrived = []
    for lo, hi in ranges:
        rows = legendre_stage(lo, hi - lo, wave_pairs, spectra_even, spectra_odd, legendre_even, legendre_odd)
        picked = pick_latitudes(all_bands, rows, hi - lo).reshape(devices, slots, 2, 2, hi - lo, width)
        arrived.append(lax.all_to_all(picked, "wave", 0, 0, tiled=True))
    table = wave_tables(all_pairs)
    result = None
    for i, (lo, hi) in enumerate(ranges):
        result = fourier_stage(arrived[i], table, devices * lo, result, i == len(ranges) - 1)
    return result.reshape(slots, 2, width // 2, NLON)


def solution(mesh):
    return jax.shard_map(
        on_device,
        mesh=mesh,
        in_specs=(
            P("wave"),
            P("wave"),
            P("wave", None, "grp"),
            P("wave", None, "grp"),
            P("wave", None, None),
            P("wave", None, None),
        ),
        out_specs=P("wave", None, "grp", None),
        check_vma=False,
    )
```

```python
import functools
import math

import jax
import jax.numpy as jnp
from jax import lax
from jax.experimental import pallas as pl
from jax.experimental.pallas import tpu as pltpu
from jax.sharding import PartitionSpec as P

M = 1280
NLON = 2688
HALF = NLON // 2
ROWS = 8
LANES = 128


def round_up(value, unit):
    return -(-value // unit) * unit


def legendre_kernel(first, direct, waves_ref, *refs):
    bands_ref = refs[0] if direct else None
    se_hbm, so_hbm, le_hbm, lo_hbm = refs[direct : direct + 4]
    rest = refs[direct + 4 :]
    se_ref, so_ref, le_ref, lo_ref, columns_ref, sems = rest[-6:]
    rows_ref = rest[-7] if direct else rest[0]
    pairs, lats, he = le_ref.shape
    ho = lo_ref.shape[2]
    groups = pairs // ROWS

    def copies(g):
        at = pl.ds(pl.multiple_of(g * ROWS, ROWS), ROWS)
        source = pl.ds(pl.multiple_of(first + g * ROWS, ROWS), ROWS)
        return (
            pltpu.make_async_copy(lo_hbm.at[source], lo_ref.at[at], sems.at[0, g]),
            pltpu.make_async_copy(so_hbm.at[source], so_ref.at[at], sems.at[1, g]),
            pltpu.make_async_copy(le_hbm.at[source], le_ref.at[at], sems.at[2, g]),
            pltpu.make_async_copy(se_hbm.at[:, source], se_ref.at[g], sems.at[3, g]),
        )

    for copy in copies(0):
        copy.start()

    ids_e = lax.broadcasted_iota(jnp.int32, (lats, he), 1)
    ids_o = lax.broadcasted_iota(jnp.int32, (lats, ho), 1)

    def split(panel, ids, count):
        in_low = ids < count
        zero = jnp.zeros_like(panel)
        lower = jnp.where(in_low, panel, zero)
        upper = jnp.where(in_low, zero, panel)
        return jnp.concatenate([lower, upper], axis=0)

    @pl.loop(0, groups)
    def _(g):
        for copy in copies(g):
            copy.wait()

        @pl.when(g + 1 < groups)
        def _():
            for copy in copies(g + 1):
                copy.start()

        base = pl.multiple_of(g * ROWS, ROWS)
        columns_ref[...] = se_ref[g].astype(jnp.float32).reshape(columns_ref.shape)
        for p in range(ROWS):
            low = waves_ref[first + base + p]
            parity = low % 2
            even = split(le_ref[base + p], ids_e, (M - low + 1) // 2)
            odd = split(lo_ref[base + p], ids_o, (M - low) // 2)
            xe = columns_ref[pl.ds(p, he, stride=ROWS), :].astype(jnp.bfloat16)
            sym = jnp.dot(even, xe, preferred_element_type=jnp.float32)
            anti = jnp.dot(odd, so_ref[base + p], preferred_element_type=jnp.float32)
            for h, rows in enumerate((sym + anti, sym - anti)):
                for w in range(2):
                    start = (parity ^ w) * (lats * pairs) + base + p
                    rows_ref[h, pl.ds(start, lats, stride=pairs), :] = rows[w * lats : (w + 1) * lats]

    if direct:
        me = lax.axis_index("wave")
        for k, out_ref in enumerate(rest[:-7]):
            for slot in range(out_ref.shape[0]):
                band = bands_ref[(me ^ k) * out_ref.shape[0] + slot]
                for h in range(2):
                    for w in range(2):
                        start = pl.multiple_of((w * lats + band) * pairs, ROWS)
                        out_ref[slot, h, w] = rows_ref[h, pl.ds(start, pairs), :].astype(jnp.bfloat16)


def in_hbm(x):
    return pltpu.with_memory_space_constraint(x, pltpu.HBM)


def in_vmem(x):
    return pltpu.with_memory_space_constraint(x, pltpu.VMEM)


def legendre_stage(first, pairs, bands, devices, waves, spectra_even, spectra_odd, legendre_even, legendre_odd):
    _, he, width = spectra_even.shape
    ho = spectra_odd.shape[1]
    lats = legendre_even.shape[1]
    by_column = jnp.transpose(spectra_even, (1, 0, 2))
    direct = bands is not None
    rows = pltpu.VMEM((2, 2 * lats * pairs, width), jnp.float32)
    scalars = [in_hbm(waves)]
    out_shape = rows
    if direct:
        scalars.append(bands)
        out_shape = [pltpu.VMEM((lats // devices, 2, 2, pairs, width), jnp.bfloat16)] * devices
    return pl.pallas_call(
        functools.partial(legendre_kernel, first, int(direct)),
        out_shape=out_shape,
        grid_spec=pltpu.PrefetchScalarGridSpec(
            num_scalar_prefetch=len(scalars),
            grid=(),
            in_specs=[pl.BlockSpec(memory_space=pl.ANY)] * 4,
            out_specs=[pl.BlockSpec(memory_space=pltpu.VMEM)] * devices if direct else pl.BlockSpec(memory_space=pltpu.VMEM),
            scratch_shapes=[rows] * direct
            + [
                pltpu.VMEM((pairs // ROWS, he, ROWS, width), jnp.bfloat16),
                pltpu.VMEM((pairs, ho, width), jnp.bfloat16),
                pltpu.VMEM((pairs, lats, he), jnp.bfloat16),
                pltpu.VMEM((pairs, lats, ho), jnp.bfloat16),
                pltpu.VMEM((he * ROWS, width), jnp.float32),
                pltpu.SemaphoreType.DMA((4, pairs // ROWS)),
            ],
        ),
        compiler_params=pltpu.CompilerParams(vmem_limit_bytes=40 * 1024 * 1024),
        cost_estimate=pl.CostEstimate(
            flops=4 * pairs * lats * 2 * (he + ho) * width,
            bytes_accessed=2 * pairs * (he + ho) * (width + lats),
            transcendentals=0,
        ),
        name=f"legendre_{first}",
    )(*scalars, in_hbm(by_column), in_hbm(spectra_odd), in_hbm(legendre_even), in_hbm(legendre_odd))


def pick_kernel(bands_ref, rows_ref, out_ref):
    lats, _, _, pairs, _ = out_ref.shape

    def emit(slot, carry):
        band = bands_ref[slot]
        for h in range(2):
            for w in range(2):
                start = pl.multiple_of((w * lats + band) * pairs, ROWS)
                out_ref[slot, h, w] = rows_ref[h, pl.ds(start, pairs), :].astype(jnp.bfloat16)
        return carry

    lax.fori_loop(0, lats, emit, 0, unroll=8)


def pick_latitudes(bands, rows, pairs):
    lats = bands.shape[0]
    width = rows.shape[2]
    return pl.pallas_call(
        pick_kernel,
        out_shape=jax.ShapeDtypeStruct((lats, 2, 2, pairs, width), jnp.bfloat16),
        grid_spec=pltpu.PrefetchScalarGridSpec(
            num_scalar_prefetch=1,
            grid=(),
            in_specs=[pl.BlockSpec(memory_space=pltpu.VMEM)],
            out_specs=pl.BlockSpec(memory_space=pltpu.VMEM),
        ),
        compiler_params=pltpu.CompilerParams(vmem_limit_bytes=16 * 1024 * 1024),
        name=f"pick_{pairs}",
    )(bands, in_vmem(rows))


def table_kernel(waves_ref, out_ref):
    low = waves_ref[...]
    even = jnp.where(low % 2 == 0, low, M - 1 - low)
    odd = M - 1 - even
    lane = lax.broadcasted_iota(jnp.int32, low.shape, 1).astype(jnp.float32)
    unit = 2.0 * math.pi / NLON

    def angle(product):
        turns = jnp.floor(product * (1.0 / NLON))
        return (product - turns * NLON) * unit

    for w, wave in enumerate((even, odd)):
        number = wave.astype(jnp.float32)
        factor = jnp.where(wave == 0, 1.0, 2.0)
        start = angle(number * lane)
        step = angle(number * LANES)
        c, s = factor * jnp.cos(start), -factor * jnp.sin(start)
        dc, ds = jnp.cos(step), jnp.sin(step)
        for b in range(0, HALF, LANES):
            size = min(LANES, HALF - b)
            out_ref[w, 0, :, b : b + size] = c[:, :size].astype(jnp.bfloat16)
            out_ref[w, 1, :, b : b + size] = s[:, :size].astype(jnp.bfloat16)
            c, s = c * dc + s * ds, s * dc - c * ds


def wave_tables(waves):
    total = waves.shape[0]
    rows = 64
    return pl.pallas_call(
        table_kernel,
        out_shape=pltpu.HBM((2, 2, total, HALF), jnp.bfloat16),
        grid=(total // rows,),
        in_specs=[pl.BlockSpec((rows, LANES), lambda i: (i, 0))],
        out_specs=pl.BlockSpec((2, 2, rows, HALF), lambda i: (0, 0, i, 0)),
        compiler_params=pltpu.CompilerParams(vmem_limit_bytes=32 * 1024 * 1024),
        cost_estimate=pl.CostEstimate(
            flops=4 * 4 * total * HALF, bytes_accessed=8 * total * HALF, transcendentals=8 * total * LANES
        ),
        name="tables",
    )(jnp.broadcast_to(waves[:, None], (total, LANES)))


def index_kernel(waves_ref, bands_ref, out_ref):
    waves, bands = waves_ref[...], bands_ref[...]
    lanes = out_ref.shape[2]
    rest = jnp.zeros((1, lanes - waves.shape[1] - bands.shape[1]), jnp.int32)
    row = jnp.concatenate([waves, bands, rest], axis=1)
    out_ref[...] = jnp.broadcast_to(row[None], out_ref.shape)


def index_rows(devices, waves, bands):
    lanes = round_up(waves.shape[0] + bands.shape[0], LANES)
    return pl.pallas_call(
        index_kernel,
        out_shape=pltpu.VMEM((devices, 1, lanes), jnp.int32),
        in_specs=[pl.BlockSpec(memory_space=pltpu.VMEM)] * 2,
        out_specs=pl.BlockSpec(memory_space=pltpu.VMEM),
        name="index",
    )(waves[None], bands[None])


def fourier_kernel(start, last, parts, added, *refs):
    arrived = refs[:parts]
    table_hbm = refs[parts]
    before_hbm = refs[parts + 1] if added else None
    out_hbm, left_ref, table_ref, sums_ref, row_ref, sems, out_sems = refs[parts + 1 + added :]
    if parts == 1:
        arrived = [arrived[0].at[d] for d in range(arrived[0].shape[0])]
    slots, _, _, pairs, width = arrived[0].shape
    fields = width // 2
    total = len(arrived) * pairs
    chunk = 256
    ends = list(range(0, HALF, chunk)) + [HALF]
    spans = list(zip(ends[:-1], ends[1:]))

    def loads(i):
        lo, hi = spans[i]
        at = table_hbm.at[:, :, start : start + total, lo:hi]
        copies = [pltpu.make_async_copy(at, table_ref.at[:, :, :, lo:hi], sems.at[0, i])]
        if added:
            copies.append(
                pltpu.make_async_copy(before_hbm.at[:, :, lo:hi], sums_ref.at[:, :, lo:hi], sems.at[1, i])
            )
        return copies

    for i in range(len(spans)):
        for copy in loads(i):
            copy.start()

    for w in range(2):
        for s in range(slots):
            for h in range(2):
                x = jnp.concatenate([rows[s, h, w] for rows in arrived], axis=0)
                xt = x.T
                r = (s * 2 + h) * fields
                left_ref[w, r : r + fields, :total] = xt[:fields]
                left_ref[w, r : r + fields, total:] = xt[fields:]

    stores = []
    sent = [0, round_up(HALF, LANES)]
    for i, (lo, hi) in enumerate(spans):
        for copy in loads(i):
            copy.wait()
        e, o = [
            jnp.dot(
                left_ref[w],
                jnp.concatenate([table_ref[w, 0, :, lo:hi], table_ref[w, 1, :, lo:hi]], axis=0),
                preferred_element_type=jnp.float32,
            )
            for w in range(2)
        ]
        plus, minus = e + o, e - o
        if added:
            plus += sums_ref[0, :, lo:hi]
            minus += sums_ref[1, :, lo:hi]
        if not last:
            sums_ref[0, :, lo:hi] = plus
            sums_ref[1, :, lo:hi] = minus
            copy = pltpu.make_async_copy(sums_ref.at[:, :, lo:hi], out_hbm.at[:, :, lo:hi], out_sems.at[0, i])
            copy.start()
            stores.append(copy)
            continue
        row_ref[:, lo:hi] = plus.astype(jnp.bfloat16)
        row_ref[:, HALF + lo : HALF + hi] = minus.astype(jnp.bfloat16)
        done = hi == HALF
        reach = (round_up(HALF, LANES) if done else hi, NLON if done else (HALF + hi) // LANES * LANES)
        for part in range(2):
            at = slice(sent[part], reach[part])
            copy = pltpu.make_async_copy(row_ref.at[:, at], out_hbm.at[:, at], out_sems.at[part, i])
            copy.start()
            stores.append(copy)
            sent[part] = reach[part]
    for copy in stores:
        copy.wait()


def fourier_stage(arrived, table, start, before, last):
    slots, _, _, pairs, width = arrived[0].shape[-5:]
    fields = width // 2
    devices = len(arrived) if len(arrived) > 1 else arrived[0].shape[0]
    total = devices * pairs
    rows = slots * 2 * fields
    spans = pl.cdiv(HALF, 256)
    operands = [*arrived, in_hbm(table)]
    if before is not None:
        operands.append(before)
    shape = jax.ShapeDtypeStruct((rows, NLON), jnp.bfloat16) if last else jax.ShapeDtypeStruct((2, rows, HALF), jnp.float32)
    return pl.pallas_call(
        functools.partial(fourier_kernel, start, last, len(arrived), int(before is not None)),
        out_shape=shape,
        in_specs=[pl.BlockSpec(memory_space=pltpu.VMEM)] * len(arrived)
        + [pl.BlockSpec(memory_space=pl.ANY)] * (len(operands) - len(arrived)),
        out_specs=pl.BlockSpec(memory_space=pl.ANY),
        scratch_shapes=[
            pltpu.VMEM((2, rows, 2 * total), jnp.bfloat16),
            pltpu.VMEM((2, 2, total, HALF), jnp.bfloat16),
            pltpu.VMEM((2, rows, HALF), jnp.float32),
            pltpu.VMEM((rows, NLON), jnp.bfloat16),
            pltpu.SemaphoreType.DMA((2, spans)),
            pltpu.SemaphoreType.DMA((2, spans)),
        ],
        compiler_params=pltpu.CompilerParams(vmem_limit_bytes=40 * 1024 * 1024),
        cost_estimate=pl.CostEstimate(
            flops=8 * rows * total * HALF, bytes_accessed=8 * total * HALF, transcendentals=0
        ),
        name=f"fourier_{start}",
    )(*operands)


def on_device(wave_pairs, band_owner, spectra_even, spectra_odd, legendre_even, legendre_odd):
    devices = lax.axis_size("wave")
    pairs = round_up(wave_pairs.shape[0], ROWS)
    extra = pairs - wave_pairs.shape[0]
    slots = band_owner.shape[0]
    width = spectra_even.shape[2]
    if extra:
        wave_pairs = jnp.pad(wave_pairs, (0, extra))
        spectra_even, spectra_odd, legendre_even, legendre_odd = (
            jnp.pad(a, ((0, extra), (0, 0), (0, 0)))
            for a in (spectra_even, spectra_odd, legendre_even, legendre_odd)
        )
    groups = pairs // ROWS
    cut = groups * 2 // 5 * ROWS or pairs

    index = lax.all_to_all(index_rows(devices, wave_pairs, band_owner), "wave", 0, 0, tiled=True)[:, 0]
    all_bands = index[:, pairs : pairs + slots].reshape(-1)
    fields = (wave_pairs, spectra_even, spectra_odd, legendre_even, legendre_odd)

    rows = legendre_stage(0, cut, None, devices, *fields)
    picked = pick_latitudes(all_bands, rows, cut).reshape(devices, slots, 2, 2, cut, width)
    next_bands, picked = lax.optimization_barrier((all_bands, picked))
    waves = [index[:, :cut].reshape(-1)]
    arrived = [[lax.all_to_all(picked, "wave", 0, 0, tiled=True)]]
    if cut < pairs:
        outgoing = legendre_stage(cut, pairs - cut, next_bands, devices, *fields)
        partner = [[(i, i ^ k) for i in range(devices)] for k in range(devices)]
        arrived.append([outgoing[0]] + [lax.ppermute(outgoing[k], "wave", partner[k]) for k in range(1, devices)])
        order = lax.axis_index("wave") ^ jnp.arange(devices)
        chosen = (order[:, None] == jnp.arange(devices)[None])[:, :, None]
        waves.append(jnp.sum(jnp.where(chosen, index[None, :, cut:pairs], 0), axis=1).reshape(-1))
    table = wave_tables(jnp.concatenate(waves))
    result, start = None, 0
    for i, some in enumerate(arrived):
        result = fourier_stage(some, table, start, result, i == len(arrived) - 1)
        start += waves[i].shape[0]
    return result.reshape(slots, 2, width // 2, NLON)


def solution(mesh):
    return jax.shard_map(
        on_device,
        mesh=mesh,
        in_specs=(
            P("wave"),
            P("wave"),
            P("wave", None, "grp"),
            P("wave", None, "grp"),
            P("wave", None, None),
            P("wave", None, None),
        ),
        out_specs=P("wave", None, "grp", None),
        check_vma=False,
    )
```

```python
import functools
import math

import jax
import jax.numpy as jnp
from jax import lax
from jax.experimental import pallas as pl
from jax.experimental.pallas import tpu as pltpu
from jax.sharding import PartitionSpec as P

M = 1280
NLON = 2688
HALF = NLON // 2
ROWS = 8
LANES = 128


def round_up(value, unit):
    return -(-value // unit) * unit


def legendre_kernel(
    waves_hbm, se_hbm, so_hbm, le_hbm, lo_hbm, out_ref,
    waves_ref, se_ref, so_ref, le_ref, lo_ref, columns_ref, anti_ref, sems, wave_sem,
):
    pairs, lats, he = le_ref.shape
    ho = lo_ref.shape[2]
    groups = pairs // ROWS

    def odd_copies(g):
        at = pl.ds(pl.multiple_of(g * ROWS, ROWS), ROWS)
        return (
            pltpu.make_async_copy(lo_hbm.at[at], lo_ref.at[at], sems.at[0, g]),
            pltpu.make_async_copy(so_hbm.at[at], so_ref.at[at], sems.at[1, g]),
        )

    def even_copies(g):
        at = pl.ds(pl.multiple_of(g * ROWS, ROWS), ROWS)
        return (
            pltpu.make_async_copy(le_hbm.at[at], le_ref.at[at], sems.at[2, g]),
            pltpu.make_async_copy(se_hbm.at[:, at], se_ref.at[g], sems.at[3, g]),
        )

    wave_copy = pltpu.make_async_copy(waves_hbm, waves_ref, wave_sem)
    wave_copy.start()
    for g in range(groups):
        for copy in odd_copies(g) + even_copies(g):
            copy.start()
    wave_copy.wait()

    ids_e = lax.broadcasted_iota(jnp.int32, (lats, he), 1)
    ids_o = lax.broadcasted_iota(jnp.int32, (lats, ho), 1)

    def split(panel, ids, count):
        in_low = ids < count
        zero = jnp.zeros_like(panel)
        lower = jnp.where(in_low, panel, zero)
        upper = jnp.where(in_low, zero, panel)
        return jnp.concatenate([lower, upper], axis=0)

    @pl.loop(0, groups)
    def _(g):
        base = pl.multiple_of(g * ROWS, ROWS)
        for copy in odd_copies(g):
            copy.wait()
        for p in range(ROWS):
            odd = split(lo_ref[base + p], ids_o, (M - waves_ref[base + p]) // 2)
            anti_ref[p] = jnp.dot(odd, so_ref[base + p], preferred_element_type=jnp.float32)
        for copy in even_copies(g):
            copy.wait()
        columns_ref[...] = se_ref[g].astype(jnp.float32).reshape(columns_ref.shape)
        for p in range(ROWS):
            low = waves_ref[base + p]
            parity = low % 2
            even = split(le_ref[base + p], ids_e, (M - low + 1) // 2)
            xe = columns_ref[pl.ds(p, he, stride=ROWS), :].astype(jnp.bfloat16)
            sym = jnp.dot(even, xe, preferred_element_type=jnp.float32)
            anti = anti_ref[p]
            for h, rows in enumerate((sym + anti, sym - anti)):
                for w in range(2):
                    start = (parity ^ w) * (lats * pairs) + base + p
                    out_ref[h, pl.ds(start, lats, stride=pairs), :] = rows[w * lats : (w + 1) * lats]


def in_hbm(x):
    return pltpu.with_memory_space_constraint(x, pltpu.HBM)


def in_vmem(x):
    return pltpu.with_memory_space_constraint(x, pltpu.VMEM)


def legendre_stage(waves, spectra_even, spectra_odd, legendre_even, legendre_odd):
    pairs, he, width = spectra_even.shape
    ho = spectra_odd.shape[1]
    lats = legendre_even.shape[1]
    by_column = jnp.transpose(spectra_even, (1, 0, 2))
    operands = (waves, by_column, spectra_odd, legendre_even, legendre_odd)
    return pl.pallas_call(
        legendre_kernel,
        out_shape=pltpu.VMEM((2, 2 * lats * pairs, width), jnp.float32),
        in_specs=[pl.BlockSpec(memory_space=pl.ANY)] * 5,
        out_specs=pl.BlockSpec(memory_space=pltpu.VMEM),
        scratch_shapes=[
            pltpu.SMEM((pairs,), jnp.int32),
            pltpu.VMEM((pairs // ROWS, he, ROWS, width), jnp.bfloat16),
            pltpu.VMEM((pairs, ho, width), jnp.bfloat16),
            pltpu.VMEM((pairs, lats, he), jnp.bfloat16),
            pltpu.VMEM((pairs, lats, ho), jnp.bfloat16),
            pltpu.VMEM((he * ROWS, width), jnp.float32),
            pltpu.VMEM((ROWS, 2 * lats, width), jnp.float32),
            pltpu.SemaphoreType.DMA((4, pairs // ROWS)),
            pltpu.SemaphoreType.DMA,
        ],
        compiler_params=pltpu.CompilerParams(vmem_limit_bytes=40 * 1024 * 1024),
        cost_estimate=pl.CostEstimate(
            flops=4 * pairs * lats * 2 * (he + ho) * width,
            bytes_accessed=2 * pairs * (he + ho) * (width + lats),
            transcendentals=0,
        ),
        name="legendre",
    )(*(in_hbm(x) for x in operands))


def pick_kernel(bands_ref, rows_ref, out_ref):
    lats, _, _, pairs, _ = out_ref.shape

    def emit(slot, carry):
        band = bands_ref[slot]
        for h in range(2):
            for w in range(2):
                start = pl.multiple_of((w * lats + band) * pairs, ROWS)
                out_ref[slot, h, w] = rows_ref[h, pl.ds(start, pairs), :].astype(jnp.bfloat16)
        return carry

    lax.fori_loop(0, lats, emit, 0, unroll=8)


def pick_latitudes(bands, rows, pairs):
    lats = bands.shape[0]
    width = rows.shape[2]
    return pl.pallas_call(
        pick_kernel,
        out_shape=jax.ShapeDtypeStruct((lats, 2, 2, pairs, width), jnp.bfloat16),
        grid_spec=pltpu.PrefetchScalarGridSpec(
            num_scalar_prefetch=1,
            grid=(),
            in_specs=[pl.BlockSpec(memory_space=pltpu.VMEM)],
            out_specs=pl.BlockSpec(memory_space=pltpu.VMEM),
        ),
        compiler_params=pltpu.CompilerParams(vmem_limit_bytes=16 * 1024 * 1024),
        name=f"pick_{pairs}",
    )(bands, in_vmem(rows))


def table_kernel(waves_ref, out_ref):
    low = waves_ref[...]
    even = jnp.where(low % 2 == 0, low, M - 1 - low)
    odd = M - 1 - even
    lane = lax.broadcasted_iota(jnp.int32, low.shape, 1).astype(jnp.float32)
    unit = 2.0 * math.pi / NLON

    def angle(product):
        turns = jnp.floor(product * (1.0 / NLON))
        return (product - turns * NLON) * unit

    for w, wave in enumerate((even, odd)):
        number = wave.astype(jnp.float32)
        factor = jnp.where(wave == 0, 1.0, 2.0)
        start = angle(number * lane)
        step = angle(number * LANES)
        c, s = factor * jnp.cos(start), -factor * jnp.sin(start)
        dc, ds = jnp.cos(step), jnp.sin(step)
        for b in range(0, HALF, LANES):
            size = min(LANES, HALF - b)
            out_ref[w, 0, :, b : b + size] = c[:, :size].astype(jnp.bfloat16)
            out_ref[w, 1, :, b : b + size] = s[:, :size].astype(jnp.bfloat16)
            c, s = c * dc + s * ds, s * dc - c * ds


def wave_tables(waves):
    total = waves.shape[0]
    rows = 64
    return pl.pallas_call(
        table_kernel,
        out_shape=pltpu.HBM((2, 2, total, HALF), jnp.bfloat16),
        grid=(total // rows,),
        in_specs=[pl.BlockSpec((rows, LANES), lambda i: (i, 0))],
        out_specs=pl.BlockSpec((2, 2, rows, HALF), lambda i: (0, 0, i, 0)),
        compiler_params=pltpu.CompilerParams(vmem_limit_bytes=32 * 1024 * 1024),
        cost_estimate=pl.CostEstimate(
            flops=4 * 4 * total * HALF, bytes_accessed=8 * total * HALF, transcendentals=8 * total * LANES
        ),
        name="tables",
    )(jnp.broadcast_to(waves[:, None], (total, LANES)))


def fourier_kernel(arrived_ref, table_hbm, out_hbm, left_ref, table_ref, row_ref, sems, out_sems):
    devices, slots, _, _, pairs, width = arrived_ref.shape
    fields = width // 2
    total = devices * pairs
    chunk = 256
    ends = list(range(0, HALF, chunk)) + [HALF]
    spans = list(zip(ends[:-1], ends[1:]))

    def load(i):
        at = slice(*spans[i])
        return pltpu.make_async_copy(table_hbm.at[:, :, :, at], table_ref.at[:, :, :, at], sems.at[i])

    for i in range(len(spans)):
        load(i).start()

    for w in range(2):
        for s in range(slots):
            for h in range(2):
                x = jnp.concatenate([arrived_ref[d, s, h, w] for d in range(devices)], axis=0)
                xt = x.T
                r = (s * 2 + h) * fields
                left_ref[w, r : r + fields, :total] = xt[:fields]
                left_ref[w, r : r + fields, total:] = xt[fields:]

    stores = []
    sent = [0, round_up(HALF, LANES)]
    for i, (lo, hi) in enumerate(spans):
        load(i).wait()
        e, o = [
            jnp.dot(
                left_ref[w],
                jnp.concatenate([table_ref[w, 0, :, lo:hi], table_ref[w, 1, :, lo:hi]], axis=0),
                preferred_element_type=jnp.float32,
            )
            for w in range(2)
        ]
        row_ref[:, lo:hi] = (e + o).astype(jnp.bfloat16)
        row_ref[:, HALF + lo : HALF + hi] = (e - o).astype(jnp.bfloat16)
        done = hi == HALF
        reach = (round_up(HALF, LANES) if done else hi, NLON if done else (HALF + hi) // LANES * LANES)
        for part in range(2):
            at = slice(sent[part], reach[part])
            copy = pltpu.make_async_copy(row_ref.at[:, at], out_hbm.at[:, at], out_sems.at[part, i])
            copy.start()
            stores.append(copy)
            sent[part] = reach[part]
    for copy in stores:
        copy.wait()


def fourier_stage(arrived, table):
    devices, slots, _, _, pairs, width = arrived.shape
    fields = width // 2
    total = devices * pairs
    rows = slots * 2 * fields
    spans = pl.cdiv(HALF, 256)
    out = pl.pallas_call(
        fourier_kernel,
        out_shape=jax.ShapeDtypeStruct((rows, NLON), jnp.bfloat16),
        in_specs=[pl.BlockSpec(memory_space=pltpu.VMEM), pl.BlockSpec(memory_space=pl.ANY)],
        out_specs=pl.BlockSpec(memory_space=pl.ANY),
        scratch_shapes=[
            pltpu.VMEM((2, rows, 2 * total), jnp.bfloat16),
            pltpu.VMEM((2, 2, total, HALF), jnp.bfloat16),
            pltpu.VMEM((rows, NLON), jnp.bfloat16),
            pltpu.SemaphoreType.DMA((spans,)),
            pltpu.SemaphoreType.DMA((2, spans)),
        ],
        compiler_params=pltpu.CompilerParams(vmem_limit_bytes=40 * 1024 * 1024),
        cost_estimate=pl.CostEstimate(
            flops=8 * rows * total * HALF, bytes_accessed=8 * total * HALF, transcendentals=0
        ),
        name="fourier",
    )(in_vmem(arrived), in_hbm(table))
    return out.reshape(slots, 2, fields, NLON)


def on_device(wave_pairs, band_owner, spectra_even, spectra_odd, legendre_even, legendre_odd):
    devices = lax.axis_size("wave")
    pairs = round_up(wave_pairs.shape[0], ROWS)
    extra = pairs - wave_pairs.shape[0]
    slots = band_owner.shape[0]
    width = spectra_even.shape[2]
    if extra:
        wave_pairs = jnp.pad(wave_pairs, (0, extra))
        spectra_even, spectra_odd, legendre_even, legendre_odd = (
            jnp.pad(a, ((0, extra), (0, 0), (0, 0)))
            for a in (spectra_even, spectra_odd, legendre_even, legendre_odd)
        )

    own = jnp.pad(jnp.concatenate([wave_pairs, band_owner]), (0, round_up(pairs + slots, LANES) - pairs - slots))
    block = lax.optimization_barrier(jnp.broadcast_to(own, (32,) + own.shape))
    index = lax.optimization_barrier(lax.all_gather(block, "wave", axis=0))[:, 0]
    all_pairs = index[:, :pairs].reshape(-1)
    all_bands = index[:, pairs : pairs + slots].reshape(-1)

    rows = legendre_stage(wave_pairs, spectra_even, spectra_odd, legendre_even, legendre_odd)
    picked = pick_latitudes(all_bands, rows, pairs).reshape(devices, slots, 2, 2, pairs, width)
    arrived = lax.all_to_all(picked, "wave", 0, 0, tiled=True)
    return fourier_stage(arrived, wave_tables(all_pairs))


def solution(mesh):
    return jax.shard_map(
        on_device,
        mesh=mesh,
        in_specs=(
            P("wave"),
            P("wave"),
            P("wave", None, "grp"),
            P("wave", None, "grp"),
            P("wave", None, None),
            P("wave", None, None),
        ),
        out_specs=P("wave", None, "grp", None),
        check_vma=False,
    )
```

```python
import functools
import math

import jax
import jax.numpy as jnp
from jax import lax
from jax.experimental import pallas as pl
from jax.experimental.pallas import tpu as pltpu
from jax.sharding import PartitionSpec as P

M = 1280
NLON = 2688
HALF = NLON // 2
ROWS = 8
LANES = 128


def round_up(value, unit):
    return -(-value // unit) * unit


def legendre_kernel(
    waves_hbm, se_hbm, so_hbm, le_hbm, lo_hbm, out_ref,
    waves_ref, se_ref, so_ref, le_ref, lo_ref, columns_ref, anti_ref, sems, wave_sem,
):
    pairs, lats, he = le_ref.shape
    ho = lo_ref.shape[2]
    groups = pairs // ROWS

    def odd_copies(g):
        at = pl.ds(pl.multiple_of(g * ROWS, ROWS), ROWS)
        return (
            pltpu.make_async_copy(lo_hbm.at[at], lo_ref.at[at], sems.at[0, g]),
            pltpu.make_async_copy(so_hbm.at[at], so_ref.at[at], sems.at[1, g]),
        )

    def even_copies(g):
        at = pl.ds(pl.multiple_of(g * ROWS, ROWS), ROWS)
        return (
            pltpu.make_async_copy(le_hbm.at[at], le_ref.at[at], sems.at[2, g]),
            pltpu.make_async_copy(se_hbm.at[:, at], se_ref.at[g], sems.at[3, g]),
        )

    wave_copy = pltpu.make_async_copy(waves_hbm, waves_ref, wave_sem)
    wave_copy.start()
    for g in range(groups):
        for copy in odd_copies(g) + even_copies(g):
            copy.start()
    wave_copy.wait()

    ids_e = lax.broadcasted_iota(jnp.int32, (lats, he), 1)
    ids_o = lax.broadcasted_iota(jnp.int32, (lats, ho), 1)

    def split(panel, ids, count):
        in_low = ids < count
        zero = jnp.zeros_like(panel)
        lower = jnp.where(in_low, panel, zero)
        upper = jnp.where(in_low, zero, panel)
        return jnp.concatenate([lower, upper], axis=0)

    @pl.loop(0, groups)
    def _(g):
        base = pl.multiple_of(g * ROWS, ROWS)
        for copy in odd_copies(g):
            copy.wait()
        for p in range(ROWS):
            odd = split(lo_ref[base + p], ids_o, (M - waves_ref[base + p]) // 2)
            anti_ref[p] = jnp.dot(odd, so_ref[base + p], preferred_element_type=jnp.float32)
        for copy in even_copies(g):
            copy.wait()
        columns_ref[...] = se_ref[g].astype(jnp.float32).reshape(columns_ref.shape)
        for p in range(ROWS):
            low = waves_ref[base + p]
            parity = low % 2
            even = split(le_ref[base + p], ids_e, (M - low + 1) // 2)
            xe = columns_ref[pl.ds(p, he, stride=ROWS), :].astype(jnp.bfloat16)
            sym = jnp.dot(even, xe, preferred_element_type=jnp.float32)
            anti = anti_ref[p]
            for h, rows in enumerate((sym + anti, sym - anti)):
                for w in range(2):
                    start = (parity ^ w) * (lats * pairs) + base + p
                    out_ref[h, pl.ds(start, lats, stride=pairs), :] = rows[w * lats : (w + 1) * lats]


def in_hbm(x):
    return pltpu.with_memory_space_constraint(x, pltpu.HBM)


def in_vmem(x):
    return pltpu.with_memory_space_constraint(x, pltpu.VMEM)


def legendre_stage(waves, spectra_even, spectra_odd, legendre_even, legendre_odd):
    pairs, he, width = spectra_even.shape
    ho = spectra_odd.shape[1]
    lats = legendre_even.shape[1]
    by_column = jnp.transpose(spectra_even, (1, 0, 2))
    operands = (waves, by_column, spectra_odd, legendre_even, legendre_odd)
    return pl.pallas_call(
        legendre_kernel,
        out_shape=pltpu.VMEM((2, 2 * lats * pairs, width), jnp.float32),
        in_specs=[pl.BlockSpec(memory_space=pl.ANY)] * 5,
        out_specs=pl.BlockSpec(memory_space=pltpu.VMEM),
        scratch_shapes=[
            pltpu.SMEM((pairs,), jnp.int32),
            pltpu.VMEM((pairs // ROWS, he, ROWS, width), jnp.bfloat16),
            pltpu.VMEM((pairs, ho, width), jnp.bfloat16),
            pltpu.VMEM((pairs, lats, he), jnp.bfloat16),
            pltpu.VMEM((pairs, lats, ho), jnp.bfloat16),
            pltpu.VMEM((he * ROWS, width), jnp.float32),
            pltpu.VMEM((ROWS, 2 * lats, width), jnp.float32),
            pltpu.SemaphoreType.DMA((4, pairs // ROWS)),
            pltpu.SemaphoreType.DMA,
        ],
        compiler_params=pltpu.CompilerParams(vmem_limit_bytes=40 * 1024 * 1024),
        cost_estimate=pl.CostEstimate(
            flops=4 * pairs * lats * 2 * (he + ho) * width,
            bytes_accessed=2 * pairs * (he + ho) * (width + lats),
            transcendentals=0,
        ),
        name="legendre",
    )(*(in_hbm(x) for x in operands))


def pick_kernel(bands_ref, rows_ref, out_hbm, out_ref, sems):
    lats, _, _, pairs, _ = out_ref.shape

    def store(slot):
        return pltpu.make_async_copy(out_ref.at[slot], out_hbm.at[slot], sems.at[slot])

    def emit(slot, carry):
        band = bands_ref[slot]
        for h in range(2):
            for w in range(2):
                start = pl.multiple_of((w * lats + band) * pairs, ROWS)
                out_ref[slot, h, w] = rows_ref[h, pl.ds(start, pairs), :].astype(jnp.bfloat16)
        store(slot).start()
        return carry

    def finish(slot, carry):
        store(slot).wait()
        return carry

    lax.fori_loop(0, lats, emit, 0, unroll=4)
    lax.fori_loop(0, lats, finish, 0)


def pick_latitudes(bands, rows, pairs):
    lats = bands.shape[0]
    width = rows.shape[2]
    shape = (lats, 2, 2, pairs, width)
    return pl.pallas_call(
        pick_kernel,
        out_shape=jax.ShapeDtypeStruct(shape, jnp.bfloat16),
        grid_spec=pltpu.PrefetchScalarGridSpec(
            num_scalar_prefetch=1,
            grid=(),
            in_specs=[pl.BlockSpec(memory_space=pltpu.VMEM)],
            out_specs=pl.BlockSpec(memory_space=pl.ANY),
            scratch_shapes=[pltpu.VMEM(shape, jnp.bfloat16), pltpu.SemaphoreType.DMA((lats,))],
        ),
        compiler_params=pltpu.CompilerParams(vmem_limit_bytes=16 * 1024 * 1024),
        name="pick",
    )(bands, in_vmem(rows))


def table_kernel(waves_ref, out_ref):
    unit = 2.0 * math.pi / NLON
    block = 64

    def angle(product):
        turns = jnp.floor(product * (1.0 / NLON))
        return (product - turns * NLON) * unit

    @pl.loop(0, waves_ref.shape[0] // block)
    def _(i):
        at = pl.ds(pl.multiple_of(i * block, block), block)
        low = waves_ref[at, :]
        even = jnp.where(low % 2 == 0, low, M - 1 - low)
        odd = M - 1 - even
        lane = lax.broadcasted_iota(jnp.int32, low.shape, 1).astype(jnp.float32)
        for w, wave in enumerate((even, odd)):
            number = wave.astype(jnp.float32)
            factor = jnp.where(wave == 0, 1.0, 2.0)
            start = angle(number * lane)
            step = angle(number * LANES)
            c, s = factor * jnp.cos(start), -factor * jnp.sin(start)
            dc, ds = jnp.cos(step), jnp.sin(step)
            for b in range(0, HALF, LANES):
                size = min(LANES, HALF - b)
                out_ref[w, 0, at, b : b + size] = c[:, :size].astype(jnp.bfloat16)
                out_ref[w, 1, at, b : b + size] = s[:, :size].astype(jnp.bfloat16)
                c, s = c * dc + s * ds, s * dc - c * ds


def wave_tables(waves):
    total = waves.shape[0]
    return pl.pallas_call(
        table_kernel,
        out_shape=pltpu.VMEM((2, 2, total, HALF), jnp.bfloat16),
        in_specs=[pl.BlockSpec(memory_space=pltpu.VMEM)],
        out_specs=pl.BlockSpec(memory_space=pltpu.VMEM),
        compiler_params=pltpu.CompilerParams(vmem_limit_bytes=16 * 1024 * 1024),
        cost_estimate=pl.CostEstimate(
            flops=4 * 4 * total * HALF, bytes_accessed=8 * total * HALF, transcendentals=8 * total * LANES
        ),
        name="tables",
    )(jnp.broadcast_to(waves[:, None], (total, LANES)))


def fourier_kernel(arrived_hbm, table_ref, out_hbm, left_ref, arrived_ref, row_ref, sems, out_sems):
    devices, slots, _, _, pairs, width = arrived_ref.shape
    fields = width // 2
    total = devices * pairs
    chunk = 256
    ends = list(range(0, HALF, chunk)) + [HALF]
    spans = list(zip(ends[:-1], ends[1:]))
    quarters = [(s, h) for s in range(slots) for h in range(2)]

    def load(i):
        s, h = quarters[i]
        return pltpu.make_async_copy(arrived_hbm.at[:, s, h], arrived_ref.at[:, s, h], sems.at[i])

    for i in range(len(quarters)):
        load(i).start()

    for i, (s, h) in enumerate(quarters):
        load(i).wait()
        for w in range(2):
            x = jnp.concatenate([arrived_ref[d, s, h, w] for d in range(devices)], axis=0)
            xt = x.T
            left_ref[w, i * fields : (i + 1) * fields, :total] = xt[:fields]
            left_ref[w, i * fields : (i + 1) * fields, total:] = xt[fields:]

    stores = []
    sent = [0, round_up(HALF, LANES)]
    for i, (lo, hi) in enumerate(spans):
        e, o = [
            jnp.dot(
                left_ref[w],
                jnp.concatenate([table_ref[w, 0, :, lo:hi], table_ref[w, 1, :, lo:hi]], axis=0),
                preferred_element_type=jnp.float32,
            )
            for w in range(2)
        ]
        row_ref[:, lo:hi] = (e + o).astype(jnp.bfloat16)
        row_ref[:, HALF + lo : HALF + hi] = (e - o).astype(jnp.bfloat16)
        done = hi == HALF
        reach = (round_up(HALF, LANES) if done else hi, NLON if done else (HALF + hi) // LANES * LANES)
        for part in range(2):
            at = slice(sent[part], reach[part])
            copy = pltpu.make_async_copy(row_ref.at[:, at], out_hbm.at[:, at], out_sems.at[part, i])
            copy.start()
            stores.append(copy)
            sent[part] = reach[part]
    for copy in stores:
        copy.wait()


def fourier_stage(arrived, table):
    devices, slots, _, _, pairs, width = arrived.shape
    fields = width // 2
    total = devices * pairs
    rows = slots * 2 * fields
    spans = pl.cdiv(HALF, 256)
    out = pl.pallas_call(
        fourier_kernel,
        out_shape=jax.ShapeDtypeStruct((rows, NLON), jnp.bfloat16),
        in_specs=[pl.BlockSpec(memory_space=pl.ANY), pl.BlockSpec(memory_space=pltpu.VMEM)],
        out_specs=pl.BlockSpec(memory_space=pl.ANY),
        scratch_shapes=[
            pltpu.VMEM((2, rows, 2 * total), jnp.bfloat16),
            pltpu.VMEM(arrived.shape, jnp.bfloat16),
            pltpu.VMEM((rows, NLON), jnp.bfloat16),
            pltpu.SemaphoreType.DMA((slots * 2,)),
            pltpu.SemaphoreType.DMA((2, spans)),
        ],
        compiler_params=pltpu.CompilerParams(vmem_limit_bytes=24 * 1024 * 1024),
        cost_estimate=pl.CostEstimate(
            flops=8 * rows * total * HALF, bytes_accessed=8 * total * HALF, transcendentals=0
        ),
        name="fourier",
    )(in_hbm(arrived), in_vmem(table))
    return out.reshape(slots, 2, fields, NLON)


def on_device(wave_pairs, band_owner, spectra_even, spectra_odd, legendre_even, legendre_odd):
    devices = lax.axis_size("wave")
    pairs = round_up(wave_pairs.shape[0], ROWS)
    extra = pairs - wave_pairs.shape[0]
    slots = band_owner.shape[0]
    width = spectra_even.shape[2]
    if extra:
        wave_pairs = jnp.pad(wave_pairs, (0, extra))
        spectra_even, spectra_odd, legendre_even, legendre_odd = (
            jnp.pad(a, ((0, extra), (0, 0), (0, 0)))
            for a in (spectra_even, spectra_odd, legendre_even, legendre_odd)
        )

    lanes = round_up(pairs + slots, LANES)
    entries = [
        jnp.broadcast_to(x, (devices, 1) + x.shape)
        for x in (wave_pairs, band_owner, jnp.zeros(lanes - pairs - slots, jnp.int32))
    ]
    index = lax.all_to_all(jnp.concatenate(entries, axis=2), "wave", 0, 0, tiled=True)[:, 0]
    all_pairs = index[:, :pairs].reshape(-1)
    all_bands = index[:, pairs : pairs + slots].reshape(-1)

    rows = legendre_stage(wave_pairs, spectra_even, spectra_odd, legendre_even, legendre_odd)
    picked = pick_latitudes(all_bands, rows, pairs).reshape(devices, slots, 2, 2, pairs, width)
    arrived = lax.all_to_all(picked, "wave", 0, 0, tiled=True)
    return fourier_stage(arrived, wave_tables(all_pairs))


def solution(mesh):
    return jax.shard_map(
        on_device,
        mesh=mesh,
        in_specs=(
            P("wave"),
            P("wave"),
            P("wave", None, "grp"),
            P("wave", None, "grp"),
            P("wave", None, None),
            P("wave", None, None),
        ),
        out_specs=P("wave", None, "grp", None),
        check_vma=False,
    )
```

```python
import functools
import math

import jax
import jax.numpy as jnp
from jax import lax
from jax.experimental import pallas as pl
from jax.experimental.pallas import tpu as pltpu
from jax.sharding import PartitionSpec as P

M = 1280
NLON = 2688
HALF = NLON // 2
ROWS = 8
LANES = 128


def round_up(value, unit):
    return -(-value // unit) * unit


def legendre_kernel(
    waves_hbm, se_hbm, so_hbm, le_hbm, lo_hbm, out_ref,
    waves_ref, se_ref, so_ref, le_ref, lo_ref, columns_ref, anti_ref, sems, wave_sem,
):
    pairs, lats, he = le_ref.shape
    ho = lo_ref.shape[2]
    groups = pairs // ROWS

    def odd_copies(g):
        at = pl.ds(pl.multiple_of(g * ROWS, ROWS), ROWS)
        return (
            pltpu.make_async_copy(lo_hbm.at[at], lo_ref.at[at], sems.at[0, g]),
            pltpu.make_async_copy(so_hbm.at[at], so_ref.at[at], sems.at[1, g]),
        )

    def even_copies(g):
        at = pl.ds(pl.multiple_of(g * ROWS, ROWS), ROWS)
        return (
            pltpu.make_async_copy(le_hbm.at[at], le_ref.at[at], sems.at[2, g]),
            pltpu.make_async_copy(se_hbm.at[:, at], se_ref.at[g], sems.at[3, g]),
        )

    wave_copy = pltpu.make_async_copy(waves_hbm, waves_ref, wave_sem)
    wave_copy.start()
    for g in range(groups):
        for copy in odd_copies(g) + even_copies(g):
            copy.start()
    wave_copy.wait()

    ids_e = lax.broadcasted_iota(jnp.int32, (lats, he), 1)
    ids_o = lax.broadcasted_iota(jnp.int32, (lats, ho), 1)

    def split(panel, ids, count):
        in_low = ids < count
        zero = jnp.zeros_like(panel)
        lower = jnp.where(in_low, panel, zero)
        upper = jnp.where(in_low, zero, panel)
        return jnp.concatenate([lower, upper], axis=0)

    @pl.loop(0, groups)
    def _(g):
        base = pl.multiple_of(g * ROWS, ROWS)
        for copy in odd_copies(g):
            copy.wait()
        for p in range(ROWS):
            odd = split(lo_ref[base + p], ids_o, (M - waves_ref[base + p]) // 2)
            anti_ref[p] = jnp.dot(odd, so_ref[base + p], preferred_element_type=jnp.float32)
        for copy in even_copies(g):
            copy.wait()
        columns_ref[...] = se_ref[g].astype(jnp.float32).reshape(columns_ref.shape)
        for p in range(ROWS):
            low = waves_ref[base + p]
            parity = low % 2
            even = split(le_ref[base + p], ids_e, (M - low + 1) // 2)
            xe = columns_ref[pl.ds(p, he, stride=ROWS), :].astype(jnp.bfloat16)
            sym = jnp.dot(even, xe, preferred_element_type=jnp.float32)
            anti = anti_ref[p]
            for h, rows in enumerate((sym + anti, sym - anti)):
                for w in range(2):
                    start = (parity ^ w) * (lats * pairs) + base + p
                    out_ref[h, pl.ds(start, lats, stride=pairs), :] = rows[w * lats : (w + 1) * lats]


def in_hbm(x):
    return pltpu.with_memory_space_constraint(x, pltpu.HBM)


def in_vmem(x):
    return pltpu.with_memory_space_constraint(x, pltpu.VMEM)


def legendre_stage(waves, spectra_even, spectra_odd, legendre_even, legendre_odd):
    pairs, he, width = spectra_even.shape
    ho = spectra_odd.shape[1]
    lats = legendre_even.shape[1]
    by_column = jnp.transpose(spectra_even, (1, 0, 2))
    operands = (waves, by_column, spectra_odd, legendre_even, legendre_odd)
    return pl.pallas_call(
        legendre_kernel,
        out_shape=pltpu.VMEM((2, 2 * lats * pairs, width), jnp.float32),
        in_specs=[pl.BlockSpec(memory_space=pl.ANY)] * 5,
        out_specs=pl.BlockSpec(memory_space=pltpu.VMEM),
        scratch_shapes=[
            pltpu.SMEM((pairs,), jnp.int32),
            pltpu.VMEM((pairs // ROWS, he, ROWS, width), jnp.bfloat16),
            pltpu.VMEM((pairs, ho, width), jnp.bfloat16),
            pltpu.VMEM((pairs, lats, he), jnp.bfloat16),
            pltpu.VMEM((pairs, lats, ho), jnp.bfloat16),
            pltpu.VMEM((he * ROWS, width), jnp.float32),
            pltpu.VMEM((ROWS, 2 * lats, width), jnp.float32),
            pltpu.SemaphoreType.DMA((4, pairs // ROWS)),
            pltpu.SemaphoreType.DMA,
        ],
        compiler_params=pltpu.CompilerParams(vmem_limit_bytes=40 * 1024 * 1024),
        cost_estimate=pl.CostEstimate(
            flops=4 * pairs * lats * 2 * (he + ho) * width,
            bytes_accessed=2 * pairs * (he + ho) * (width + lats),
            transcendentals=0,
        ),
        name="legendre",
    )(*(in_hbm(x) for x in operands))


def pick_kernel(crossed, column, *refs):
    *index_refs, rows_ref, out_ref = refs
    lats, _, _, pairs, _ = out_ref.shape
    me = lax.axis_index("wave") if crossed else 0
    first = 0
    for index_ref in index_refs:
        count = index_ref.shape[0]
        slots = lats // (count * len(index_refs))

        def emit(row, carry, index_ref=index_ref, first=first, slots=slots):
            owner = me ^ (first + row)
            for s in range(slots):
                band = index_ref[row, column + s]
                for h in range(2):
                    for w in range(2):
                        start = pl.multiple_of((w * lats + band) * pairs, ROWS)
                        out_ref[owner * slots + s, h, w] = rows_ref[h, pl.ds(start, pairs), :].astype(jnp.bfloat16)
            return carry

        lax.fori_loop(0, count, emit, 0, unroll=4)
        first += count


def pick_latitudes(crossed, column, index, rows, lats, pairs):
    width = rows.shape[2]
    return pl.pallas_call(
        functools.partial(pick_kernel, crossed, column),
        out_shape=jax.ShapeDtypeStruct((lats, 2, 2, pairs, width), jnp.bfloat16),
        grid_spec=pltpu.PrefetchScalarGridSpec(
            num_scalar_prefetch=len(index),
            grid=(),
            in_specs=[pl.BlockSpec(memory_space=pltpu.VMEM)],
            out_specs=pl.BlockSpec(memory_space=pltpu.VMEM),
        ),
        compiler_params=pltpu.CompilerParams(vmem_limit_bytes=16 * 1024 * 1024),
        name="pick",
    )(*index, in_vmem(rows))


def table_kernel(waves_ref, out_ref):
    unit = 2.0 * math.pi / NLON
    block = 64

    def angle(product):
        turns = jnp.floor(product * (1.0 / NLON))
        return (product - turns * NLON) * unit

    @pl.loop(0, waves_ref.shape[0] // block)
    def _(i):
        at = pl.ds(pl.multiple_of(i * block, block), block)
        low = waves_ref[at, :]
        even = jnp.where(low % 2 == 0, low, M - 1 - low)
        odd = M - 1 - even
        lane = lax.broadcasted_iota(jnp.int32, low.shape, 1).astype(jnp.float32)
        for w, wave in enumerate((even, odd)):
            number = wave.astype(jnp.float32)
            factor = jnp.where(wave == 0, 1.0, 2.0)
            start = angle(number * lane)
            step = angle(number * LANES)
            c, s = factor * jnp.cos(start), -factor * jnp.sin(start)
            dc, ds = jnp.cos(step), jnp.sin(step)
            for b in range(0, HALF, LANES):
                size = min(LANES, HALF - b)
                out_ref[w, 0, at, b : b + size] = c[:, :size].astype(jnp.bfloat16)
                out_ref[w, 1, at, b : b + size] = s[:, :size].astype(jnp.bfloat16)
                c, s = c * dc + s * ds, s * dc - c * ds


def wave_tables(waves):
    total = waves.shape[0]
    return pl.pallas_call(
        table_kernel,
        out_shape=jax.ShapeDtypeStruct((2, 2, total, HALF), jnp.bfloat16),
        in_specs=[pl.BlockSpec(memory_space=pltpu.VMEM)],
        out_specs=pl.BlockSpec(memory_space=pltpu.VMEM),
        compiler_params=pltpu.CompilerParams(vmem_limit_bytes=16 * 1024 * 1024),
        cost_estimate=pl.CostEstimate(
            flops=4 * 4 * total * HALF, bytes_accessed=8 * total * HALF, transcendentals=8 * total * LANES
        ),
        name="tables",
    )(jnp.broadcast_to(waves[:, None], (total, LANES)))


def fourier_kernel(arrived_ref, table_hbm, out_hbm, left_ref, table_ref, row_ref, sems, out_sems):
    devices, slots, _, _, pairs, width = arrived_ref.shape
    fields = width // 2
    total = devices * pairs
    chunk = 256
    ends = list(range(0, HALF, chunk)) + [HALF]
    spans = list(zip(ends[:-1], ends[1:]))

    def load(i):
        at = slice(*spans[i])
        return pltpu.make_async_copy(table_hbm.at[:, :, :, at], table_ref.at[:, :, :, at], sems.at[i])

    for i in range(len(spans)):
        load(i).start()

    for w in range(2):
        for s in range(slots):
            for h in range(2):
                x = jnp.concatenate([arrived_ref[d, s, h, w] for d in range(devices)], axis=0)
                xt = x.T
                r = (s * 2 + h) * fields
                left_ref[w, r : r + fields, :total] = xt[:fields]
                left_ref[w, r : r + fields, total:] = xt[fields:]

    stores = []
    sent = [0, round_up(HALF, LANES)]
    for i, (lo, hi) in enumerate(spans):
        load(i).wait()
        e, o = [
            jnp.dot(
                left_ref[w],
                jnp.concatenate([table_ref[w, 0, :, lo:hi], table_ref[w, 1, :, lo:hi]], axis=0),
                preferred_element_type=jnp.float32,
            )
            for w in range(2)
        ]
        row_ref[:, lo:hi] = (e + o).astype(jnp.bfloat16)
        row_ref[:, HALF + lo : HALF + hi] = (e - o).astype(jnp.bfloat16)
        done = hi == HALF
        reach = (round_up(HALF, LANES) if done else hi, NLON if done else (HALF + hi) // LANES * LANES)
        for part in range(2):
            at = slice(sent[part], reach[part])
            copy = pltpu.make_async_copy(row_ref.at[:, at], out_hbm.at[:, at], out_sems.at[part, i])
            copy.start()
            stores.append(copy)
            sent[part] = reach[part]
    for copy in stores:
        copy.wait()


def fourier_stage(arrived, table):
    devices, slots, _, _, pairs, width = arrived.shape
    fields = width // 2
    total = devices * pairs
    rows = slots * 2 * fields
    spans = pl.cdiv(HALF, 256)
    out = pl.pallas_call(
        fourier_kernel,
        out_shape=jax.ShapeDtypeStruct((rows, NLON), jnp.bfloat16),
        in_specs=[pl.BlockSpec(memory_space=pltpu.VMEM), pl.BlockSpec(memory_space=pl.ANY)],
        out_specs=pl.BlockSpec(memory_space=pl.ANY),
        scratch_shapes=[
            pltpu.VMEM((2, rows, 2 * total), jnp.bfloat16),
            pltpu.VMEM((2, 2, total, HALF), jnp.bfloat16),
            pltpu.VMEM((rows, NLON), jnp.bfloat16),
            pltpu.SemaphoreType.DMA((spans,)),
            pltpu.SemaphoreType.DMA((2, spans)),
        ],
        compiler_params=pltpu.CompilerParams(vmem_limit_bytes=40 * 1024 * 1024),
        cost_estimate=pl.CostEstimate(
            flops=8 * rows * total * HALF, bytes_accessed=8 * total * HALF, transcendentals=0
        ),
        name="fourier",
    )(arrived, table)
    return out.reshape(slots, 2, fields, NLON)


def on_device(wave_pairs, band_owner, spectra_even, spectra_odd, legendre_even, legendre_odd):
    devices = lax.axis_size("wave")
    pairs = round_up(wave_pairs.shape[0], ROWS)
    extra = pairs - wave_pairs.shape[0]
    slots = band_owner.shape[0]
    width = spectra_even.shape[2]
    if extra:
        wave_pairs = jnp.pad(wave_pairs, (0, extra))
        spectra_even, spectra_odd, legendre_even, legendre_odd = (
            jnp.pad(a, ((0, extra), (0, 0), (0, 0)))
            for a in (spectra_even, spectra_odd, legendre_even, legendre_odd)
        )

    crossed = devices == 16
    index = gather_index(devices, crossed, wave_pairs, band_owner)
    rows = legendre_stage(wave_pairs, spectra_even, spectra_odd, legendre_even, legendre_odd)
    picked = pick_latitudes(crossed, pairs, index, rows, devices * slots, pairs)
    index, picked = lax.optimization_barrier((index, picked))
    arrived = lax.all_to_all(picked.reshape(devices, slots, 2, 2, pairs, width), "wave", 0, 0, tiled=True)
    all_pairs = jnp.concatenate(index, axis=0)[:, :pairs]
    if crossed:
        order = lax.axis_index("wave") ^ jnp.arange(devices)
        chosen = (order[:, None] == jnp.arange(devices)[None])[:, :, None]
        all_pairs = jnp.sum(jnp.where(chosen, all_pairs[None], 0), axis=1)
    return fourier_stage(arrived, wave_tables(all_pairs.reshape(-1)))


def gather_index(devices, crossed, waves, bands):
    rest = round_up(waves.shape[0] + bands.shape[0], LANES) - waves.shape[0] - bands.shape[0]
    own = jnp.concatenate([waves, bands, jnp.zeros(rest, jnp.int32)])
    if not crossed:
        own = jnp.broadcast_to(own, (devices, 1) + own.shape)
        return [lax.all_to_all(own, "wave", 0, 0, tiled=True)[:, 0]]

    def send(x, k):
        return lax.ppermute(x, "wave", [(i, i ^ k) for i in range(devices)])

    near = jnp.concatenate([own[None]] + [send(own[None], k) for k in (1, 2, 3)], axis=0)
    return [near] + [send(near, k) for k in (4, 8, 12)]


def solution(mesh):
    return jax.shard_map(
        on_device,
        mesh=mesh,
        in_specs=(
            P("wave"),
            P("wave"),
            P("wave", None, "grp"),
            P("wave", None, "grp"),
            P("wave", None, None),
            P("wave", None, None),
        ),
        out_specs=P("wave", None, "grp", None),
        check_vma=False,
    )
```

```python
import functools
import math

import jax
import jax.numpy as jnp
from jax import lax
from jax.experimental import pallas as pl
from jax.experimental.pallas import tpu as pltpu
from jax.sharding import PartitionSpec as P

M = 1280
NLON = 2688
QUARTER = NLON // 4
CHUNK = 256
ROWS = 8
LANES = 128


def round_up(value, unit):
    return -(-value // unit) * unit


def legendre_kernel(
    waves_hbm, se_hbm, so_hbm, le_hbm, lo_hbm, out_ref,
    waves_ref, se_ref, so_ref, le_ref, lo_ref, columns_ref, anti_ref, sems, wave_sem,
):
    pairs, lats, he = le_ref.shape
    ho = lo_ref.shape[2]
    groups = pairs // ROWS

    def odd_copies(g):
        at = pl.ds(pl.multiple_of(g * ROWS, ROWS), ROWS)
        return (
            pltpu.make_async_copy(lo_hbm.at[at], lo_ref.at[at], sems.at[0, g]),
            pltpu.make_async_copy(so_hbm.at[at], so_ref.at[at], sems.at[1, g]),
        )

    def even_copies(g):
        at = pl.ds(pl.multiple_of(g * ROWS, ROWS), ROWS)
        return (
            pltpu.make_async_copy(le_hbm.at[at], le_ref.at[at], sems.at[2, g]),
            pltpu.make_async_copy(se_hbm.at[:, at], se_ref.at[g], sems.at[3, g]),
        )

    wave_copy = pltpu.make_async_copy(waves_hbm, waves_ref, wave_sem)
    wave_copy.start()
    ahead = 2
    for g in range(min(ahead, groups)):
        for copy in odd_copies(g) + even_copies(g):
            copy.start()
    wave_copy.wait()

    ids_e = lax.broadcasted_iota(jnp.int32, (lats, he), 1)
    ids_o = lax.broadcasted_iota(jnp.int32, (lats, ho), 1)

    def split(panel, ids, count):
        in_low = ids < count
        zero = jnp.zeros_like(panel)
        lower = jnp.where(in_low, panel, zero)
        upper = jnp.where(in_low, zero, panel)
        return jnp.concatenate([lower, upper], axis=0)

    @pl.loop(0, groups)
    def _(g):
        base = pl.multiple_of(g * ROWS, ROWS)
        for copy in odd_copies(g):
            copy.wait()

        @pl.when(g + ahead < groups)
        def _():
            for copy in odd_copies(g + ahead) + even_copies(g + ahead):
                copy.start()

        for p in range(ROWS):
            odd = split(lo_ref[base + p], ids_o, (M - waves_ref[base + p]) // 2)
            anti_ref[p] = jnp.dot(odd, so_ref[base + p], preferred_element_type=jnp.float32)
        for copy in even_copies(g):
            copy.wait()
        columns_ref[...] = se_ref[g].astype(jnp.float32).reshape(columns_ref.shape)
        for p in range(ROWS):
            low = waves_ref[base + p]
            parity = low % 2
            even = split(le_ref[base + p], ids_e, (M - low + 1) // 2)
            xe = columns_ref[pl.ds(p, he, stride=ROWS), :].astype(jnp.bfloat16)
            sym = jnp.dot(even, xe, preferred_element_type=jnp.float32)
            anti = anti_ref[p]
            for h, rows in enumerate((sym + anti, sym - anti)):
                for w in range(2):
                    start = (parity ^ w) * (lats * pairs) + base + p
                    out_ref[h, pl.ds(start, lats, stride=pairs), :] = rows[w * lats : (w + 1) * lats]


def in_hbm(x):
    return pltpu.with_memory_space_constraint(x, pltpu.HBM)


def in_vmem(x):
    return pltpu.with_memory_space_constraint(x, pltpu.VMEM)


def legendre_stage(waves, spectra_even, spectra_odd, legendre_even, legendre_odd):
    pairs, he, width = spectra_even.shape
    ho = spectra_odd.shape[1]
    lats = legendre_even.shape[1]
    by_column = jnp.transpose(spectra_even, (1, 0, 2))
    operands = (waves, by_column, spectra_odd, legendre_even, legendre_odd)
    return pl.pallas_call(
        legendre_kernel,
        out_shape=pltpu.VMEM((2, 2 * lats * pairs, width), jnp.float32),
        in_specs=[pl.BlockSpec(memory_space=pl.ANY)] * 5,
        out_specs=pl.BlockSpec(memory_space=pltpu.VMEM),
        scratch_shapes=[
            pltpu.SMEM((pairs,), jnp.int32),
            pltpu.VMEM((pairs // ROWS, he, ROWS, width), jnp.bfloat16),
            pltpu.VMEM((pairs, ho, width), jnp.bfloat16),
            pltpu.VMEM((pairs, lats, he), jnp.bfloat16),
            pltpu.VMEM((pairs, lats, ho), jnp.bfloat16),
            pltpu.VMEM((he * ROWS, width), jnp.float32),
            pltpu.VMEM((ROWS, 2 * lats, width), jnp.float32),
            pltpu.SemaphoreType.DMA((4, pairs // ROWS)),
            pltpu.SemaphoreType.DMA,
        ],
        compiler_params=pltpu.CompilerParams(vmem_limit_bytes=40 * 1024 * 1024),
        cost_estimate=pl.CostEstimate(
            flops=4 * pairs * lats * 2 * (he + ho) * width,
            bytes_accessed=2 * pairs * (he + ho) * (width + lats),
            transcendentals=0,
        ),
        name="legendre",
    )(*(in_hbm(x) for x in operands))


def pick_kernel(bands_ref, rows_ref, out_hbm, out_ref, sems):
    lats, _, _, pairs, _ = out_ref.shape
    piece = lats // sems.shape[0]

    def store(i):
        at = pl.ds(i * piece, piece)
        return pltpu.make_async_copy(out_ref.at[at], out_hbm.at[at], sems.at[i])

    def emit(slot, carry):
        band = bands_ref[slot]
        for h in range(2):
            for w in range(2):
                start = pl.multiple_of((w * lats + band) * pairs, ROWS)
                out_ref[slot, h, w] = rows_ref[h, pl.ds(start, pairs), :].astype(jnp.bfloat16)
        return carry

    for i in range(sems.shape[0]):
        lax.fori_loop(i * piece, (i + 1) * piece, emit, 0, unroll=4)
        store(i).start()
    for i in range(sems.shape[0]):
        store(i).wait()


def pick_latitudes(bands, rows, pairs):
    lats = bands.shape[0]
    width = rows.shape[2]
    shape = (lats, 2, 2, pairs, width)
    return pl.pallas_call(
        pick_kernel,
        out_shape=pltpu.HBM(shape, jnp.bfloat16),
        grid_spec=pltpu.PrefetchScalarGridSpec(
            num_scalar_prefetch=1,
            grid=(),
            in_specs=[pl.BlockSpec(memory_space=pltpu.VMEM)],
            out_specs=pl.BlockSpec(memory_space=pl.ANY),
            scratch_shapes=[pltpu.VMEM(shape, jnp.bfloat16), pltpu.SemaphoreType.DMA((4,))],
        ),
        compiler_params=pltpu.CompilerParams(vmem_limit_bytes=16 * 1024 * 1024),
        name="pick",
    )(bands, in_vmem(rows))


def even_wave(low):
    return jnp.where(low % 2 == 0, low, M - 1 - low)


def table_kernel(waves_ref, out_ref):
    even = even_wave(waves_ref[...])
    odd = M - 1 - even
    lane = lax.broadcasted_iota(jnp.int32, even.shape, 1).astype(jnp.float32)
    unit = 2.0 * math.pi / NLON

    def angle(product):
        turns = jnp.floor(product * (1.0 / NLON))
        return (product - turns * NLON) * unit

    for w, wave in enumerate((even, odd)):
        number = wave.astype(jnp.float32)
        factor = jnp.where(wave == 0, 1.0, 2.0)
        start = angle(number * lane)
        step = angle(number * LANES)
        c, s = factor * jnp.cos(start), -factor * jnp.sin(start)
        dc, ds = jnp.cos(step), jnp.sin(step)
        for b in range(0, QUARTER, LANES):
            at = slice(b % CHUNK, b % CHUNK + LANES)
            out_ref[b // CHUNK, w, 0, :, at] = c.astype(jnp.bfloat16)
            out_ref[b // CHUNK, w, 1, :, at] = s.astype(jnp.bfloat16)
            c, s = c * dc + s * ds, s * dc - c * ds


def wave_tables(waves):
    total = waves.shape[0]
    rows = 64
    chunks = pl.cdiv(QUARTER, CHUNK)
    return pl.pallas_call(
        table_kernel,
        out_shape=pltpu.HBM((chunks, 2, 2, total, CHUNK), jnp.bfloat16),
        grid=(total // rows,),
        in_specs=[pl.BlockSpec((rows, LANES), lambda i: (i, 0))],
        out_specs=pl.BlockSpec((chunks, 2, 2, rows, CHUNK), lambda i: (0, 0, 0, i, 0)),
        compiler_params=pltpu.CompilerParams(vmem_limit_bytes=32 * 1024 * 1024),
        cost_estimate=pl.CostEstimate(
            flops=16 * total * QUARTER, bytes_accessed=8 * total * QUARTER, transcendentals=8 * total * LANES
        ),
        name="tables",
    )(jnp.broadcast_to(waves[:, None], (total, LANES)))


def fourier_kernel(
    arrived_ref, sign_hbm, table_hbm, out_hbm, left_ref, sign_ref, table_ref, row_ref, sems, sign_sem, out_sems
):
    devices, slots, _, _, pairs, width = arrived_ref.shape
    fields = width // 2
    total = devices * pairs
    chunks = table_ref.shape[0]
    rows = 2 * fields

    def load(i):
        return pltpu.make_async_copy(table_hbm.at[i], table_ref.at[i], sems.at[i])

    sign_copy = pltpu.make_async_copy(sign_hbm, sign_ref, sign_sem)
    sign_copy.start()
    for i in range(chunks):
        load(i).start()

    stores = []
    for s in range(slots):
        turned = []
        for h in range(2):
            for w in range(2):
                x = jnp.concatenate([arrived_ref[d, s, h, w] for d in range(devices)], axis=0)
                xt = x.T
                at = slice(h * fields, (h + 1) * fields)
                left_ref[s, w, at, :total] = xt[:fields]
                left_ref[s, w, at, total:] = xt[fields:]
                turned.append((h, w, xt))
        if s == 0:
            sign_copy.wait()
        sign = sign_ref[0:1, :]
        for h, w, xt in turned:
            at = slice(rows + h * fields, rows + (h + 1) * fields)
            signed = (xt.astype(jnp.float32) * sign).astype(jnp.bfloat16)
            re, im = signed[:fields], signed[fields:]
            left_ref[s, w, at, :total] = im if w else re
            left_ref[s, w, at, total:] = -re if w else im
        base = slice(s * rows, (s + 1) * rows)
        for i in range(chunks):
            if s == 0:
                load(i).wait()
            lo, hi = i * CHUNK, min((i + 1) * CHUNK, QUARTER)
            e, o = [
                jnp.dot(
                    left_ref[s, w],
                    table_ref[i, w].reshape(2 * total, CHUNK),
                    preferred_element_type=jnp.float32,
                )[:, : hi - lo]
                for w in range(2)
            ]
            plus, minus = e + o, e - o
            for k, part in enumerate((plus[:rows], plus[rows:], minus[:rows], minus[rows:])):
                row_ref[base, k * QUARTER + lo : k * QUARTER + hi] = part.astype(jnp.bfloat16)
        copy = pltpu.make_async_copy(row_ref.at[base], out_hbm.at[base], out_sems.at[s])
        copy.start()
        stores.append(copy)
    for copy in stores:
        copy.wait()


def fourier_stage(arrived, sign, table):
    devices, slots, _, _, pairs, width = arrived.shape
    fields = width // 2
    total = devices * pairs
    rows = slots * 2 * fields
    out = pl.pallas_call(
        fourier_kernel,
        out_shape=jax.ShapeDtypeStruct((rows, NLON), jnp.bfloat16),
        in_specs=[pl.BlockSpec(memory_space=pltpu.VMEM)] + [pl.BlockSpec(memory_space=pl.ANY)] * 2,
        out_specs=pl.BlockSpec(memory_space=pl.ANY),
        scratch_shapes=[
            pltpu.VMEM((slots, 2, 4 * fields, 2 * total), jnp.bfloat16),
            pltpu.VMEM(sign.shape, jnp.float32),
            pltpu.VMEM(table.shape, jnp.bfloat16),
            pltpu.VMEM((rows, NLON), jnp.bfloat16),
            pltpu.SemaphoreType.DMA((table.shape[0],)),
            pltpu.SemaphoreType.DMA,
            pltpu.SemaphoreType.DMA((slots,)),
        ],
        compiler_params=pltpu.CompilerParams(vmem_limit_bytes=32 * 1024 * 1024),
        cost_estimate=pl.CostEstimate(
            flops=16 * rows * total * QUARTER, bytes_accessed=8 * total * QUARTER, transcendentals=0
        ),
        name="fourier",
    )(arrived, in_hbm(sign), in_hbm(table))
    return out.reshape(slots, 2, fields, NLON)


def on_device(wave_pairs, band_owner, spectra_even, spectra_odd, legendre_even, legendre_odd):
    devices = lax.axis_size("wave")
    pairs = round_up(wave_pairs.shape[0], ROWS)
    extra = pairs - wave_pairs.shape[0]
    slots = band_owner.shape[0]
    width = spectra_even.shape[2]
    if extra:
        wave_pairs = jnp.pad(wave_pairs, (0, extra))
        spectra_even, spectra_odd, legendre_even, legendre_odd = (
            jnp.pad(a, ((0, extra), (0, 0), (0, 0)))
            for a in (spectra_even, spectra_odd, legendre_even, legendre_odd)
        )

    rest = round_up(pairs + slots, LANES) - pairs - slots
    own = jnp.concatenate([wave_pairs, band_owner, jnp.zeros(rest, jnp.int32)])
    own = jnp.broadcast_to(own, (devices, 1) + own.shape)
    index = lax.all_to_all(own, "wave", 0, 0, tiled=True)[:, 0]
    all_bands = index[:, pairs : pairs + slots].reshape(-1)
    rows = legendre_stage(wave_pairs, spectra_even, spectra_odd, legendre_even, legendre_odd)
    picked = pick_latitudes(all_bands, rows, pairs)
    index, picked = lax.optimization_barrier((index, picked))
    arrived = lax.all_to_all(picked.reshape(devices, slots, 2, 2, pairs, width), "wave", 0, 0, tiled=True)
    all_pairs = index[:, :pairs].reshape(-1)
    sign = jnp.where(even_wave(all_pairs) % 4 == 0, 1.0, -1.0).astype(jnp.float32)
    sign = jnp.broadcast_to(sign, (ROWS,) + sign.shape)
    return fourier_stage(arrived, sign, wave_tables(all_pairs))


def solution(mesh):
    return jax.shard_map(
        on_device,
        mesh=mesh,
        in_specs=(
            P("wave"),
            P("wave"),
            P("wave", None, "grp"),
            P("wave", None, "grp"),
            P("wave", None, None),
            P("wave", None, None),
        ),
        out_specs=P("wave", None, "grp", None),
        check_vma=False,
    )
```

```python
import functools
import math

import jax
import jax.numpy as jnp
from jax import lax
from jax.experimental import pallas as pl
from jax.experimental.pallas import tpu as pltpu
from jax.sharding import PartitionSpec as P

M = 1280
NLON = 2688
QUARTER = NLON // 4
CHUNK = 256
ROWS = 8
LANES = 128


def round_up(value, unit):
    return -(-value // unit) * unit


def legendre_kernel(
    waves_hbm, se_hbm, so_hbm, le_hbm, lo_hbm, out_ref,
    waves_ref, se_ref, so_ref, le_ref, lo_ref, columns_ref, anti_ref, sems, wave_sem,
):
    pairs, lats, he = le_ref.shape
    ho = lo_ref.shape[2]
    groups = pairs // ROWS

    def odd_copies(g):
        at = pl.ds(pl.multiple_of(g * ROWS, ROWS), ROWS)
        return (
            pltpu.make_async_copy(lo_hbm.at[at], lo_ref.at[at], sems.at[0, g]),
            pltpu.make_async_copy(so_hbm.at[at], so_ref.at[at], sems.at[1, g]),
        )

    def even_copies(g):
        at = pl.ds(pl.multiple_of(g * ROWS, ROWS), ROWS)
        return (
            pltpu.make_async_copy(le_hbm.at[at], le_ref.at[at], sems.at[2, g]),
            pltpu.make_async_copy(se_hbm.at[:, at], se_ref.at[g], sems.at[3, g]),
        )

    wave_copy = pltpu.make_async_copy(waves_hbm, waves_ref, wave_sem)
    wave_copy.start()
    ahead = 2
    for g in range(min(ahead, groups)):
        for copy in odd_copies(g) + even_copies(g):
            copy.start()
    wave_copy.wait()

    ids_e = lax.broadcasted_iota(jnp.int32, (1, he), 1)
    ids_o = lax.broadcasted_iota(jnp.int32, (1, ho), 1)

    def split(panel, ids, count):
        in_low = jnp.where(ids < count, 1.0, 0.0).astype(jnp.bfloat16)
        lower = panel * in_low
        return jnp.concatenate([lower, panel - lower], axis=0)

    @pl.loop(0, groups)
    def _(g):
        base = pl.multiple_of(g * ROWS, ROWS)
        for copy in odd_copies(g):
            copy.wait()

        @pl.when(g + ahead < groups)
        def _():
            for copy in odd_copies(g + ahead) + even_copies(g + ahead):
                copy.start()

        for p in range(ROWS):
            odd = split(lo_ref[base + p], ids_o, (M - waves_ref[base + p]) // 2)
            anti_ref[p] = jnp.dot(odd, so_ref[base + p], preferred_element_type=jnp.float32)
        for copy in even_copies(g):
            copy.wait()
        columns_ref[...] = se_ref[g].astype(jnp.float32).reshape(columns_ref.shape)
        for p in range(ROWS):
            low = waves_ref[base + p]
            parity = low % 2
            even = split(le_ref[base + p], ids_e, (M - low + 1) // 2)
            xe = columns_ref[pl.ds(p, he, stride=ROWS), :].astype(jnp.bfloat16)
            sym = jnp.dot(even, xe, preferred_element_type=jnp.float32)
            anti = anti_ref[p]
            for h, rows in enumerate((sym + anti, sym - anti)):
                for w in range(2):
                    start = (parity ^ w) * (lats * pairs) + base + p
                    out_ref[h, pl.ds(start, lats, stride=pairs), :] = rows[w * lats : (w + 1) * lats]


def in_hbm(x):
    return pltpu.with_memory_space_constraint(x, pltpu.HBM)


def in_vmem(x):
    return pltpu.with_memory_space_constraint(x, pltpu.VMEM)


def legendre_stage(waves, spectra_even, spectra_odd, legendre_even, legendre_odd):
    pairs, he, width = spectra_even.shape
    ho = spectra_odd.shape[1]
    lats = legendre_even.shape[1]
    by_column = jnp.transpose(spectra_even, (1, 0, 2))
    operands = (waves, by_column, spectra_odd, legendre_even, legendre_odd)
    return pl.pallas_call(
        legendre_kernel,
        out_shape=pltpu.VMEM((2, 2 * lats * pairs, width), jnp.float32),
        in_specs=[pl.BlockSpec(memory_space=pl.ANY)] * 5,
        out_specs=pl.BlockSpec(memory_space=pltpu.VMEM),
        scratch_shapes=[
            pltpu.SMEM((pairs,), jnp.int32),
            pltpu.VMEM((pairs // ROWS, he, ROWS, width), jnp.bfloat16),
            pltpu.VMEM((pairs, ho, width), jnp.bfloat16),
            pltpu.VMEM((pairs, lats, he), jnp.bfloat16),
            pltpu.VMEM((pairs, lats, ho), jnp.bfloat16),
            pltpu.VMEM((he * ROWS, width), jnp.float32),
            pltpu.VMEM((ROWS, 2 * lats, width), jnp.float32),
            pltpu.SemaphoreType.DMA((4, pairs // ROWS)),
            pltpu.SemaphoreType.DMA,
        ],
        compiler_params=pltpu.CompilerParams(vmem_limit_bytes=40 * 1024 * 1024),
        cost_estimate=pl.CostEstimate(
            flops=4 * pairs * lats * 2 * (he + ho) * width,
            bytes_accessed=2 * pairs * (he + ho) * (width + lats),
            transcendentals=0,
        ),
        name="legendre",
    )(*(in_hbm(x) for x in operands))


def pick_kernel(bands_ref, rows_ref, out_hbm, out_ref, sems):
    lats, _, _, pairs, _ = out_ref.shape
    piece = lats // sems.shape[0]

    def store(i):
        at = pl.ds(i * piece, piece)
        return pltpu.make_async_copy(out_ref.at[at], out_hbm.at[at], sems.at[i])

    def emit(slot, carry):
        band = bands_ref[slot]
        for h in range(2):
            for w in range(2):
                start = pl.multiple_of((w * lats + band) * pairs, ROWS)
                out_ref[slot, h, w] = rows_ref[h, pl.ds(start, pairs), :].astype(jnp.bfloat16)
        return carry

    for i in range(sems.shape[0]):
        lax.fori_loop(i * piece, (i + 1) * piece, emit, 0, unroll=4)
        store(i).start()
    for i in range(sems.shape[0]):
        store(i).wait()


def pick_latitudes(bands, rows, pairs):
    lats = bands.shape[0]
    width = rows.shape[2]
    shape = (lats, 2, 2, pairs, width)
    return pl.pallas_call(
        pick_kernel,
        out_shape=pltpu.HBM(shape, jnp.bfloat16),
        grid_spec=pltpu.PrefetchScalarGridSpec(
            num_scalar_prefetch=1,
            grid=(),
            in_specs=[pl.BlockSpec(memory_space=pltpu.VMEM)],
            out_specs=pl.BlockSpec(memory_space=pl.ANY),
            scratch_shapes=[pltpu.VMEM(shape, jnp.bfloat16), pltpu.SemaphoreType.DMA((4,))],
        ),
        compiler_params=pltpu.CompilerParams(vmem_limit_bytes=16 * 1024 * 1024),
        name="pick",
    )(bands, in_vmem(rows))


def even_wave(low):
    return jnp.where(low % 2 == 0, low, M - 1 - low)


def table_kernel(waves_ref, out_ref):
    even = even_wave(waves_ref[...])
    odd = M - 1 - even
    lane = lax.broadcasted_iota(jnp.int32, even.shape, 1).astype(jnp.float32)
    unit = 2.0 * math.pi / NLON

    def angle(product):
        turns = jnp.floor(product * (1.0 / NLON))
        return (product - turns * NLON) * unit

    for w, wave in enumerate((even, odd)):
        number = wave.astype(jnp.float32)
        factor = jnp.where(wave == 0, 1.0, 2.0)
        start = angle(number * lane)
        step = angle(number * LANES)
        c, s = factor * jnp.cos(start), -factor * jnp.sin(start)
        dc, ds = jnp.cos(step), jnp.sin(step)
        for b in range(0, QUARTER, LANES):
            at = slice(b % CHUNK, b % CHUNK + LANES)
            out_ref[b // CHUNK, w, 0, :, at] = c.astype(jnp.bfloat16)
            out_ref[b // CHUNK, w, 1, :, at] = s.astype(jnp.bfloat16)
            c, s = c * dc + s * ds, s * dc - c * ds


def wave_tables(waves):
    total = waves.shape[0]
    rows = 64
    chunks = pl.cdiv(QUARTER, CHUNK)
    return pl.pallas_call(
        table_kernel,
        out_shape=jax.ShapeDtypeStruct((chunks, 2, 2, total, CHUNK), jnp.bfloat16),
        grid=(total // rows,),
        in_specs=[pl.BlockSpec((rows, LANES), lambda i: (i, 0))],
        out_specs=pl.BlockSpec((chunks, 2, 2, rows, CHUNK), lambda i: (0, 0, 0, i, 0)),
        compiler_params=pltpu.CompilerParams(vmem_limit_bytes=16 * 1024 * 1024),
        cost_estimate=pl.CostEstimate(
            flops=16 * total * QUARTER, bytes_accessed=8 * total * QUARTER, transcendentals=8 * total * LANES
        ),
        name="tables",
    )(jnp.broadcast_to(waves[:, None], (total, LANES)))


def fourier_kernel(
    arrived_ref, table_ref, sign_hbm, out_hbm, left_ref, sign_ref, row_ref, sign_sem, out_sems
):
    devices, slots, _, _, pairs, width = arrived_ref.shape
    fields = width // 2
    total = devices * pairs
    chunks = table_ref.shape[0]
    rows = 2 * fields

    sign_copy = pltpu.make_async_copy(sign_hbm, sign_ref, sign_sem)
    sign_copy.start()

    stores = []
    for s in range(slots):
        turned = []
        for h in range(2):
            for w in range(2):
                x = jnp.concatenate([arrived_ref[d, s, h, w] for d in range(devices)], axis=0)
                xt = x.T
                at = slice(h * fields, (h + 1) * fields)
                left_ref[s, w, at, :total] = xt[:fields]
                left_ref[s, w, at, total:] = xt[fields:]
                turned.append((h, w, xt))
        if s == 0:
            sign_copy.wait()
        sign = sign_ref[0:1, :]
        for h, w, xt in turned:
            at = slice(rows + h * fields, rows + (h + 1) * fields)
            signed = (xt.astype(jnp.float32) * sign).astype(jnp.bfloat16)
            re, im = signed[:fields], signed[fields:]
            left_ref[s, w, at, :total] = im if w else re
            left_ref[s, w, at, total:] = -re if w else im
        base = slice(s * rows, (s + 1) * rows)
        for i in range(chunks):
            lo, hi = i * CHUNK, min((i + 1) * CHUNK, QUARTER)
            e, o = [
                jnp.dot(
                    left_ref[s, w],
                    table_ref[i, w].reshape(2 * total, CHUNK),
                    preferred_element_type=jnp.float32,
                )[:, : hi - lo]
                for w in range(2)
            ]
            plus, minus = e + o, e - o
            for k, part in enumerate((plus[:rows], plus[rows:], minus[:rows], minus[rows:])):
                row_ref[base, k * QUARTER + lo : k * QUARTER + hi] = part.astype(jnp.bfloat16)
        copy = pltpu.make_async_copy(row_ref.at[base], out_hbm.at[base], out_sems.at[s])
        copy.start()
        stores.append(copy)
    for copy in stores:
        copy.wait()


def fourier_stage(arrived, sign, table):
    devices, slots, _, _, pairs, width = arrived.shape
    fields = width // 2
    total = devices * pairs
    rows = slots * 2 * fields
    out = pl.pallas_call(
        fourier_kernel,
        out_shape=jax.ShapeDtypeStruct((rows, NLON), jnp.bfloat16),
        in_specs=[pl.BlockSpec(memory_space=pltpu.VMEM)] * 2 + [pl.BlockSpec(memory_space=pl.ANY)],
        out_specs=pl.BlockSpec(memory_space=pl.ANY),
        scratch_shapes=[
            pltpu.VMEM((slots, 2, 4 * fields, 2 * total), jnp.bfloat16),
            pltpu.VMEM(sign.shape, jnp.float32),
            pltpu.VMEM((rows, NLON), jnp.bfloat16),
            pltpu.SemaphoreType.DMA,
            pltpu.SemaphoreType.DMA((slots,)),
        ],
        compiler_params=pltpu.CompilerParams(vmem_limit_bytes=16 * 1024 * 1024),
        cost_estimate=pl.CostEstimate(
            flops=16 * rows * total * QUARTER, bytes_accessed=8 * total * QUARTER, transcendentals=0
        ),
        name="fourier",
    )(arrived, table, in_hbm(sign))
    return out.reshape(slots, 2, fields, NLON)


def on_device(wave_pairs, band_owner, spectra_even, spectra_odd, legendre_even, legendre_odd):
    devices = lax.axis_size("wave")
    pairs = round_up(wave_pairs.shape[0], ROWS)
    extra = pairs - wave_pairs.shape[0]
    slots = band_owner.shape[0]
    width = spectra_even.shape[2]
    if extra:
        wave_pairs = jnp.pad(wave_pairs, (0, extra))
        spectra_even, spectra_odd, legendre_even, legendre_odd = (
            jnp.pad(a, ((0, extra), (0, 0), (0, 0)))
            for a in (spectra_even, spectra_odd, legendre_even, legendre_odd)
        )

    rest = round_up(pairs + slots, LANES) - pairs - slots
    own = jnp.concatenate([wave_pairs, band_owner, jnp.zeros(rest, jnp.int32)])
    own = jnp.broadcast_to(own, (devices, 1) + own.shape)
    index = lax.all_to_all(own, "wave", 0, 0, tiled=True)[:, 0]
    all_bands = index[:, pairs : pairs + slots].reshape(-1)
    rows = legendre_stage(wave_pairs, spectra_even, spectra_odd, legendre_even, legendre_odd)
    picked = pick_latitudes(all_bands, rows, pairs)
    index, picked = lax.optimization_barrier((index, picked))
    arrived = lax.all_to_all(picked.reshape(devices, slots, 2, 2, pairs, width), "wave", 0, 0, tiled=True)
    all_pairs = index[:, :pairs].reshape(-1)
    sign = jnp.where(even_wave(all_pairs) % 4 == 0, 1.0, -1.0).astype(jnp.float32)
    sign, all_pairs = lax.optimization_barrier((jnp.broadcast_to(sign, (ROWS,) + sign.shape), all_pairs))
    return fourier_stage(arrived, sign, wave_tables(all_pairs))


def solution(mesh):
    return jax.shard_map(
        on_device,
        mesh=mesh,
        in_specs=(
            P("wave"),
            P("wave"),
            P("wave", None, "grp"),
            P("wave", None, "grp"),
            P("wave", None, None),
            P("wave", None, None),
        ),
        out_specs=P("wave", None, "grp", None),
        check_vma=False,
    )
```

```python
import functools
import math

import jax
import jax.numpy as jnp
from jax import lax
from jax.experimental import pallas as pl
from jax.experimental.pallas import tpu as pltpu
from jax.sharding import PartitionSpec as P

M = 1280
NLON = 2688
QUARTER = NLON // 4
CHUNK = 256
ROWS = 8
LANES = 128


def round_up(value, unit):
    return -(-value // unit) * unit


def legendre_kernel(
    waves_hbm, se_hbm, so_hbm, le_hbm, lo_hbm, out_ref,
    waves_ref, se_ref, so_ref, le_ref, lo_ref, columns_ref, anti_ref, sems, wave_sem,
):
    pairs, lats, he = le_ref.shape
    ho = lo_ref.shape[2]
    groups = pairs // ROWS

    def odd_copies(g):
        at = pl.ds(pl.multiple_of(g * ROWS, ROWS), ROWS)
        return (
            pltpu.make_async_copy(lo_hbm.at[at], lo_ref.at[at], sems.at[0, g]),
            pltpu.make_async_copy(so_hbm.at[at], so_ref.at[at], sems.at[1, g]),
        )

    def even_copies(g):
        at = pl.ds(pl.multiple_of(g * ROWS, ROWS), ROWS)
        return (
            pltpu.make_async_copy(le_hbm.at[at], le_ref.at[at], sems.at[2, g]),
            pltpu.make_async_copy(se_hbm.at[:, at], se_ref.at[g], sems.at[3, g]),
        )

    wave_copy = pltpu.make_async_copy(waves_hbm, waves_ref, wave_sem)
    wave_copy.start()
    ahead = 2
    for g in range(min(ahead, groups)):
        for copy in odd_copies(g) + even_copies(g):
            copy.start()
    wave_copy.wait()

    ids_e = lax.broadcasted_iota(jnp.int32, (1, he), 1)
    ids_o = lax.broadcasted_iota(jnp.int32, (1, ho), 1)

    def split(panel, ids, count):
        in_low = jnp.where(ids < count, 1.0, 0.0).astype(jnp.bfloat16)
        lower = panel * in_low
        return jnp.concatenate([lower, panel - lower], axis=0)

    @pl.loop(0, groups)
    def _(g):
        base = pl.multiple_of(g * ROWS, ROWS)
        for copy in odd_copies(g):
            copy.wait()

        @pl.when(g + ahead < groups)
        def _():
            for copy in odd_copies(g + ahead) + even_copies(g + ahead):
                copy.start()

        for p in range(ROWS):
            odd = split(lo_ref[base + p], ids_o, (M - waves_ref[base + p]) // 2)
            anti_ref[p] = jnp.dot(odd, so_ref[base + p], preferred_element_type=jnp.float32)
        for copy in even_copies(g):
            copy.wait()
        columns_ref[...] = se_ref[g].astype(jnp.float32).reshape(columns_ref.shape)
        for p in range(ROWS):
            low = waves_ref[base + p]
            parity = low % 2
            even = split(le_ref[base + p], ids_e, (M - low + 1) // 2)
            xe = columns_ref[pl.ds(p, he, stride=ROWS), :].astype(jnp.bfloat16)
            sym = jnp.dot(even, xe, preferred_element_type=jnp.float32)
            anti = anti_ref[p]
            for h, rows in enumerate((sym + anti, sym - anti)):
                for w in range(2):
                    start = (parity ^ w) * (lats * pairs) + base + p
                    out_ref[h, pl.ds(start, lats, stride=pairs), :] = rows[w * lats : (w + 1) * lats]


def in_hbm(x):
    return pltpu.with_memory_space_constraint(x, pltpu.HBM)


def in_vmem(x):
    return pltpu.with_memory_space_constraint(x, pltpu.VMEM)


def legendre_stage(waves, spectra_even, spectra_odd, legendre_even, legendre_odd):
    pairs, he, width = spectra_even.shape
    ho = spectra_odd.shape[1]
    lats = legendre_even.shape[1]
    by_column = jnp.transpose(spectra_even, (1, 0, 2))
    operands = (waves, by_column, spectra_odd, legendre_even, legendre_odd)
    return pl.pallas_call(
        legendre_kernel,
        out_shape=pltpu.VMEM((2, 2 * lats * pairs, width), jnp.float32),
        in_specs=[pl.BlockSpec(memory_space=pl.ANY)] * 5,
        out_specs=pl.BlockSpec(memory_space=pltpu.VMEM),
        scratch_shapes=[
            pltpu.SMEM((pairs,), jnp.int32),
            pltpu.VMEM((pairs // ROWS, he, ROWS, width), jnp.bfloat16),
            pltpu.VMEM((pairs, ho, width), jnp.bfloat16),
            pltpu.VMEM((pairs, lats, he), jnp.bfloat16),
            pltpu.VMEM((pairs, lats, ho), jnp.bfloat16),
            pltpu.VMEM((he * ROWS, width), jnp.float32),
            pltpu.VMEM((ROWS, 2 * lats, width), jnp.float32),
            pltpu.SemaphoreType.DMA((4, pairs // ROWS)),
            pltpu.SemaphoreType.DMA,
        ],
        compiler_params=pltpu.CompilerParams(vmem_limit_bytes=40 * 1024 * 1024),
        cost_estimate=pl.CostEstimate(
            flops=4 * pairs * lats * 2 * (he + ho) * width,
            bytes_accessed=2 * pairs * (he + ho) * (width + lats),
            transcendentals=0,
        ),
        name="legendre",
    )(*(in_hbm(x) for x in operands))


def pick_kernel(bands_ref, rows_ref, out_hbm, out_ref, sems):
    lats, _, _, pairs, _ = out_ref.shape
    piece = lats // sems.shape[0]

    def store(i):
        at = pl.ds(i * piece, piece)
        return pltpu.make_async_copy(out_ref.at[at], out_hbm.at[at], sems.at[i])

    def emit(slot, carry):
        band = bands_ref[slot]
        for h in range(2):
            for w in range(2):
                start = pl.multiple_of((w * lats + band) * pairs, ROWS)
                out_ref[slot, h, w] = rows_ref[h, pl.ds(start, pairs), :].astype(jnp.bfloat16)
        return carry

    for i in range(sems.shape[0]):
        lax.fori_loop(i * piece, (i + 1) * piece, emit, 0, unroll=4)
        store(i).start()
    for i in range(sems.shape[0]):
        store(i).wait()


def pick_latitudes(bands, rows, pairs):
    lats = bands.shape[0]
    width = rows.shape[2]
    shape = (lats, 2, 2, pairs, width)
    return pl.pallas_call(
        pick_kernel,
        out_shape=pltpu.HBM(shape, jnp.bfloat16),
        grid_spec=pltpu.PrefetchScalarGridSpec(
            num_scalar_prefetch=1,
            grid=(),
            in_specs=[pl.BlockSpec(memory_space=pltpu.VMEM)],
            out_specs=pl.BlockSpec(memory_space=pl.ANY),
            scratch_shapes=[pltpu.VMEM(shape, jnp.bfloat16), pltpu.SemaphoreType.DMA((4,))],
        ),
        compiler_params=pltpu.CompilerParams(vmem_limit_bytes=16 * 1024 * 1024),
        name="pick",
    )(bands, in_vmem(rows))


def even_wave(low):
    return jnp.where(low % 2 == 0, low, M - 1 - low)


def table_kernel(waves_ref, first_ref, rest_ref):
    even = even_wave(waves_ref[...])
    odd = M - 1 - even
    lane = lax.broadcasted_iota(jnp.int32, even.shape, 1).astype(jnp.float32)
    unit = 2.0 * math.pi / NLON

    def angle(product):
        turns = jnp.floor(product * (1.0 / NLON))
        return (product - turns * NLON) * unit

    for w, wave in enumerate((even, odd)):
        number = wave.astype(jnp.float32)
        factor = jnp.where(wave == 0, 1.0, 2.0)
        start = angle(number * lane)
        step = angle(number * LANES)
        c, s = factor * jnp.cos(start), -factor * jnp.sin(start)
        dc, ds = jnp.cos(step), jnp.sin(step)
        for b in range(0, QUARTER, LANES):
            at = slice(b % CHUNK, b % CHUNK + LANES)
            out_ref = rest_ref.at[b // CHUNK - 1] if b >= CHUNK else first_ref
            out_ref[w, 0, :, at] = c.astype(jnp.bfloat16)
            out_ref[w, 1, :, at] = s.astype(jnp.bfloat16)
            c, s = c * dc + s * ds, s * dc - c * ds


def wave_tables(waves):
    total = waves.shape[0]
    rows = 64
    rest = pl.cdiv(QUARTER, CHUNK) - 1
    return pl.pallas_call(
        table_kernel,
        out_shape=[
            jax.ShapeDtypeStruct((2, 2, total, CHUNK), jnp.bfloat16),
            pltpu.HBM((rest, 2, 2, total, CHUNK), jnp.bfloat16),
        ],
        grid=(total // rows,),
        in_specs=[pl.BlockSpec((rows, LANES), lambda i: (i, 0))],
        out_specs=[
            pl.BlockSpec((2, 2, rows, CHUNK), lambda i: (0, 0, i, 0)),
            pl.BlockSpec((rest, 2, 2, rows, CHUNK), lambda i: (0, 0, 0, i, 0)),
        ],
        compiler_params=pltpu.CompilerParams(vmem_limit_bytes=16 * 1024 * 1024),
        cost_estimate=pl.CostEstimate(
            flops=16 * total * QUARTER, bytes_accessed=8 * total * QUARTER, transcendentals=8 * total * LANES
        ),
        name="tables",
    )(jnp.broadcast_to(waves[:, None], (total, LANES)))


def fourier_kernel(
    arrived_ref, first_ref, rest_hbm, sign_hbm, out_hbm,
    left_ref, rest_ref, sign_ref, row_ref, sems, sign_sem, out_sems,
):
    devices, slots, _, _, pairs, width = arrived_ref.shape
    fields = width // 2
    total = devices * pairs
    chunks = 1 + rest_ref.shape[0]
    rows = 2 * fields

    def load(i):
        return pltpu.make_async_copy(rest_hbm.at[i - 1], rest_ref.at[i - 1], sems.at[i - 1])

    sign_copy = pltpu.make_async_copy(sign_hbm, sign_ref, sign_sem)
    sign_copy.start()
    for i in range(1, chunks):
        load(i).start()

    stores = []
    for s in range(slots):
        turned = []
        for h in range(2):
            for w in range(2):
                x = jnp.concatenate([arrived_ref[d, s, h, w] for d in range(devices)], axis=0)
                xt = x.T
                at = slice(h * fields, (h + 1) * fields)
                left_ref[s, w, at, :total] = xt[:fields]
                left_ref[s, w, at, total:] = xt[fields:]
                turned.append((h, w, xt))
        if s == 0:
            sign_copy.wait()
        sign = sign_ref[0:1, :]
        for h, w, xt in turned:
            at = slice(rows + h * fields, rows + (h + 1) * fields)
            signed = (xt.astype(jnp.float32) * sign).astype(jnp.bfloat16)
            re, im = signed[:fields], signed[fields:]
            left_ref[s, w, at, :total] = im if w else re
            left_ref[s, w, at, total:] = -re if w else im
        base = slice(s * rows, (s + 1) * rows)
        for i in range(chunks):
            if s == 0 and i > 0:
                load(i).wait()
            table_ref = rest_ref.at[i - 1] if i else first_ref
            lo, hi = i * CHUNK, min((i + 1) * CHUNK, QUARTER)
            e, o = [
                jnp.dot(
                    left_ref[s, w],
                    table_ref[w].reshape(2 * total, CHUNK),
                    preferred_element_type=jnp.float32,
                )[:, : hi - lo]
                for w in range(2)
            ]
            plus, minus = e + o, e - o
            for k, part in enumerate((plus[:rows], plus[rows:], minus[:rows], minus[rows:])):
                row_ref[base, k * QUARTER + lo : k * QUARTER + hi] = part.astype(jnp.bfloat16)
        copy = pltpu.make_async_copy(row_ref.at[base], out_hbm.at[base], out_sems.at[s])
        copy.start()
        stores.append(copy)
    for copy in stores:
        copy.wait()


def fourier_stage(arrived, sign, first, rest):
    devices, slots, _, _, pairs, width = arrived.shape
    fields = width // 2
    total = devices * pairs
    rows = slots * 2 * fields
    out = pl.pallas_call(
        fourier_kernel,
        out_shape=jax.ShapeDtypeStruct((rows, NLON), jnp.bfloat16),
        in_specs=[pl.BlockSpec(memory_space=pltpu.VMEM)] * 2 + [pl.BlockSpec(memory_space=pl.ANY)] * 2,
        out_specs=pl.BlockSpec(memory_space=pl.ANY),
        scratch_shapes=[
            pltpu.VMEM((slots, 2, 4 * fields, 2 * total), jnp.bfloat16),
            pltpu.VMEM(rest.shape, jnp.bfloat16),
            pltpu.VMEM(sign.shape, jnp.float32),
            pltpu.VMEM((rows, NLON), jnp.bfloat16),
            pltpu.SemaphoreType.DMA((rest.shape[0],)),
            pltpu.SemaphoreType.DMA,
            pltpu.SemaphoreType.DMA((slots,)),
        ],
        compiler_params=pltpu.CompilerParams(vmem_limit_bytes=16 * 1024 * 1024),
        cost_estimate=pl.CostEstimate(
            flops=16 * rows * total * QUARTER, bytes_accessed=8 * total * QUARTER, transcendentals=0
        ),
        name="fourier",
    )(arrived, first, in_hbm(rest), in_hbm(sign))
    return out.reshape(slots, 2, fields, NLON)


def on_device(wave_pairs, band_owner, spectra_even, spectra_odd, legendre_even, legendre_odd):
    devices = lax.axis_size("wave")
    pairs = round_up(wave_pairs.shape[0], ROWS)
    extra = pairs - wave_pairs.shape[0]
    slots = band_owner.shape[0]
    width = spectra_even.shape[2]
    if extra:
        wave_pairs = jnp.pad(wave_pairs, (0, extra))
        spectra_even, spectra_odd, legendre_even, legendre_odd = (
            jnp.pad(a, ((0, extra), (0, 0), (0, 0)))
            for a in (spectra_even, spectra_odd, legendre_even, legendre_odd)
        )

    rest = round_up(pairs + slots, LANES) - pairs - slots
    own = jnp.concatenate([wave_pairs, band_owner, jnp.zeros(rest, jnp.int32)])
    own = jnp.broadcast_to(own, (devices, 1) + own.shape)
    index = lax.all_to_all(own, "wave", 0, 0, tiled=True)[:, 0]
    all_bands = index[:, pairs : pairs + slots].reshape(-1)
    rows = legendre_stage(wave_pairs, spectra_even, spectra_odd, legendre_even, legendre_odd)
    picked = pick_latitudes(all_bands, rows, pairs)
    index, picked = lax.optimization_barrier((index, picked))
    arrived = lax.all_to_all(picked.reshape(devices, slots, 2, 2, pairs, width), "wave", 0, 0, tiled=True)
    all_pairs = index[:, :pairs].reshape(-1)
    sign = jnp.where(even_wave(all_pairs) % 4 == 0, 1.0, -1.0).astype(jnp.float32)
    sign, all_pairs = lax.optimization_barrier((jnp.broadcast_to(sign, (ROWS,) + sign.shape), all_pairs))
    return fourier_stage(arrived, sign, *wave_tables(all_pairs))


def solution(mesh):
    return jax.shard_map(
        on_device,
        mesh=mesh,
        in_specs=(
            P("wave"),
            P("wave"),
            P("wave", None, "grp"),
            P("wave", None, "grp"),
            P("wave", None, None),
            P("wave", None, None),
        ),
        out_specs=P("wave", None, "grp", None),
        check_vma=False,
    )
```

```python
import functools
import math

import jax
import jax.numpy as jnp
from jax import lax
from jax.experimental import pallas as pl
from jax.experimental.pallas import tpu as pltpu
from jax.sharding import PartitionSpec as P

M = 1280
NLON = 2688
QUARTER = NLON // 4
CHUNK = 256
ROWS = 8
LANES = 128


def round_up(value, unit):
    return -(-value // unit) * unit


def legendre_kernel(
    waves_hbm, se_hbm, so_hbm, le_hbm, lo_hbm, out_ref,
    waves_ref, se_ref, so_ref, le_ref, lo_ref, columns_ref, sym_ref, sems, wave_sem,
):
    pairs, lats, he = le_ref.shape
    ho = lo_ref.shape[2]
    groups = pairs // ROWS

    def odd_copies(g):
        at = pl.ds(pl.multiple_of(g * ROWS, ROWS), ROWS)
        return (
            pltpu.make_async_copy(lo_hbm.at[at], lo_ref.at[at], sems.at[0, g]),
            pltpu.make_async_copy(so_hbm.at[at], so_ref.at[at], sems.at[1, g]),
        )

    def even_copies(g):
        at = pl.ds(pl.multiple_of(g * ROWS, ROWS), ROWS)
        return (
            pltpu.make_async_copy(le_hbm.at[at], le_ref.at[at], sems.at[2, g]),
            pltpu.make_async_copy(se_hbm.at[:, at], se_ref.at[g], sems.at[3, g]),
        )

    wave_copy = pltpu.make_async_copy(waves_hbm, waves_ref, wave_sem)
    wave_copy.start()
    ahead = 2
    for g in range(min(ahead, groups)):
        for copy in even_copies(g) + odd_copies(g):
            copy.start()
    wave_copy.wait()

    ids_e = lax.broadcasted_iota(jnp.int32, (1, he), 1)
    ids_o = lax.broadcasted_iota(jnp.int32, (1, ho), 1)

    def split(panel, ids, count):
        in_low = jnp.where(ids < count, 1.0, 0.0).astype(jnp.bfloat16)
        lower = panel * in_low
        return jnp.concatenate([lower, panel - lower], axis=0)

    @pl.loop(0, groups)
    def _(g):
        base = pl.multiple_of(g * ROWS, ROWS)
        for copy in even_copies(g):
            copy.wait()

        @pl.when(g + ahead < groups)
        def _():
            for copy in even_copies(g + ahead) + odd_copies(g + ahead):
                copy.start()

        columns_ref[...] = se_ref[g].astype(jnp.float32).reshape(columns_ref.shape)
        for p in range(ROWS):
            even = split(le_ref[base + p], ids_e, (M - waves_ref[base + p] + 1) // 2)
            xe = columns_ref[pl.ds(p, he, stride=ROWS), :].astype(jnp.bfloat16)
            sym_ref[p] = jnp.dot(even, xe, preferred_element_type=jnp.float32)
        for copy in odd_copies(g):
            copy.wait()
        for p in range(ROWS):
            low = waves_ref[base + p]
            parity = low % 2
            odd = split(lo_ref[base + p], ids_o, (M - low) // 2)
            anti = jnp.dot(odd, so_ref[base + p], preferred_element_type=jnp.float32)
            sym = sym_ref[p]
            for h, rows in enumerate((sym + anti, sym - anti)):
                for w in range(2):
                    start = (parity ^ w) * (lats * pairs) + base + p
                    out_ref[h, pl.ds(start, lats, stride=pairs), :] = rows[w * lats : (w + 1) * lats]


def in_hbm(x):
    return pltpu.with_memory_space_constraint(x, pltpu.HBM)


def in_vmem(x):
    return pltpu.with_memory_space_constraint(x, pltpu.VMEM)


def legendre_stage(waves, spectra_even, spectra_odd, legendre_even, legendre_odd):
    pairs, he, width = spectra_even.shape
    ho = spectra_odd.shape[1]
    lats = legendre_even.shape[1]
    by_column = jnp.transpose(spectra_even, (1, 0, 2))
    operands = (waves, by_column, spectra_odd, legendre_even, legendre_odd)
    return pl.pallas_call(
        legendre_kernel,
        out_shape=pltpu.VMEM((2, 2 * lats * pairs, width), jnp.float32),
        in_specs=[pl.BlockSpec(memory_space=pl.ANY)] * 5,
        out_specs=pl.BlockSpec(memory_space=pltpu.VMEM),
        scratch_shapes=[
            pltpu.SMEM((pairs,), jnp.int32),
            pltpu.VMEM((pairs // ROWS, he, ROWS, width), jnp.bfloat16),
            pltpu.VMEM((pairs, ho, width), jnp.bfloat16),
            pltpu.VMEM((pairs, lats, he), jnp.bfloat16),
            pltpu.VMEM((pairs, lats, ho), jnp.bfloat16),
            pltpu.VMEM((he * ROWS, width), jnp.float32),
            pltpu.VMEM((ROWS, 2 * lats, width), jnp.float32),
            pltpu.SemaphoreType.DMA((4, pairs // ROWS)),
            pltpu.SemaphoreType.DMA,
        ],
        compiler_params=pltpu.CompilerParams(vmem_limit_bytes=40 * 1024 * 1024),
        cost_estimate=pl.CostEstimate(
            flops=4 * pairs * lats * 2 * (he + ho) * width,
            bytes_accessed=2 * pairs * (he + ho) * (width + lats),
            transcendentals=0,
        ),
        name="legendre",
    )(*(in_hbm(x) for x in operands))


def pick_kernel(bands_ref, rows_ref, out_hbm, out_ref, sems):
    lats, _, _, pairs, _ = out_ref.shape
    piece = lats // sems.shape[0]

    def store(i):
        at = pl.ds(i * piece, piece)
        return pltpu.make_async_copy(out_ref.at[at], out_hbm.at[at], sems.at[i])

    def emit(slot, carry):
        band = bands_ref[slot]
        for h in range(2):
            for w in range(2):
                start = pl.multiple_of((w * lats + band) * pairs, ROWS)
                out_ref[slot, h, w] = rows_ref[h, pl.ds(start, pairs), :].astype(jnp.bfloat16)
        return carry

    for i in range(sems.shape[0]):
        lax.fori_loop(i * piece, (i + 1) * piece, emit, 0, unroll=4)
        store(i).start()
    for i in range(sems.shape[0]):
        store(i).wait()


def pick_latitudes(bands, rows, pairs):
    lats = bands.shape[0]
    width = rows.shape[2]
    shape = (lats, 2, 2, pairs, width)
    return pl.pallas_call(
        pick_kernel,
        out_shape=pltpu.HBM(shape, jnp.bfloat16),
        grid_spec=pltpu.PrefetchScalarGridSpec(
            num_scalar_prefetch=1,
            grid=(),
            in_specs=[pl.BlockSpec(memory_space=pltpu.VMEM)],
            out_specs=pl.BlockSpec(memory_space=pl.ANY),
            scratch_shapes=[pltpu.VMEM(shape, jnp.bfloat16), pltpu.SemaphoreType.DMA((4,))],
        ),
        compiler_params=pltpu.CompilerParams(vmem_limit_bytes=16 * 1024 * 1024),
        name="pick",
    )(bands, in_vmem(rows))


def even_wave(low):
    return jnp.where(low % 2 == 0, low, M - 1 - low)


def table_kernel(waves_ref, first_ref, rest_ref):
    even = even_wave(waves_ref[...])
    odd = M - 1 - even
    lane = lax.broadcasted_iota(jnp.int32, even.shape, 1).astype(jnp.float32)
    unit = 2.0 * math.pi / NLON

    def angle(product):
        turns = jnp.floor(product * (1.0 / NLON))
        return (product - turns * NLON) * unit

    for w, wave in enumerate((even, odd)):
        number = wave.astype(jnp.float32)
        factor = jnp.where(wave == 0, 1.0, 2.0)
        start = angle(number * lane)
        step = angle(number * LANES)
        c, s = factor * jnp.cos(start), -factor * jnp.sin(start)
        dc, ds = jnp.cos(step), jnp.sin(step)
        for b in range(0, QUARTER, LANES):
            at = slice(b % CHUNK, b % CHUNK + LANES)
            out_ref = rest_ref.at[b // CHUNK - 1] if b >= CHUNK else first_ref
            out_ref[w, 0, :, at] = c.astype(jnp.bfloat16)
            out_ref[w, 1, :, at] = s.astype(jnp.bfloat16)
            c, s = c * dc + s * ds, s * dc - c * ds


def wave_tables(waves):
    total = waves.shape[0]
    rows = 64
    rest = pl.cdiv(QUARTER, CHUNK) - 1
    return pl.pallas_call(
        table_kernel,
        out_shape=[
            jax.ShapeDtypeStruct((2, 2, total, CHUNK), jnp.bfloat16),
            pltpu.HBM((rest, 2, 2, total, CHUNK), jnp.bfloat16),
        ],
        grid=(total // rows,),
        in_specs=[pl.BlockSpec((rows, LANES), lambda i: (i, 0))],
        out_specs=[
            pl.BlockSpec((2, 2, rows, CHUNK), lambda i: (0, 0, i, 0)),
            pl.BlockSpec((rest, 2, 2, rows, CHUNK), lambda i: (0, 0, 0, i, 0)),
        ],
        compiler_params=pltpu.CompilerParams(vmem_limit_bytes=16 * 1024 * 1024),
        cost_estimate=pl.CostEstimate(
            flops=16 * total * QUARTER, bytes_accessed=8 * total * QUARTER, transcendentals=8 * total * LANES
        ),
        name="tables",
    )(jnp.broadcast_to(waves[:, None], (total, LANES)))


def fourier_kernel(
    arrived_ref, first_ref, rest_hbm, sign_hbm, out_hbm,
    left_ref, rest_ref, sign_ref, row_ref, sems, sign_sem, out_sems,
):
    devices, slots, _, _, pairs, width = arrived_ref.shape
    fields = width // 2
    total = devices * pairs
    chunks = 1 + rest_ref.shape[0]
    rows = 2 * fields

    def load(i):
        return pltpu.make_async_copy(rest_hbm.at[i - 1], rest_ref.at[i - 1], sems.at[i - 1])

    def block(s, i):
        table_ref = rest_ref.at[i - 1] if i else first_ref
        lo, hi = i * CHUNK, min((i + 1) * CHUNK, QUARTER)
        e, o = [
            jnp.dot(
                left_ref[s, w],
                table_ref[w].reshape(2 * total, CHUNK),
                preferred_element_type=jnp.float32,
            )[:, : hi - lo]
            for w in range(2)
        ]
        plus, minus = e + o, e - o
        for k, part in enumerate((plus[:rows], plus[rows:], minus[:rows], minus[rows:])):
            at = slice(k * QUARTER + lo, k * QUARTER + hi)
            row_ref[s * rows : (s + 1) * rows, at] = part.astype(jnp.bfloat16)

    sign_copy = pltpu.make_async_copy(sign_hbm, sign_ref, sign_sem)
    sign_copy.start()
    for i in range(1, chunks):
        load(i).start()

    stores = []
    for s in range(slots):
        turned = []
        for h in range(2):
            for w in range(2):
                x = jnp.concatenate([arrived_ref[d, s, h, w] for d in range(devices)], axis=0)
                xt = x.T
                at = slice(h * fields, (h + 1) * fields)
                left_ref[s, w, at, :total] = xt[:fields]
                left_ref[s, w, at, total:] = xt[fields:]
                turned.append((h, w, xt))
        if s == 0:
            sign_copy.wait()
        sign = sign_ref[0:1, :]
        for h, w, xt in turned:
            at = slice(rows + h * fields, rows + (h + 1) * fields)
            signed = (xt.astype(jnp.float32) * sign).astype(jnp.bfloat16)
            re, im = signed[:fields], signed[fields:]
            left_ref[s, w, at, :total] = im if w else re
            left_ref[s, w, at, total:] = -re if w else im
        block(s, 0)
    for i in range(1, chunks):
        load(i).wait()
    for s in range(slots):
        for i in range(1, chunks):
            block(s, i)
        base = slice(s * rows, (s + 1) * rows)
        copy = pltpu.make_async_copy(row_ref.at[base], out_hbm.at[base], out_sems.at[s])
        copy.start()
        stores.append(copy)
    for copy in stores:
        copy.wait()


def fourier_stage(arrived, sign, first, rest):
    devices, slots, _, _, pairs, width = arrived.shape
    fields = width // 2
    total = devices * pairs
    rows = slots * 2 * fields
    out = pl.pallas_call(
        fourier_kernel,
        out_shape=jax.ShapeDtypeStruct((rows, NLON), jnp.bfloat16),
        in_specs=[pl.BlockSpec(memory_space=pltpu.VMEM)] * 2 + [pl.BlockSpec(memory_space=pl.ANY)] * 2,
        out_specs=pl.BlockSpec(memory_space=pl.ANY),
        scratch_shapes=[
            pltpu.VMEM((slots, 2, 4 * fields, 2 * total), jnp.bfloat16),
            pltpu.VMEM(rest.shape, jnp.bfloat16),
            pltpu.VMEM(sign.shape, jnp.float32),
            pltpu.VMEM((rows, NLON), jnp.bfloat16),
            pltpu.SemaphoreType.DMA((rest.shape[0],)),
            pltpu.SemaphoreType.DMA,
            pltpu.SemaphoreType.DMA((slots,)),
        ],
        compiler_params=pltpu.CompilerParams(vmem_limit_bytes=16 * 1024 * 1024),
        cost_estimate=pl.CostEstimate(
            flops=16 * rows * total * QUARTER, bytes_accessed=8 * total * QUARTER, transcendentals=0
        ),
        name="fourier",
    )(arrived, first, in_hbm(rest), in_hbm(sign))
    return out.reshape(slots, 2, fields, NLON)


def on_device(wave_pairs, band_owner, spectra_even, spectra_odd, legendre_even, legendre_odd):
    devices = lax.axis_size("wave")
    pairs = round_up(wave_pairs.shape[0], ROWS)
    extra = pairs - wave_pairs.shape[0]
    slots = band_owner.shape[0]
    width = spectra_even.shape[2]
    if extra:
        wave_pairs = jnp.pad(wave_pairs, (0, extra))
        spectra_even, spectra_odd, legendre_even, legendre_odd = (
            jnp.pad(a, ((0, extra), (0, 0), (0, 0)))
            for a in (spectra_even, spectra_odd, legendre_even, legendre_odd)
        )

    rest = round_up(pairs + slots, LANES) - pairs - slots
    own = jnp.concatenate([wave_pairs, band_owner, jnp.zeros(rest, jnp.int32)])
    own = jnp.broadcast_to(own, (devices, 1) + own.shape)
    index = lax.all_to_all(own, "wave", 0, 0, tiled=True)[:, 0]
    all_bands = index[:, pairs : pairs + slots].reshape(-1)
    rows = legendre_stage(wave_pairs, spectra_even, spectra_odd, legendre_even, legendre_odd)
    picked = pick_latitudes(all_bands, rows, pairs)
    index, picked = lax.optimization_barrier((index, picked))
    arrived = lax.all_to_all(picked.reshape(devices, slots, 2, 2, pairs, width), "wave", 0, 0, tiled=True)
    all_pairs = index[:, :pairs].reshape(-1)
    sign = jnp.where(even_wave(all_pairs) % 4 == 0, 1.0, -1.0).astype(jnp.float32)
    sign, all_pairs = lax.optimization_barrier((jnp.broadcast_to(sign, (ROWS,) + sign.shape), all_pairs))
    return fourier_stage(arrived, sign, *wave_tables(all_pairs))


def solution(mesh):
    return jax.shard_map(
        on_device,
        mesh=mesh,
        in_specs=(
            P("wave"),
            P("wave"),
            P("wave", None, "grp"),
            P("wave", None, "grp"),
            P("wave", None, None),
            P("wave", None, None),
        ),
        out_specs=P("wave", None, "grp", None),
        check_vma=False,
    )
```

```python
import functools
import math

import jax
import jax.numpy as jnp
from jax import lax
from jax.experimental import pallas as pl
from jax.experimental.pallas import tpu as pltpu
from jax.sharding import PartitionSpec as P

M = 1280
NLON = 2688
QUARTER = NLON // 4
CHUNK = 256
ROWS = 8
LANES = 128


def round_up(value, unit):
    return -(-value // unit) * unit


def legendre_kernel(
    waves_hbm, se_hbm, so_hbm, le_hbm, lo_hbm, out_ref,
    waves_ref, se_ref, so_ref, le_ref, lo_ref, columns_ref, sym_ref, sems, wave_sem,
):
    pairs, lats, he = le_ref.shape
    ho = lo_ref.shape[2]
    groups = pairs // ROWS

    def odd_copies(g):
        at = pl.ds(pl.multiple_of(g * ROWS, ROWS), ROWS)
        return (
            pltpu.make_async_copy(lo_hbm.at[at], lo_ref.at[at], sems.at[0, g]),
            pltpu.make_async_copy(so_hbm.at[at], so_ref.at[at], sems.at[1, g]),
        )

    def even_copies(g):
        at = pl.ds(pl.multiple_of(g * ROWS, ROWS), ROWS)
        return (
            pltpu.make_async_copy(le_hbm.at[at], le_ref.at[at], sems.at[2, g]),
            pltpu.make_async_copy(se_hbm.at[:, at], se_ref.at[g], sems.at[3, g]),
        )

    wave_copy = pltpu.make_async_copy(waves_hbm, waves_ref, wave_sem)
    wave_copy.start()
    ahead = 2
    for g in range(min(ahead, groups)):
        for copy in even_copies(g) + odd_copies(g):
            copy.start()
    wave_copy.wait()

    ids_e = lax.broadcasted_iota(jnp.int32, (1, he), 1)
    ids_o = lax.broadcasted_iota(jnp.int32, (1, ho), 1)

    def split(panel, ids, count):
        in_low = jnp.where(ids < count, 1.0, 0.0).astype(jnp.bfloat16)
        lower = panel * in_low
        return jnp.concatenate([lower, panel - lower], axis=0)

    def both(panels, spectra):
        rows, width = panels[0].shape[0], spectra[0].shape[1]
        product = jnp.dot(
            jnp.concatenate(panels, axis=0),
            jnp.concatenate(spectra, axis=1),
            preferred_element_type=jnp.float32,
        )
        return product[:rows, :width], product[rows:, width:]

    @pl.loop(0, groups)
    def _(g):
        base = pl.multiple_of(g * ROWS, ROWS)
        for copy in even_copies(g):
            copy.wait()

        @pl.when(g + ahead < groups)
        def _():
            for copy in even_copies(g + ahead) + odd_copies(g + ahead):
                copy.start()

        columns_ref[...] = se_ref[g].astype(jnp.float32).reshape(columns_ref.shape)
        for p in range(0, ROWS, 2):
            even = [split(le_ref[base + q], ids_e, (M - waves_ref[base + q] + 1) // 2) for q in (p, p + 1)]
            xe = [columns_ref[pl.ds(q, he, stride=ROWS), :].astype(jnp.bfloat16) for q in (p, p + 1)]
            sym_ref[p], sym_ref[p + 1] = both(even, xe)
        for copy in odd_copies(g):
            copy.wait()
        for p in range(0, ROWS, 2):
            lows = [waves_ref[base + q] for q in (p, p + 1)]
            odd = [split(lo_ref[base + p + i], ids_o, (M - low) // 2) for i, low in enumerate(lows)]
            antis = both(odd, [so_ref[base + p], so_ref[base + p + 1]])
            for i, (low, anti) in enumerate(zip(lows, antis)):
                parity = low % 2
                sym = sym_ref[p + i]
                for h, rows in enumerate((sym + anti, sym - anti)):
                    for w in range(2):
                        start = (parity ^ w) * (lats * pairs) + base + p + i
                        out_ref[h, pl.ds(start, lats, stride=pairs), :] = rows[w * lats : (w + 1) * lats]


def in_hbm(x):
    return pltpu.with_memory_space_constraint(x, pltpu.HBM)


def in_vmem(x):
    return pltpu.with_memory_space_constraint(x, pltpu.VMEM)


def legendre_stage(waves, spectra_even, spectra_odd, legendre_even, legendre_odd):
    pairs, he, width = spectra_even.shape
    ho = spectra_odd.shape[1]
    lats = legendre_even.shape[1]
    by_column = jnp.transpose(spectra_even, (1, 0, 2))
    operands = (waves, by_column, spectra_odd, legendre_even, legendre_odd)
    return pl.pallas_call(
        legendre_kernel,
        out_shape=pltpu.VMEM((2, 2 * lats * pairs, width), jnp.float32),
        in_specs=[pl.BlockSpec(memory_space=pl.ANY)] * 5,
        out_specs=pl.BlockSpec(memory_space=pltpu.VMEM),
        scratch_shapes=[
            pltpu.SMEM((pairs,), jnp.int32),
            pltpu.VMEM((pairs // ROWS, he, ROWS, width), jnp.bfloat16),
            pltpu.VMEM((pairs, ho, width), jnp.bfloat16),
            pltpu.VMEM((pairs, lats, he), jnp.bfloat16),
            pltpu.VMEM((pairs, lats, ho), jnp.bfloat16),
            pltpu.VMEM((he * ROWS, width), jnp.float32),
            pltpu.VMEM((ROWS, 2 * lats, width), jnp.float32),
            pltpu.SemaphoreType.DMA((4, pairs // ROWS)),
            pltpu.SemaphoreType.DMA,
        ],
        compiler_params=pltpu.CompilerParams(vmem_limit_bytes=40 * 1024 * 1024),
        cost_estimate=pl.CostEstimate(
            flops=4 * pairs * lats * 2 * (he + ho) * width,
            bytes_accessed=2 * pairs * (he + ho) * (width + lats),
            transcendentals=0,
        ),
        name="legendre",
    )(*(in_hbm(x) for x in operands))


def pick_kernel(bands_ref, rows_ref, out_hbm, out_ref, sems):
    lats, _, _, pairs, _ = out_ref.shape
    piece = lats // sems.shape[0]

    def store(i):
        at = pl.ds(i * piece, piece)
        return pltpu.make_async_copy(out_ref.at[at], out_hbm.at[at], sems.at[i])

    def emit(slot, carry):
        band = bands_ref[slot]
        for h in range(2):
            for w in range(2):
                start = pl.multiple_of((w * lats + band) * pairs, ROWS)
                out_ref[slot, h, w] = rows_ref[h, pl.ds(start, pairs), :].astype(jnp.bfloat16)
        return carry

    for i in range(sems.shape[0]):
        lax.fori_loop(i * piece, (i + 1) * piece, emit, 0, unroll=4)
        store(i).start()
    for i in range(sems.shape[0]):
        store(i).wait()


def pick_latitudes(bands, rows, pairs):
    lats = bands.shape[0]
    width = rows.shape[2]
    shape = (lats, 2, 2, pairs, width)
    return pl.pallas_call(
        pick_kernel,
        out_shape=pltpu.HBM(shape, jnp.bfloat16),
        grid_spec=pltpu.PrefetchScalarGridSpec(
            num_scalar_prefetch=1,
            grid=(),
            in_specs=[pl.BlockSpec(memory_space=pltpu.VMEM)],
            out_specs=pl.BlockSpec(memory_space=pl.ANY),
            scratch_shapes=[pltpu.VMEM(shape, jnp.bfloat16), pltpu.SemaphoreType.DMA((4,))],
        ),
        compiler_params=pltpu.CompilerParams(vmem_limit_bytes=16 * 1024 * 1024),
        name="pick",
    )(bands, in_vmem(rows))


def even_wave(low):
    return jnp.where(low % 2 == 0, low, M - 1 - low)


def table_kernel(waves_ref, first_ref, rest_ref):
    even = even_wave(waves_ref[...])
    odd = M - 1 - even
    lane = lax.broadcasted_iota(jnp.int32, even.shape, 1).astype(jnp.float32)
    unit = 2.0 * math.pi / NLON

    def angle(product):
        turns = jnp.floor(product * (1.0 / NLON))
        return (product - turns * NLON) * unit

    for w, wave in enumerate((even, odd)):
        number = wave.astype(jnp.float32)
        factor = jnp.where(wave == 0, 1.0, 2.0)
        start = angle(number * lane)
        step = angle(number * LANES)
        c, s = factor * jnp.cos(start), -factor * jnp.sin(start)
        dc, ds = jnp.cos(step), jnp.sin(step)
        for b in range(0, QUARTER, LANES):
            at = slice(b % CHUNK, b % CHUNK + LANES)
            out_ref = rest_ref.at[b // CHUNK - 1] if b >= CHUNK else first_ref
            out_ref[w, 0, :, at] = c.astype(jnp.bfloat16)
            out_ref[w, 1, :, at] = s.astype(jnp.bfloat16)
            c, s = c * dc + s * ds, s * dc - c * ds


def wave_tables(waves):
    total = waves.shape[0]
    rows = 64
    rest = pl.cdiv(QUARTER, CHUNK) - 1
    return pl.pallas_call(
        table_kernel,
        out_shape=[
            jax.ShapeDtypeStruct((2, 2, total, CHUNK), jnp.bfloat16),
            pltpu.HBM((rest, 2, 2, total, CHUNK), jnp.bfloat16),
        ],
        grid=(total // rows,),
        in_specs=[pl.BlockSpec((rows, LANES), lambda i: (i, 0))],
        out_specs=[
            pl.BlockSpec((2, 2, rows, CHUNK), lambda i: (0, 0, i, 0)),
            pl.BlockSpec((rest, 2, 2, rows, CHUNK), lambda i: (0, 0, 0, i, 0)),
        ],
        compiler_params=pltpu.CompilerParams(vmem_limit_bytes=16 * 1024 * 1024),
        cost_estimate=pl.CostEstimate(
            flops=16 * total * QUARTER, bytes_accessed=8 * total * QUARTER, transcendentals=8 * total * LANES
        ),
        name="tables",
    )(jnp.broadcast_to(waves[:, None], (total, LANES)))


def fourier_kernel(
    arrived_ref, first_ref, rest_hbm, sign_hbm, out_hbm,
    left_ref, rest_ref, sign_ref, row_ref, sems, sign_sem, out_sems,
):
    devices, slots, _, _, pairs, width = arrived_ref.shape
    fields = width // 2
    total = devices * pairs
    chunks = 1 + rest_ref.shape[0]
    rows = 2 * fields

    def load(i):
        return pltpu.make_async_copy(rest_hbm.at[i - 1], rest_ref.at[i - 1], sems.at[i - 1])

    def block(s, i):
        table_ref = rest_ref.at[i - 1] if i else first_ref
        lo, hi = i * CHUNK, min((i + 1) * CHUNK, QUARTER)
        e, o = [
            jnp.dot(
                left_ref[s, w],
                table_ref[w].reshape(2 * total, CHUNK),
                preferred_element_type=jnp.float32,
            )[:, : hi - lo]
            for w in range(2)
        ]
        plus, minus = e + o, e - o
        for k, part in enumerate((plus[:rows], plus[rows:], minus[:rows], minus[rows:])):
            at = slice(k * QUARTER + lo, k * QUARTER + hi)
            row_ref[s * rows : (s + 1) * rows, at] = part.astype(jnp.bfloat16)

    sign_copy = pltpu.make_async_copy(sign_hbm, sign_ref, sign_sem)
    sign_copy.start()
    for i in range(1, chunks):
        load(i).start()

    stores = []
    for s in range(slots):
        turned = []
        for h in range(2):
            for w in range(2):
                x = jnp.concatenate([arrived_ref[d, s, h, w] for d in range(devices)], axis=0)
                xt = x.T
                at = slice(h * fields, (h + 1) * fields)
                left_ref[s, w, at, :total] = xt[:fields]
                left_ref[s, w, at, total:] = xt[fields:]
                turned.append((h, w, xt))
        if s == 0:
            sign_copy.wait()
        sign = sign_ref[0:1, :]
        for h, w, xt in turned:
            at = slice(rows + h * fields, rows + (h + 1) * fields)
            signed = (xt.astype(jnp.float32) * sign).astype(jnp.bfloat16)
            re, im = signed[:fields], signed[fields:]
            left_ref[s, w, at, :total] = im if w else re
            left_ref[s, w, at, total:] = -re if w else im
        block(s, 0)
    for i in range(1, chunks):
        load(i).wait()
    for s in range(slots):
        for i in range(1, chunks):
            block(s, i)
        base = slice(s * rows, (s + 1) * rows)
        copy = pltpu.make_async_copy(row_ref.at[base], out_hbm.at[base], out_sems.at[s])
        copy.start()
        stores.append(copy)
    for copy in stores:
        copy.wait()


def fourier_stage(arrived, sign, first, rest):
    devices, slots, _, _, pairs, width = arrived.shape
    fields = width // 2
    total = devices * pairs
    rows = slots * 2 * fields
    out = pl.pallas_call(
        fourier_kernel,
        out_shape=jax.ShapeDtypeStruct((rows, NLON), jnp.bfloat16),
        in_specs=[pl.BlockSpec(memory_space=pltpu.VMEM)] * 2 + [pl.BlockSpec(memory_space=pl.ANY)] * 2,
        out_specs=pl.BlockSpec(memory_space=pl.ANY),
        scratch_shapes=[
            pltpu.VMEM((slots, 2, 4 * fields, 2 * total), jnp.bfloat16),
            pltpu.VMEM(rest.shape, jnp.bfloat16),
            pltpu.VMEM(sign.shape, jnp.float32),
            pltpu.VMEM((rows, NLON), jnp.bfloat16),
            pltpu.SemaphoreType.DMA((rest.shape[0],)),
            pltpu.SemaphoreType.DMA,
            pltpu.SemaphoreType.DMA((slots,)),
        ],
        compiler_params=pltpu.CompilerParams(vmem_limit_bytes=16 * 1024 * 1024),
        cost_estimate=pl.CostEstimate(
            flops=16 * rows * total * QUARTER, bytes_accessed=8 * total * QUARTER, transcendentals=0
        ),
        name="fourier",
    )(arrived, first, in_hbm(rest), in_hbm(sign))
    return out.reshape(slots, 2, fields, NLON)


def on_device(wave_pairs, band_owner, spectra_even, spectra_odd, legendre_even, legendre_odd):
    devices = lax.axis_size("wave")
    pairs = round_up(wave_pairs.shape[0], ROWS)
    extra = pairs - wave_pairs.shape[0]
    slots = band_owner.shape[0]
    width = spectra_even.shape[2]
    if extra:
        wave_pairs = jnp.pad(wave_pairs, (0, extra))
        spectra_even, spectra_odd, legendre_even, legendre_odd = (
            jnp.pad(a, ((0, extra), (0, 0), (0, 0)))
            for a in (spectra_even, spectra_odd, legendre_even, legendre_odd)
        )

    rest = round_up(pairs + slots, LANES) - pairs - slots
    own = jnp.concatenate([wave_pairs, band_owner, jnp.zeros(rest, jnp.int32)])
    own = jnp.broadcast_to(own, (devices, 1) + own.shape)
    index = lax.all_to_all(own, "wave", 0, 0, tiled=True)[:, 0]
    all_bands = index[:, pairs : pairs + slots].reshape(-1)
    rows = legendre_stage(wave_pairs, spectra_even, spectra_odd, legendre_even, legendre_odd)
    picked = pick_latitudes(all_bands, rows, pairs)
    index, picked = lax.optimization_barrier((index, picked))
    arrived = lax.all_to_all(picked.reshape(devices, slots, 2, 2, pairs, width), "wave", 0, 0, tiled=True)
    all_pairs = index[:, :pairs].reshape(-1)
    sign = jnp.where(even_wave(all_pairs) % 4 == 0, 1.0, -1.0).astype(jnp.float32)
    sign, all_pairs = lax.optimization_barrier((jnp.broadcast_to(sign, (ROWS,) + sign.shape), all_pairs))
    return fourier_stage(arrived, sign, *wave_tables(all_pairs))


def solution(mesh):
    return jax.shard_map(
        on_device,
        mesh=mesh,
        in_specs=(
            P("wave"),
            P("wave"),
            P("wave", None, "grp"),
            P("wave", None, "grp"),
            P("wave", None, None),
            P("wave", None, None),
        ),
        out_specs=P("wave", None, "grp", None),
        check_vma=False,
    )
```

```python
import functools
import math

import jax
import jax.numpy as jnp
from jax import lax
from jax.experimental import pallas as pl
from jax.experimental.pallas import tpu as pltpu
from jax.sharding import PartitionSpec as P

M = 1280
NLON = 2688
QUARTER = NLON // 4
CHUNK = 256
ROWS = 8
LANES = 128


def round_up(value, unit):
    return -(-value // unit) * unit


def legendre_kernel(
    waves_hbm, se_hbm, so_hbm, le_hbm, lo_hbm, out_ref,
    waves_ref, se_ref, so_ref, le_ref, lo_ref, columns_ref, anti_ref, sems, wave_sem,
):
    pairs, lats, he = le_ref.shape
    ho = lo_ref.shape[2]
    groups = pairs // ROWS

    def odd_copies(g):
        at = pl.ds(pl.multiple_of(g * ROWS, ROWS), ROWS)
        return (
            pltpu.make_async_copy(lo_hbm.at[at], lo_ref.at[at], sems.at[0, g]),
            pltpu.make_async_copy(so_hbm.at[at], so_ref.at[at], sems.at[1, g]),
        )

    def even_copies(g):
        at = pl.ds(pl.multiple_of(g * ROWS, ROWS), ROWS)
        return (
            pltpu.make_async_copy(le_hbm.at[at], le_ref.at[at], sems.at[2, g]),
            pltpu.make_async_copy(se_hbm.at[:, at], se_ref.at[g], sems.at[3, g]),
        )

    wave_copy = pltpu.make_async_copy(waves_hbm, waves_ref, wave_sem)
    wave_copy.start()
    ahead = 3
    for g in range(min(ahead, groups)):
        for copy in odd_copies(g) + even_copies(g):
            copy.start()
    wave_copy.wait()

    ids_e = lax.broadcasted_iota(jnp.int32, (1, he), 1)
    ids_o = lax.broadcasted_iota(jnp.int32, (1, ho), 1)

    def split(panel, ids, count):
        in_low = jnp.where(ids < count, 1.0, 0.0).astype(jnp.bfloat16)
        lower = panel * in_low
        return jnp.concatenate([lower, panel - lower], axis=0)

    def both(panels, spectra):
        rows, width = panels[0].shape[0], spectra[0].shape[1]
        product = jnp.dot(
            jnp.concatenate(panels, axis=0),
            jnp.concatenate(spectra, axis=1),
            preferred_element_type=jnp.float32,
        )
        return product[:rows, :width], product[rows:, width:]

    @pl.loop(0, groups)
    def _(g):
        base = pl.multiple_of(g * ROWS, ROWS)
        for copy in odd_copies(g) + even_copies(g):
            copy.wait()

        @pl.when(g + ahead < groups)
        def _():
            for copy in odd_copies(g + ahead) + even_copies(g + ahead):
                copy.start()

        for p in range(0, ROWS, 2):
            odd = [split(lo_ref[base + q], ids_o, (M - waves_ref[base + q]) // 2) for q in (p, p + 1)]
            anti_ref[p], anti_ref[p + 1] = both(odd, [so_ref[base + p], so_ref[base + p + 1]])
        columns_ref[...] = se_ref[g].astype(jnp.float32).reshape(columns_ref.shape)
        for p in range(0, ROWS, 2):
            lows = [waves_ref[base + q] for q in (p, p + 1)]
            even = [split(le_ref[base + p + i], ids_e, (M - low + 1) // 2) for i, low in enumerate(lows)]
            xe = [columns_ref[pl.ds(q, he, stride=ROWS), :].astype(jnp.bfloat16) for q in (p, p + 1)]
            for i, (low, sym) in enumerate(zip(lows, both(even, xe))):
                parity = low % 2
                anti = anti_ref[p + i]
                for h, rows in enumerate((sym + anti, sym - anti)):
                    for w in range(2):
                        start = (parity ^ w) * (lats * pairs) + base + p + i
                        out_ref[h, pl.ds(start, lats, stride=pairs), :] = rows[w * lats : (w + 1) * lats]


def in_hbm(x):
    return pltpu.with_memory_space_constraint(x, pltpu.HBM)


def in_vmem(x):
    return pltpu.with_memory_space_constraint(x, pltpu.VMEM)


def legendre_stage(waves, spectra_even, spectra_odd, legendre_even, legendre_odd):
    pairs, he, width = spectra_even.shape
    ho = spectra_odd.shape[1]
    lats = legendre_even.shape[1]
    by_column = jnp.transpose(spectra_even, (1, 0, 2))
    operands = (waves, by_column, spectra_odd, legendre_even, legendre_odd)
    return pl.pallas_call(
        legendre_kernel,
        out_shape=pltpu.VMEM((2, 2 * lats * pairs, width), jnp.float32),
        in_specs=[pl.BlockSpec(memory_space=pl.ANY)] * 5,
        out_specs=pl.BlockSpec(memory_space=pltpu.VMEM),
        scratch_shapes=[
            pltpu.SMEM((pairs,), jnp.int32),
            pltpu.VMEM((pairs // ROWS, he, ROWS, width), jnp.bfloat16),
            pltpu.VMEM((pairs, ho, width), jnp.bfloat16),
            pltpu.VMEM((pairs, lats, he), jnp.bfloat16),
            pltpu.VMEM((pairs, lats, ho), jnp.bfloat16),
            pltpu.VMEM((he * ROWS, width), jnp.float32),
            pltpu.VMEM((ROWS, 2 * lats, width), jnp.float32),
            pltpu.SemaphoreType.DMA((4, pairs // ROWS)),
            pltpu.SemaphoreType.DMA,
        ],
        compiler_params=pltpu.CompilerParams(vmem_limit_bytes=40 * 1024 * 1024),
        cost_estimate=pl.CostEstimate(
            flops=4 * pairs * lats * 2 * (he + ho) * width,
            bytes_accessed=2 * pairs * (he + ho) * (width + lats),
            transcendentals=0,
        ),
        name="legendre",
    )(*(in_hbm(x) for x in operands))


def pick_kernel(bands_ref, rows_ref, out_hbm, out_ref, sems):
    lats, _, _, pairs, _ = out_ref.shape
    piece = lats // sems.shape[0]

    def store(i):
        at = pl.ds(i * piece, piece)
        return pltpu.make_async_copy(out_ref.at[at], out_hbm.at[at], sems.at[i])

    def emit(slot, carry):
        band = bands_ref[slot]
        for h in range(2):
            for w in range(2):
                start = pl.multiple_of((w * lats + band) * pairs, ROWS)
                out_ref[slot, h, w] = rows_ref[h, pl.ds(start, pairs), :].astype(jnp.bfloat16)
        return carry

    for i in range(sems.shape[0]):
        lax.fori_loop(i * piece, (i + 1) * piece, emit, 0, unroll=4)
        store(i).start()
    for i in range(sems.shape[0]):
        store(i).wait()


def pick_latitudes(bands, rows, pairs):
    lats = bands.shape[0]
    width = rows.shape[2]
    shape = (lats, 2, 2, pairs, width)
    return pl.pallas_call(
        pick_kernel,
        out_shape=pltpu.HBM(shape, jnp.bfloat16),
        grid_spec=pltpu.PrefetchScalarGridSpec(
            num_scalar_prefetch=1,
            grid=(),
            in_specs=[pl.BlockSpec(memory_space=pltpu.VMEM)],
            out_specs=pl.BlockSpec(memory_space=pl.ANY),
            scratch_shapes=[pltpu.VMEM(shape, jnp.bfloat16), pltpu.SemaphoreType.DMA((4,))],
        ),
        compiler_params=pltpu.CompilerParams(vmem_limit_bytes=16 * 1024 * 1024),
        name="pick",
    )(bands, in_vmem(rows))


def even_wave(low):
    return jnp.where(low % 2 == 0, low, M - 1 - low)


def table_kernel(waves_ref, first_ref, rest_ref):
    even = even_wave(waves_ref[...])
    odd = M - 1 - even
    lane = lax.broadcasted_iota(jnp.int32, even.shape, 1).astype(jnp.float32)
    unit = 2.0 * math.pi / NLON

    def angle(product):
        turns = jnp.floor(product * (1.0 / NLON))
        return (product - turns * NLON) * unit

    for w, wave in enumerate((even, odd)):
        number = wave.astype(jnp.float32)
        factor = jnp.where(wave == 0, 1.0, 2.0)
        start = angle(number * lane)
        step = angle(number * LANES)
        c, s = factor * jnp.cos(start), -factor * jnp.sin(start)
        dc, ds = jnp.cos(step), jnp.sin(step)
        for b in range(0, QUARTER, LANES):
            at = slice(b % CHUNK, b % CHUNK + LANES)
            out_ref = rest_ref.at[b // CHUNK - 1] if b >= CHUNK else first_ref
            out_ref[w, 0, :, at] = c.astype(jnp.bfloat16)
            out_ref[w, 1, :, at] = s.astype(jnp.bfloat16)
            c, s = c * dc + s * ds, s * dc - c * ds


def wave_tables(waves):
    total = waves.shape[0]
    rows = 64
    rest = pl.cdiv(QUARTER, CHUNK) - 1
    return pl.pallas_call(
        table_kernel,
        out_shape=[
            jax.ShapeDtypeStruct((2, 2, total, CHUNK), jnp.bfloat16),
            pltpu.HBM((rest, 2, 2, total, CHUNK), jnp.bfloat16),
        ],
        grid=(total // rows,),
        in_specs=[pl.BlockSpec((rows, LANES), lambda i: (i, 0))],
        out_specs=[
            pl.BlockSpec((2, 2, rows, CHUNK), lambda i: (0, 0, i, 0)),
            pl.BlockSpec((rest, 2, 2, rows, CHUNK), lambda i: (0, 0, 0, i, 0)),
        ],
        compiler_params=pltpu.CompilerParams(vmem_limit_bytes=16 * 1024 * 1024),
        cost_estimate=pl.CostEstimate(
            flops=16 * total * QUARTER, bytes_accessed=8 * total * QUARTER, transcendentals=8 * total * LANES
        ),
        name="tables",
    )(jnp.broadcast_to(waves[:, None], (total, LANES)))


def fourier_kernel(
    arrived_ref, first_ref, rest_hbm, sign_hbm, out_hbm,
    left_ref, rest_ref, sign_ref, row_ref, sems, sign_sem, out_sems,
):
    devices, slots, _, _, pairs, width = arrived_ref.shape
    fields = width // 2
    total = devices * pairs
    chunks = 1 + rest_ref.shape[0]
    rows = 2 * fields

    def load(i):
        return pltpu.make_async_copy(rest_hbm.at[i - 1], rest_ref.at[i - 1], sems.at[i - 1])

    def block(s, i):
        table_ref = rest_ref.at[i - 1] if i else first_ref
        lo, hi = i * CHUNK, min((i + 1) * CHUNK, QUARTER)
        e, o = [
            jnp.dot(
                left_ref[s, w],
                table_ref[w].reshape(2 * total, CHUNK),
                preferred_element_type=jnp.float32,
            )[:, : hi - lo]
            for w in range(2)
        ]
        plus, minus = e + o, e - o
        for k, part in enumerate((plus[:rows], plus[rows:], minus[:rows], minus[rows:])):
            at = slice(k * QUARTER + lo, k * QUARTER + hi)
            row_ref[s * rows : (s + 1) * rows, at] = part.astype(jnp.bfloat16)

    sign_copy = pltpu.make_async_copy(sign_hbm, sign_ref, sign_sem)
    sign_copy.start()
    for i in range(1, chunks):
        load(i).start()

    stores = []
    for s in range(slots):
        turned = []
        for h in range(2):
            for w in range(2):
                x = jnp.concatenate([arrived_ref[d, s, h, w] for d in range(devices)], axis=0)
                xt = x.T
                at = slice(h * fields, (h + 1) * fields)
                left_ref[s, w, at, :total] = xt[:fields]
                left_ref[s, w, at, total:] = xt[fields:]
                turned.append((h, w, xt))
        if s == 0:
            sign_copy.wait()
        sign = sign_ref[0:1, :]
        for h, w, xt in turned:
            at = slice(rows + h * fields, rows + (h + 1) * fields)
            signed = (xt.astype(jnp.float32) * sign).astype(jnp.bfloat16)
            re, im = signed[:fields], signed[fields:]
            left_ref[s, w, at, :total] = im if w else re
            left_ref[s, w, at, total:] = -re if w else im
        block(s, 0)
    for s in range(slots):
        for i in range(1, chunks):
            if s == 0:
                load(i).wait()
            block(s, i)
        base = slice(s * rows, (s + 1) * rows)
        copy = pltpu.make_async_copy(row_ref.at[base], out_hbm.at[base], out_sems.at[s])
        copy.start()
        stores.append(copy)
    for copy in stores:
        copy.wait()


def fourier_stage(arrived, sign, first, rest):
    devices, slots, _, _, pairs, width = arrived.shape
    fields = width // 2
    total = devices * pairs
    rows = slots * 2 * fields
    out = pl.pallas_call(
        fourier_kernel,
        out_shape=jax.ShapeDtypeStruct((rows, NLON), jnp.bfloat16),
        in_specs=[pl.BlockSpec(memory_space=pltpu.VMEM)] * 2 + [pl.BlockSpec(memory_space=pl.ANY)] * 2,
        out_specs=pl.BlockSpec(memory_space=pl.ANY),
        scratch_shapes=[
            pltpu.VMEM((slots, 2, 4 * fields, 2 * total), jnp.bfloat16),
            pltpu.VMEM(rest.shape, jnp.bfloat16),
            pltpu.VMEM(sign.shape, jnp.float32),
            pltpu.VMEM((rows, NLON), jnp.bfloat16),
            pltpu.SemaphoreType.DMA((rest.shape[0],)),
            pltpu.SemaphoreType.DMA,
            pltpu.SemaphoreType.DMA((slots,)),
        ],
        compiler_params=pltpu.CompilerParams(vmem_limit_bytes=16 * 1024 * 1024),
        cost_estimate=pl.CostEstimate(
            flops=16 * rows * total * QUARTER, bytes_accessed=8 * total * QUARTER, transcendentals=0
        ),
        name="fourier",
    )(arrived, first, in_hbm(rest), in_hbm(sign))
    return out.reshape(slots, 2, fields, NLON)


def on_device(wave_pairs, band_owner, spectra_even, spectra_odd, legendre_even, legendre_odd):
    devices = lax.axis_size("wave")
    pairs = round_up(wave_pairs.shape[0], ROWS)
    extra = pairs - wave_pairs.shape[0]
    slots = band_owner.shape[0]
    width = spectra_even.shape[2]
    if extra:
        wave_pairs = jnp.pad(wave_pairs, (0, extra))
        spectra_even, spectra_odd, legendre_even, legendre_odd = (
            jnp.pad(a, ((0, extra), (0, 0), (0, 0)))
            for a in (spectra_even, spectra_odd, legendre_even, legendre_odd)
        )

    rest = round_up(pairs + slots, LANES) - pairs - slots
    own = jnp.concatenate([wave_pairs, band_owner, jnp.zeros(rest, jnp.int32)])
    own = jnp.broadcast_to(own, (devices, 1) + own.shape)
    index = lax.all_to_all(own, "wave", 0, 0, tiled=True)[:, 0]
    all_bands = index[:, pairs : pairs + slots].reshape(-1)
    rows = legendre_stage(wave_pairs, spectra_even, spectra_odd, legendre_even, legendre_odd)
    picked = pick_latitudes(all_bands, rows, pairs)
    index, picked = lax.optimization_barrier((index, picked))
    arrived = lax.all_to_all(picked.reshape(devices, slots, 2, 2, pairs, width), "wave", 0, 0, tiled=True)
    all_pairs = index[:, :pairs].reshape(-1)
    sign = jnp.where(even_wave(all_pairs) % 4 == 0, 1.0, -1.0).astype(jnp.float32)
    sign, all_pairs = lax.optimization_barrier((jnp.broadcast_to(sign, (ROWS,) + sign.shape), all_pairs))
    return fourier_stage(arrived, sign, *wave_tables(all_pairs))


def solution(mesh):
    return jax.shard_map(
        on_device,
        mesh=mesh,
        in_specs=(
            P("wave"),
            P("wave"),
            P("wave", None, "grp"),
            P("wave", None, "grp"),
            P("wave", None, None),
            P("wave", None, None),
        ),
        out_specs=P("wave", None, "grp", None),
        check_vma=False,
    )
```

```python
import functools
import math

import jax
import jax.numpy as jnp
from jax import lax
from jax.experimental import pallas as pl
from jax.experimental.pallas import tpu as pltpu
from jax.sharding import PartitionSpec as P

M = 1280
NLON = 2688
QUARTER = NLON // 4
CHUNK = 256
ROWS = 8
LANES = 128


def round_up(value, unit):
    return -(-value // unit) * unit


def legendre_kernel(
    waves_hbm, se_hbm, so_hbm, le_hbm, lo_hbm, out_ref,
    waves_ref, se_ref, so_ref, le_ref, lo_ref, columns_ref, anti_ref, sems, wave_sem,
):
    pairs, lats, he = le_ref.shape
    ho = lo_ref.shape[2]
    groups = pairs // ROWS

    def odd_copies(g):
        at = pl.ds(pl.multiple_of(g * ROWS, ROWS), ROWS)
        return (
            pltpu.make_async_copy(lo_hbm.at[at], lo_ref.at[at], sems.at[0, g]),
            pltpu.make_async_copy(so_hbm.at[at], so_ref.at[at], sems.at[1, g]),
        )

    def even_copies(g):
        at = pl.ds(pl.multiple_of(g * ROWS, ROWS), ROWS)
        return (
            pltpu.make_async_copy(le_hbm.at[at], le_ref.at[at], sems.at[2, g]),
            pltpu.make_async_copy(se_hbm.at[:, at], se_ref.at[g], sems.at[3, g]),
        )

    wave_copy = pltpu.make_async_copy(waves_hbm, waves_ref, wave_sem)
    wave_copy.start()
    ahead = 3
    for g in range(min(ahead, groups)):
        for copy in odd_copies(g) + even_copies(g):
            copy.start()
    wave_copy.wait()

    ids_e = lax.broadcasted_iota(jnp.int32, (1, he), 1)
    ids_o = lax.broadcasted_iota(jnp.int32, (1, ho), 1)

    def split(panel, ids, count):
        in_low = jnp.where(ids < count, 1.0, 0.0).astype(jnp.bfloat16)
        lower = panel * in_low
        return jnp.concatenate([lower, panel - lower], axis=0)

    def both(panels, spectra):
        rows, width = panels[0].shape[0], spectra[0].shape[1]
        product = jnp.dot(
            jnp.concatenate(panels, axis=0),
            jnp.concatenate(spectra, axis=1),
            preferred_element_type=jnp.float32,
        )
        return product[:rows, :width], product[rows:, width:]

    @pl.loop(0, groups)
    def _(g):
        base = pl.multiple_of(g * ROWS, ROWS)
        for copy in odd_copies(g) + even_copies(g):
            copy.wait()

        @pl.when(g + ahead < groups)
        def _():
            for copy in odd_copies(g + ahead) + even_copies(g + ahead):
                copy.start()

        for p in range(0, ROWS, 2):
            odd = [split(lo_ref[base + q], ids_o, (M - waves_ref[base + q]) // 2) for q in (p, p + 1)]
            anti_ref[p], anti_ref[p + 1] = both(odd, [so_ref[base + p], so_ref[base + p + 1]])
        columns_ref[...] = se_ref[g].astype(jnp.float32).reshape(columns_ref.shape)
        for p in range(0, ROWS, 2):
            lows = [waves_ref[base + q] for q in (p, p + 1)]
            even = [split(le_ref[base + p + i], ids_e, (M - low + 1) // 2) for i, low in enumerate(lows)]
            xe = [columns_ref[pl.ds(q, he, stride=ROWS), :].astype(jnp.bfloat16) for q in (p, p + 1)]
            for i, (low, sym) in enumerate(zip(lows, both(even, xe))):
                parity = low % 2
                anti = anti_ref[p + i]
                for h, rows in enumerate((sym + anti, sym - anti)):
                    for w in range(2):
                        start = (parity ^ w) * (lats * pairs) + base + p + i
                        out_ref[h, pl.ds(start, lats, stride=pairs), :] = rows[w * lats : (w + 1) * lats]


def in_hbm(x):
    return pltpu.with_memory_space_constraint(x, pltpu.HBM)


def in_vmem(x):
    return pltpu.with_memory_space_constraint(x, pltpu.VMEM)


def legendre_stage(waves, spectra_even, spectra_odd, legendre_even, legendre_odd):
    pairs, he, width = spectra_even.shape
    ho = spectra_odd.shape[1]
    lats = legendre_even.shape[1]
    by_column = jnp.transpose(spectra_even, (1, 0, 2))
    operands = (waves, by_column, spectra_odd, legendre_even, legendre_odd)
    return pl.pallas_call(
        legendre_kernel,
        out_shape=pltpu.VMEM((2, 2 * lats * pairs, width), jnp.float32),
        in_specs=[pl.BlockSpec(memory_space=pl.ANY)] * 5,
        out_specs=pl.BlockSpec(memory_space=pltpu.VMEM),
        scratch_shapes=[
            pltpu.SMEM((pairs,), jnp.int32),
            pltpu.VMEM((pairs // ROWS, he, ROWS, width), jnp.bfloat16),
            pltpu.VMEM((pairs, ho, width), jnp.bfloat16),
            pltpu.VMEM((pairs, lats, he), jnp.bfloat16),
            pltpu.VMEM((pairs, lats, ho), jnp.bfloat16),
            pltpu.VMEM((he * ROWS, width), jnp.float32),
            pltpu.VMEM((ROWS, 2 * lats, width), jnp.float32),
            pltpu.SemaphoreType.DMA((4, pairs // ROWS)),
            pltpu.SemaphoreType.DMA,
        ],
        compiler_params=pltpu.CompilerParams(vmem_limit_bytes=40 * 1024 * 1024),
        cost_estimate=pl.CostEstimate(
            flops=4 * pairs * lats * 2 * (he + ho) * width,
            bytes_accessed=2 * pairs * (he + ho) * (width + lats),
            transcendentals=0,
        ),
        name="legendre",
    )(*(in_hbm(x) for x in operands))


def pick_kernel(bands_ref, rows_ref, out_hbm, out_ref, sems):
    lats, _, _, pairs, _ = out_ref.shape
    piece = lats // sems.shape[0]

    def store(i):
        at = pl.ds(i * piece, piece)
        return pltpu.make_async_copy(out_ref.at[at], out_hbm.at[at], sems.at[i])

    def emit(slot, carry):
        band = bands_ref[slot]
        for h in range(2):
            for w in range(2):
                start = pl.multiple_of((w * lats + band) * pairs, ROWS)
                out_ref[slot, h, w] = rows_ref[h, pl.ds(start, pairs), :].astype(jnp.bfloat16)
        return carry

    for i in range(sems.shape[0]):
        lax.fori_loop(i * piece, (i + 1) * piece, emit, 0, unroll=4)
        store(i).start()
    for i in range(sems.shape[0]):
        store(i).wait()


def pick_latitudes(bands, rows, pairs):
    lats = bands.shape[0]
    width = rows.shape[2]
    shape = (lats, 2, 2, pairs, width)
    return pl.pallas_call(
        pick_kernel,
        out_shape=pltpu.HBM(shape, jnp.bfloat16),
        grid_spec=pltpu.PrefetchScalarGridSpec(
            num_scalar_prefetch=1,
            grid=(),
            in_specs=[pl.BlockSpec(memory_space=pltpu.VMEM)],
            out_specs=pl.BlockSpec(memory_space=pl.ANY),
            scratch_shapes=[pltpu.VMEM(shape, jnp.bfloat16), pltpu.SemaphoreType.DMA((4,))],
        ),
        compiler_params=pltpu.CompilerParams(vmem_limit_bytes=16 * 1024 * 1024),
        name="pick",
    )(bands, in_vmem(rows))


def even_wave(low):
    return jnp.where(low % 2 == 0, low, M - 1 - low)


def table_part(w, i, first_ref, second_ref, rest_ref):
    if i == 0:
        return first_ref.at[w]
    return second_ref if (w, i) == (0, 1) else rest_ref.at[2 * i + w - 3]


def table_kernel(waves_ref, first_ref, second_ref, rest_ref):
    even = even_wave(waves_ref[...])
    odd = M - 1 - even
    lane = lax.broadcasted_iota(jnp.int32, even.shape, 1).astype(jnp.float32)
    unit = 2.0 * math.pi / NLON

    def angle(product):
        turns = jnp.floor(product * (1.0 / NLON))
        return (product - turns * NLON) * unit

    for w, wave in enumerate((even, odd)):
        number = wave.astype(jnp.float32)
        factor = jnp.where(wave == 0, 1.0, 2.0)
        start = angle(number * lane)
        step = angle(number * LANES)
        c, s = factor * jnp.cos(start), -factor * jnp.sin(start)
        dc, ds = jnp.cos(step), jnp.sin(step)
        for b in range(0, QUARTER, LANES):
            at = slice(b % CHUNK, b % CHUNK + LANES)
            out_ref = table_part(w, b // CHUNK, first_ref, second_ref, rest_ref)
            out_ref[0, :, at] = c.astype(jnp.bfloat16)
            out_ref[1, :, at] = s.astype(jnp.bfloat16)
            c, s = c * dc + s * ds, s * dc - c * ds


def wave_tables(waves):
    total = waves.shape[0]
    rows = 64
    rest = 2 * pl.cdiv(QUARTER, CHUNK) - 3
    return pl.pallas_call(
        table_kernel,
        out_shape=[
            jax.ShapeDtypeStruct((2, 2, total, CHUNK), jnp.bfloat16),
            jax.ShapeDtypeStruct((2, total, CHUNK), jnp.bfloat16),
            pltpu.HBM((rest, 2, total, CHUNK), jnp.bfloat16),
        ],
        grid=(total // rows,),
        in_specs=[pl.BlockSpec((rows, LANES), lambda i: (i, 0))],
        out_specs=[
            pl.BlockSpec((2, 2, rows, CHUNK), lambda i: (0, 0, i, 0)),
            pl.BlockSpec((2, rows, CHUNK), lambda i: (0, i, 0)),
            pl.BlockSpec((rest, 2, rows, CHUNK), lambda i: (0, 0, i, 0)),
        ],
        compiler_params=pltpu.CompilerParams(vmem_limit_bytes=16 * 1024 * 1024),
        cost_estimate=pl.CostEstimate(
            flops=16 * total * QUARTER, bytes_accessed=8 * total * QUARTER, transcendentals=8 * total * LANES
        ),
        name="tables",
    )(jnp.broadcast_to(waves[:, None], (total, LANES)))


def fourier_kernel(
    arrived_ref, first_ref, second_ref, rest_hbm, sign_hbm, out_hbm,
    left_ref, rest_ref, sign_ref, row_ref, sems, sign_sem, out_sems,
):
    devices, slots, _, _, pairs, width = arrived_ref.shape
    fields = width // 2
    total = devices * pairs
    chunks = (rest_ref.shape[0] + 3) // 2
    rows = 2 * fields

    def load(i):
        return pltpu.make_async_copy(rest_hbm.at[i], rest_ref.at[i], sems.at[i])

    def block(s, i):
        lo, hi = i * CHUNK, min((i + 1) * CHUNK, QUARTER)
        e, o = [
            jnp.dot(
                left_ref[s, w],
                table_part(w, i, first_ref, second_ref, rest_ref)[...].reshape(2 * total, CHUNK),
                preferred_element_type=jnp.float32,
            )[:, : hi - lo]
            for w in range(2)
        ]
        plus, minus = e + o, e - o
        for k, part in enumerate((plus[:rows], plus[rows:], minus[:rows], minus[rows:])):
            at = slice(k * QUARTER + lo, k * QUARTER + hi)
            row_ref[s * rows : (s + 1) * rows, at] = part.astype(jnp.bfloat16)

    sign_copy = pltpu.make_async_copy(sign_hbm, sign_ref, sign_sem)
    sign_copy.start()
    for i in range(rest_ref.shape[0]):
        load(i).start()

    stores = []
    for s in range(slots):
        turned = []
        for h in range(2):
            for w in range(2):
                x = jnp.concatenate([arrived_ref[d, s, h, w] for d in range(devices)], axis=0)
                xt = x.T
                at = slice(h * fields, (h + 1) * fields)
                left_ref[s, w, at, :total] = xt[:fields]
                left_ref[s, w, at, total:] = xt[fields:]
                turned.append((h, w, xt))
        if s == 0:
            sign_copy.wait()
        sign = sign_ref[0:1, :]
        for h, w, xt in turned:
            at = slice(rows + h * fields, rows + (h + 1) * fields)
            signed = (xt.astype(jnp.float32) * sign).astype(jnp.bfloat16)
            re, im = signed[:fields], signed[fields:]
            left_ref[s, w, at, :total] = im if w else re
            left_ref[s, w, at, total:] = -re if w else im
        block(s, 0)
    for i in range(rest_ref.shape[0]):
        load(i).wait()
    for s in range(slots):
        for i in range(1, chunks):
            block(s, i)
        base = slice(s * rows, (s + 1) * rows)
        copy = pltpu.make_async_copy(row_ref.at[base], out_hbm.at[base], out_sems.at[s])
        copy.start()
        stores.append(copy)
    for copy in stores:
        copy.wait()


def fourier_stage(arrived, sign, first, second, rest):
    devices, slots, _, _, pairs, width = arrived.shape
    fields = width // 2
    total = devices * pairs
    rows = slots * 2 * fields
    out = pl.pallas_call(
        fourier_kernel,
        out_shape=jax.ShapeDtypeStruct((rows, NLON), jnp.bfloat16),
        in_specs=[pl.BlockSpec(memory_space=pltpu.VMEM)] * 3 + [pl.BlockSpec(memory_space=pl.ANY)] * 2,
        out_specs=pl.BlockSpec(memory_space=pl.ANY),
        scratch_shapes=[
            pltpu.VMEM((slots, 2, 4 * fields, 2 * total), jnp.bfloat16),
            pltpu.VMEM(rest.shape, jnp.bfloat16),
            pltpu.VMEM(sign.shape, jnp.float32),
            pltpu.VMEM((rows, NLON), jnp.bfloat16),
            pltpu.SemaphoreType.DMA((rest.shape[0],)),
            pltpu.SemaphoreType.DMA,
            pltpu.SemaphoreType.DMA((slots,)),
        ],
        compiler_params=pltpu.CompilerParams(vmem_limit_bytes=16 * 1024 * 1024),
        cost_estimate=pl.CostEstimate(
            flops=16 * rows * total * QUARTER, bytes_accessed=8 * total * QUARTER, transcendentals=0
        ),
        name="fourier",
    )(arrived, first, second, in_hbm(rest), in_hbm(sign))
    return out.reshape(slots, 2, fields, NLON)


def on_device(wave_pairs, band_owner, spectra_even, spectra_odd, legendre_even, legendre_odd):
    devices = lax.axis_size("wave")
    pairs = round_up(wave_pairs.shape[0], ROWS)
    extra = pairs - wave_pairs.shape[0]
    slots = band_owner.shape[0]
    width = spectra_even.shape[2]
    if extra:
        wave_pairs = jnp.pad(wave_pairs, (0, extra))
        spectra_even, spectra_odd, legendre_even, legendre_odd = (
            jnp.pad(a, ((0, extra), (0, 0), (0, 0)))
            for a in (spectra_even, spectra_odd, legendre_even, legendre_odd)
        )

    rest = round_up(pairs + slots, LANES) - pairs - slots
    own = jnp.concatenate([wave_pairs, band_owner, jnp.zeros(rest, jnp.int32)])
    own = jnp.broadcast_to(own, (devices, 1) + own.shape)
    index = lax.all_to_all(own, "wave", 0, 0, tiled=True)[:, 0]
    all_bands = index[:, pairs : pairs + slots].reshape(-1)
    rows = legendre_stage(wave_pairs, spectra_even, spectra_odd, legendre_even, legendre_odd)
    picked = pick_latitudes(all_bands, rows, pairs)
    index, picked = lax.optimization_barrier((index, picked))
    arrived = lax.all_to_all(picked.reshape(devices, slots, 2, 2, pairs, width), "wave", 0, 0, tiled=True)
    all_pairs = index[:, :pairs].reshape(-1)
    sign = jnp.where(even_wave(all_pairs) % 4 == 0, 1.0, -1.0).astype(jnp.float32)
    sign, all_pairs = lax.optimization_barrier((jnp.broadcast_to(sign, (ROWS,) + sign.shape), all_pairs))
    return fourier_stage(arrived, sign, *wave_tables(all_pairs))


def solution(mesh):
    return jax.shard_map(
        on_device,
        mesh=mesh,
        in_specs=(
            P("wave"),
            P("wave"),
            P("wave", None, "grp"),
            P("wave", None, "grp"),
            P("wave", None, None),
            P("wave", None, None),
        ),
        out_specs=P("wave", None, "grp", None),
        check_vma=False,
    )
```

```python
import functools
import math

import jax
import jax.numpy as jnp
from jax import lax
from jax.experimental import pallas as pl
from jax.experimental.pallas import tpu as pltpu
from jax.sharding import PartitionSpec as P

M = 1280
NLON = 2688
QUARTER = NLON // 4
CHUNK = 256
ROWS = 8
LANES = 128


def round_up(value, unit):
    return -(-value // unit) * unit


def legendre_kernel(
    waves_hbm, se_hbm, so_hbm, le_hbm, lo_hbm, out_ref,
    waves_ref, se_ref, so_ref, le_ref, lo_ref, columns_ref, anti_ref, sems, wave_sem,
):
    pairs, lats, he = le_ref.shape
    ho = lo_ref.shape[2]
    groups = pairs // ROWS

    def odd_copies(g):
        at = pl.ds(pl.multiple_of(g * ROWS, ROWS), ROWS)
        return (
            pltpu.make_async_copy(lo_hbm.at[at], lo_ref.at[at], sems.at[0, g]),
            pltpu.make_async_copy(so_hbm.at[at], so_ref.at[at], sems.at[1, g]),
        )

    def even_copies(g):
        at = pl.ds(pl.multiple_of(g * ROWS, ROWS), ROWS)
        return (
            pltpu.make_async_copy(le_hbm.at[at], le_ref.at[at], sems.at[2, g]),
            pltpu.make_async_copy(se_hbm.at[:, at], se_ref.at[g], sems.at[3, g]),
        )

    wave_copy = pltpu.make_async_copy(waves_hbm, waves_ref, wave_sem)
    wave_copy.start()
    ahead = groups
    for g in range(min(ahead, groups)):
        for copy in odd_copies(g) + even_copies(g):
            copy.start()
    wave_copy.wait()

    ids_e = lax.broadcasted_iota(jnp.int32, (1, he), 1)
    ids_o = lax.broadcasted_iota(jnp.int32, (1, ho), 1)

    def split(panel, ids, count):
        in_low = jnp.where(ids < count, 1.0, 0.0).astype(jnp.bfloat16)
        lower = panel * in_low
        return jnp.concatenate([lower, panel - lower], axis=0)

    def both(panels, spectra):
        rows, width = panels[0].shape[0], spectra[0].shape[1]
        product = jnp.dot(
            jnp.concatenate(panels, axis=0),
            jnp.concatenate(spectra, axis=1),
            preferred_element_type=jnp.float32,
        )
        return product[:rows, :width], product[rows:, width:]

    @pl.loop(0, groups)
    def _(g):
        base = pl.multiple_of(g * ROWS, ROWS)
        for copy in odd_copies(g) + even_copies(g):
            copy.wait()

        @pl.when(g + ahead < groups)
        def _():
            for copy in odd_copies(g + ahead) + even_copies(g + ahead):
                copy.start()

        for p in range(0, ROWS, 2):
            odd = [split(lo_ref[base + q], ids_o, (M - waves_ref[base + q]) // 2) for q in (p, p + 1)]
            anti_ref[p], anti_ref[p + 1] = both(odd, [so_ref[base + p], so_ref[base + p + 1]])
        columns_ref[...] = se_ref[g].astype(jnp.float32).reshape(columns_ref.shape)
        for p in range(0, ROWS, 2):
            lows = [waves_ref[base + q] for q in (p, p + 1)]
            even = [split(le_ref[base + p + i], ids_e, (M - low + 1) // 2) for i, low in enumerate(lows)]
            xe = [columns_ref[pl.ds(q, he, stride=ROWS), :].astype(jnp.bfloat16) for q in (p, p + 1)]
            for i, (low, sym) in enumerate(zip(lows, both(even, xe))):
                parity = low % 2
                anti = anti_ref[p + i]
                for h, rows in enumerate((sym + anti, sym - anti)):
                    for w in range(2):
                        start = (parity ^ w) * (lats * pairs) + base + p + i
                        out_ref[h, pl.ds(start, lats, stride=pairs), :] = rows[w * lats : (w + 1) * lats]


def in_hbm(x):
    return pltpu.with_memory_space_constraint(x, pltpu.HBM)


def in_vmem(x):
    return pltpu.with_memory_space_constraint(x, pltpu.VMEM)


def legendre_stage(waves, spectra_even, spectra_odd, legendre_even, legendre_odd):
    pairs, he, width = spectra_even.shape
    ho = spectra_odd.shape[1]
    lats = legendre_even.shape[1]
    by_column = jnp.transpose(spectra_even, (1, 0, 2))
    operands = (waves, by_column, spectra_odd, legendre_even, legendre_odd)
    return pl.pallas_call(
        legendre_kernel,
        out_shape=pltpu.VMEM((2, 2 * lats * pairs, width), jnp.float32),
        in_specs=[pl.BlockSpec(memory_space=pl.ANY)] * 5,
        out_specs=pl.BlockSpec(memory_space=pltpu.VMEM),
        scratch_shapes=[
            pltpu.SMEM((pairs,), jnp.int32),
            pltpu.VMEM((pairs // ROWS, he, ROWS, width), jnp.bfloat16),
            pltpu.VMEM((pairs, ho, width), jnp.bfloat16),
            pltpu.VMEM((pairs, lats, he), jnp.bfloat16),
            pltpu.VMEM((pairs, lats, ho), jnp.bfloat16),
            pltpu.VMEM((he * ROWS, width), jnp.float32),
            pltpu.VMEM((ROWS, 2 * lats, width), jnp.float32),
            pltpu.SemaphoreType.DMA((4, pairs // ROWS)),
            pltpu.SemaphoreType.DMA,
        ],
        compiler_params=pltpu.CompilerParams(vmem_limit_bytes=40 * 1024 * 1024),
        cost_estimate=pl.CostEstimate(
            flops=4 * pairs * lats * 2 * (he + ho) * width,
            bytes_accessed=2 * pairs * (he + ho) * (width + lats),
            transcendentals=0,
        ),
        name="legendre",
    )(*(in_hbm(x) for x in operands))


def pick_kernel(bands_ref, rows_ref, out_hbm, out_ref, sems):
    lats, _, _, pairs, _ = out_ref.shape
    piece = lats // sems.shape[0]

    def store(i):
        at = pl.ds(i * piece, piece)
        return pltpu.make_async_copy(out_ref.at[at], out_hbm.at[at], sems.at[i])

    def emit(slot, carry):
        band = bands_ref[slot]
        for h in range(2):
            for w in range(2):
                start = pl.multiple_of((w * lats + band) * pairs, ROWS)
                out_ref[slot, h, w] = rows_ref[h, pl.ds(start, pairs), :].astype(jnp.bfloat16)
        return carry

    for i in range(sems.shape[0]):
        lax.fori_loop(i * piece, (i + 1) * piece, emit, 0, unroll=4)
        store(i).start()
    for i in range(sems.shape[0]):
        store(i).wait()


def pick_latitudes(bands, rows, pairs):
    lats = bands.shape[0]
    width = rows.shape[2]
    shape = (lats, 2, 2, pairs, width)
    return pl.pallas_call(
        pick_kernel,
        out_shape=pltpu.HBM(shape, jnp.bfloat16),
        grid_spec=pltpu.PrefetchScalarGridSpec(
            num_scalar_prefetch=1,
            grid=(),
            in_specs=[pl.BlockSpec(memory_space=pltpu.VMEM)],
            out_specs=pl.BlockSpec(memory_space=pl.ANY),
            scratch_shapes=[pltpu.VMEM(shape, jnp.bfloat16), pltpu.SemaphoreType.DMA((4,))],
        ),
        compiler_params=pltpu.CompilerParams(vmem_limit_bytes=16 * 1024 * 1024),
        name="pick",
    )(bands, in_vmem(rows))


def even_wave(low):
    return jnp.where(low % 2 == 0, low, M - 1 - low)


def table_part(w, i, first_ref, second_ref, rest_ref):
    if i == 0:
        return first_ref.at[w]
    return second_ref if (w, i) == (0, 1) else rest_ref.at[2 * i + w - 3]


def table_kernel(waves_ref, first_ref, second_ref, rest_ref):
    even = even_wave(waves_ref[...])
    odd = M - 1 - even
    lane = lax.broadcasted_iota(jnp.int32, even.shape, 1).astype(jnp.float32)
    unit = 2.0 * math.pi / NLON

    def angle(product):
        turns = jnp.floor(product * (1.0 / NLON))
        return (product - turns * NLON) * unit

    for w, wave in enumerate((even, odd)):
        number = wave.astype(jnp.float32)
        factor = jnp.where(wave == 0, 1.0, 2.0)
        start = angle(number * lane)
        step = angle(number * LANES)
        c, s = factor * jnp.cos(start), -factor * jnp.sin(start)
        dc, ds = jnp.cos(step), jnp.sin(step)
        for b in range(0, QUARTER, LANES):
            at = slice(b % CHUNK, b % CHUNK + LANES)
            out_ref = table_part(w, b // CHUNK, first_ref, second_ref, rest_ref)
            out_ref[0, :, at] = c.astype(jnp.bfloat16)
            out_ref[1, :, at] = s.astype(jnp.bfloat16)
            c, s = c * dc + s * ds, s * dc - c * ds


def wave_tables(waves):
    total = waves.shape[0]
    rows = 64
    rest = 2 * pl.cdiv(QUARTER, CHUNK) - 3
    return pl.pallas_call(
        table_kernel,
        out_shape=[
            jax.ShapeDtypeStruct((2, 2, total, CHUNK), jnp.bfloat16),
            jax.ShapeDtypeStruct((2, total, CHUNK), jnp.bfloat16),
            pltpu.HBM((rest, 2, total, CHUNK), jnp.bfloat16),
        ],
        grid=(total // rows,),
        in_specs=[pl.BlockSpec((rows, LANES), lambda i: (i, 0))],
        out_specs=[
            pl.BlockSpec((2, 2, rows, CHUNK), lambda i: (0, 0, i, 0)),
            pl.BlockSpec((2, rows, CHUNK), lambda i: (0, i, 0)),
            pl.BlockSpec((rest, 2, rows, CHUNK), lambda i: (0, 0, i, 0)),
        ],
        compiler_params=pltpu.CompilerParams(vmem_limit_bytes=16 * 1024 * 1024),
        cost_estimate=pl.CostEstimate(
            flops=16 * total * QUARTER, bytes_accessed=8 * total * QUARTER, transcendentals=8 * total * LANES
        ),
        name="tables",
    )(jnp.broadcast_to(waves[:, None], (total, LANES)))


def fourier_kernel(
    arrived_ref, first_ref, second_ref, rest_hbm, sign_hbm, out_hbm,
    left_ref, rest_ref, sign_ref, row_ref, sems, sign_sem, out_sems,
):
    devices, slots, _, _, pairs, width = arrived_ref.shape
    fields = width // 2
    total = devices * pairs
    chunks = (rest_ref.shape[0] + 3) // 2
    rows = 2 * fields

    def load(i):
        return pltpu.make_async_copy(rest_hbm.at[i], rest_ref.at[i], sems.at[i])

    def block(s, i):
        lo, hi = i * CHUNK, min((i + 1) * CHUNK, QUARTER)
        e, o = [
            jnp.dot(
                left_ref[s, w],
                table_part(w, i, first_ref, second_ref, rest_ref)[...].reshape(2 * total, CHUNK),
                preferred_element_type=jnp.float32,
            )[:, : hi - lo]
            for w in range(2)
        ]
        plus, minus = e + o, e - o
        for k, part in enumerate((plus[:rows], plus[rows:], minus[:rows], minus[rows:])):
            at = slice(k * QUARTER + lo, k * QUARTER + hi)
            row_ref[s * rows : (s + 1) * rows, at] = part.astype(jnp.bfloat16)

    sign_copy = pltpu.make_async_copy(sign_hbm, sign_ref, sign_sem)
    sign_copy.start()
    for i in range(rest_ref.shape[0]):
        load(i).start()

    stores = []
    for s in range(slots):
        turned = []
        for h in range(2):
            for w in range(2):
                x = jnp.concatenate([arrived_ref[d, s, h, w] for d in range(devices)], axis=0)
                xt = x.T
                at = slice(h * fields, (h + 1) * fields)
                left_ref[s, w, at, :total] = xt[:fields]
                left_ref[s, w, at, total:] = xt[fields:]
                turned.append((h, w, xt))
        if s == 0:
            sign_copy.wait()
        sign = sign_ref[0:1, :]
        for h, w, xt in turned:
            at = slice(rows + h * fields, rows + (h + 1) * fields)
            signed = (xt.astype(jnp.float32) * sign).astype(jnp.bfloat16)
            re, im = signed[:fields], signed[fields:]
            left_ref[s, w, at, :total] = im if w else re
            left_ref[s, w, at, total:] = -re if w else im
        if s == 0:
            block(s, 0)
    for i in range(rest_ref.shape[0]):
        load(i).wait()
    for s in range(slots):
        for i in range(s == 0, chunks):
            block(s, i)
        base = slice(s * rows, (s + 1) * rows)
        copy = pltpu.make_async_copy(row_ref.at[base], out_hbm.at[base], out_sems.at[s])
        copy.start()
        stores.append(copy)
    for copy in stores:
        copy.wait()


def fourier_stage(arrived, sign, first, second, rest):
    devices, slots, _, _, pairs, width = arrived.shape
    fields = width // 2
    total = devices * pairs
    rows = slots * 2 * fields
    out = pl.pallas_call(
        fourier_kernel,
        out_shape=jax.ShapeDtypeStruct((rows, NLON), jnp.bfloat16),
        in_specs=[pl.BlockSpec(memory_space=pltpu.VMEM)] * 3 + [pl.BlockSpec(memory_space=pl.ANY)] * 2,
        out_specs=pl.BlockSpec(memory_space=pl.ANY),
        scratch_shapes=[
            pltpu.VMEM((slots, 2, 4 * fields, 2 * total), jnp.bfloat16),
            pltpu.VMEM(rest.shape, jnp.bfloat16),
            pltpu.VMEM(sign.shape, jnp.float32),
            pltpu.VMEM((rows, NLON), jnp.bfloat16),
            pltpu.SemaphoreType.DMA((rest.shape[0],)),
            pltpu.SemaphoreType.DMA,
            pltpu.SemaphoreType.DMA((slots,)),
        ],
        compiler_params=pltpu.CompilerParams(vmem_limit_bytes=16 * 1024 * 1024),
        cost_estimate=pl.CostEstimate(
            flops=16 * rows * total * QUARTER, bytes_accessed=8 * total * QUARTER, transcendentals=0
        ),
        name="fourier",
    )(arrived, first, second, in_hbm(rest), in_hbm(sign))
    return out.reshape(slots, 2, fields, NLON)


def on_device(wave_pairs, band_owner, spectra_even, spectra_odd, legendre_even, legendre_odd):
    devices = lax.axis_size("wave")
    pairs = round_up(wave_pairs.shape[0], ROWS)
    extra = pairs - wave_pairs.shape[0]
    slots = band_owner.shape[0]
    width = spectra_even.shape[2]
    if extra:
        wave_pairs = jnp.pad(wave_pairs, (0, extra))
        spectra_even, spectra_odd, legendre_even, legendre_odd = (
            jnp.pad(a, ((0, extra), (0, 0), (0, 0)))
            for a in (spectra_even, spectra_odd, legendre_even, legendre_odd)
        )

    rest = round_up(pairs + slots, LANES) - pairs - slots
    own = jnp.concatenate([wave_pairs, band_owner, jnp.zeros(rest, jnp.int32)])
    own = jnp.broadcast_to(own, (devices, 1) + own.shape)
    index = lax.all_to_all(own, "wave", 0, 0, tiled=True)[:, 0]
    all_bands = index[:, pairs : pairs + slots].reshape(-1)
    rows = legendre_stage(wave_pairs, spectra_even, spectra_odd, legendre_even, legendre_odd)
    picked = pick_latitudes(all_bands, rows, pairs)
    index, picked = lax.optimization_barrier((index, picked))
    arrived = lax.all_to_all(picked.reshape(devices, slots, 2, 2, pairs, width), "wave", 0, 0, tiled=True)
    all_pairs = index[:, :pairs].reshape(-1)
    sign = jnp.where(even_wave(all_pairs) % 4 == 0, 1.0, -1.0).astype(jnp.float32)
    sign, all_pairs = lax.optimization_barrier((jnp.broadcast_to(sign, (ROWS,) + sign.shape), all_pairs))
    return fourier_stage(arrived, sign, *wave_tables(all_pairs))


def solution(mesh):
    return jax.shard_map(
        on_device,
        mesh=mesh,
        in_specs=(
            P("wave"),
            P("wave"),
            P("wave", None, "grp"),
            P("wave", None, "grp"),
            P("wave", None, None),
            P("wave", None, None),
        ),
        out_specs=P("wave", None, "grp", None),
        check_vma=False,
    )
```

```python
import functools
import math

import jax
import jax.numpy as jnp
from jax import lax
from jax.experimental import pallas as pl
from jax.experimental.pallas import tpu as pltpu
from jax.sharding import PartitionSpec as P

M = 1280
NLON = 2688
QUARTER = NLON // 4
CHUNK = 256
ROWS = 8
LANES = 128


def round_up(value, unit):
    return -(-value // unit) * unit


def legendre_kernel(
    waves_hbm, se_hbm, so_hbm, le_hbm, lo_hbm, out_ref,
    waves_ref, se_ref, so_ref, le_ref, lo_ref, columns_ref, anti_ref, sems, wave_sem,
):
    pairs, lats, he = le_ref.shape
    ho = lo_ref.shape[2]
    groups = pairs // ROWS

    def odd_copies(g):
        at = pl.ds(pl.multiple_of(g * ROWS, ROWS), ROWS)
        return (
            pltpu.make_async_copy(lo_hbm.at[at], lo_ref.at[at], sems.at[0, g]),
            pltpu.make_async_copy(so_hbm.at[at], so_ref.at[at], sems.at[1, g]),
        )

    def even_copies(g):
        at = pl.ds(pl.multiple_of(g * ROWS, ROWS), ROWS)
        return (
            pltpu.make_async_copy(le_hbm.at[at], le_ref.at[at], sems.at[2, g]),
            pltpu.make_async_copy(se_hbm.at[:, at], se_ref.at[g], sems.at[3, g]),
        )

    wave_copy = pltpu.make_async_copy(waves_hbm, waves_ref, wave_sem)
    wave_copy.start()
    ahead = 3
    for g in range(min(ahead, groups)):
        for copy in odd_copies(g) + even_copies(g):
            copy.start()
    wave_copy.wait()

    ids_e = lax.broadcasted_iota(jnp.int32, (1, he), 1)
    ids_o = lax.broadcasted_iota(jnp.int32, (1, ho), 1)

    def split(panel, ids, count):
        in_low = jnp.where(ids < count, 1.0, 0.0).astype(jnp.bfloat16)
        lower = panel * in_low
        return jnp.concatenate([lower, panel - lower], axis=0)

    def both(panels, spectra):
        rows, width = panels[0].shape[0], spectra[0].shape[1]
        product = jnp.dot(
            jnp.concatenate(panels, axis=0),
            jnp.concatenate(spectra, axis=1),
            preferred_element_type=jnp.float32,
        )
        return product[:rows, :width], product[rows:, width:]

    @pl.loop(0, groups)
    def _(g):
        base = pl.multiple_of(g * ROWS, ROWS)
        for copy in odd_copies(g) + even_copies(g):
            copy.wait()

        @pl.when(g + ahead < groups)
        def _():
            for copy in odd_copies(g + ahead) + even_copies(g + ahead):
                copy.start()

        for p in range(0, ROWS, 2):
            odd = [split(lo_ref[base + q], ids_o, (M - waves_ref[base + q]) // 2) for q in (p, p + 1)]
            anti_ref[p], anti_ref[p + 1] = both(odd, [so_ref[base + p], so_ref[base + p + 1]])
        columns_ref[...] = se_ref[g].astype(jnp.float32).reshape(columns_ref.shape)
        for p in range(0, ROWS, 2):
            lows = [waves_ref[base + q] for q in (p, p + 1)]
            even = [split(le_ref[base + p + i], ids_e, (M - low + 1) // 2) for i, low in enumerate(lows)]
            xe = [columns_ref[pl.ds(q, he, stride=ROWS), :].astype(jnp.bfloat16) for q in (p, p + 1)]
            for i, (low, sym) in enumerate(zip(lows, both(even, xe))):
                parity = low % 2
                anti = anti_ref[p + i]
                for h, rows in enumerate((sym + anti, sym - anti)):
                    for w in range(2):
                        start = (parity ^ w) * (lats * pairs) + base + p + i
                        out_ref[h, pl.ds(start, lats, stride=pairs), :] = rows[w * lats : (w + 1) * lats]


def in_hbm(x):
    return pltpu.with_memory_space_constraint(x, pltpu.HBM)


def in_vmem(x):
    return pltpu.with_memory_space_constraint(x, pltpu.VMEM)


def legendre_stage(waves, spectra_even, spectra_odd, legendre_even, legendre_odd):
    pairs, he, width = spectra_even.shape
    ho = spectra_odd.shape[1]
    lats = legendre_even.shape[1]
    by_column = jnp.transpose(spectra_even, (1, 0, 2))
    operands = (waves, by_column, spectra_odd, legendre_even, legendre_odd)
    return pl.pallas_call(
        legendre_kernel,
        out_shape=pltpu.VMEM((2, 2 * lats * pairs, width), jnp.float32),
        in_specs=[pl.BlockSpec(memory_space=pl.ANY)] * 5,
        out_specs=pl.BlockSpec(memory_space=pltpu.VMEM),
        scratch_shapes=[
            pltpu.SMEM((pairs,), jnp.int32),
            pltpu.VMEM((pairs // ROWS, he, ROWS, width), jnp.bfloat16),
            pltpu.VMEM((pairs, ho, width), jnp.bfloat16),
            pltpu.VMEM((pairs, lats, he), jnp.bfloat16),
            pltpu.VMEM((pairs, lats, ho), jnp.bfloat16),
            pltpu.VMEM((he * ROWS, width), jnp.float32),
            pltpu.VMEM((ROWS, 2 * lats, width), jnp.float32),
            pltpu.SemaphoreType.DMA((4, pairs // ROWS)),
            pltpu.SemaphoreType.DMA,
        ],
        compiler_params=pltpu.CompilerParams(vmem_limit_bytes=40 * 1024 * 1024),
        cost_estimate=pl.CostEstimate(
            flops=4 * pairs * lats * 2 * (he + ho) * width,
            bytes_accessed=2 * pairs * (he + ho) * (width + lats),
            transcendentals=0,
        ),
        name="legendre",
    )(*(in_hbm(x) for x in operands))


def pick_kernel(bands_ref, rows_ref, out_hbm, out_ref, sems):
    lats, _, _, pairs, _ = out_ref.shape
    piece = lats // sems.shape[0]

    def store(i):
        at = pl.ds(i * piece, piece)
        return pltpu.make_async_copy(out_ref.at[at], out_hbm.at[at], sems.at[i])

    def emit(slot, carry):
        band = bands_ref[slot]
        for h in range(2):
            for w in range(2):
                start = pl.multiple_of((w * lats + band) * pairs, ROWS)
                out_ref[slot, h, w] = rows_ref[h, pl.ds(start, pairs), :].astype(jnp.bfloat16)
        return carry

    for i in range(sems.shape[0]):
        lax.fori_loop(i * piece, (i + 1) * piece, emit, 0, unroll=8)
        store(i).start()
    for i in range(sems.shape[0]):
        store(i).wait()


def pick_latitudes(bands, rows, pairs):
    lats = bands.shape[0]
    width = rows.shape[2]
    shape = (lats, 2, 2, pairs, width)
    return pl.pallas_call(
        pick_kernel,
        out_shape=pltpu.HBM(shape, jnp.bfloat16),
        grid_spec=pltpu.PrefetchScalarGridSpec(
            num_scalar_prefetch=1,
            grid=(),
            in_specs=[pl.BlockSpec(memory_space=pltpu.VMEM)],
            out_specs=pl.BlockSpec(memory_space=pl.ANY),
            scratch_shapes=[pltpu.VMEM(shape, jnp.bfloat16), pltpu.SemaphoreType.DMA((4,))],
        ),
        compiler_params=pltpu.CompilerParams(vmem_limit_bytes=16 * 1024 * 1024),
        name="pick",
    )(bands, in_vmem(rows))


def even_wave(low):
    return jnp.where(low % 2 == 0, low, M - 1 - low)


def table_part(w, i, first_ref, second_ref, rest_ref):
    if i == 0:
        return first_ref.at[w]
    return second_ref if (w, i) == (0, 1) else rest_ref.at[2 * i + w - 3]


def table_kernel(waves_ref, first_ref, second_ref, rest_ref):
    even = even_wave(waves_ref[...])
    odd = M - 1 - even
    lane = lax.broadcasted_iota(jnp.int32, even.shape, 1).astype(jnp.float32)
    unit = 2.0 * math.pi / NLON

    def angle(product):
        turns = jnp.floor(product * (1.0 / NLON))
        return (product - turns * NLON) * unit

    for w, wave in enumerate((even, odd)):
        number = wave.astype(jnp.float32)
        factor = jnp.where(wave == 0, 1.0, 2.0)
        start = angle(number * lane)
        step = angle(number * LANES)
        c, s = factor * jnp.cos(start), -factor * jnp.sin(start)
        dc, ds = jnp.cos(step), jnp.sin(step)
        for b in range(0, QUARTER, LANES):
            at = slice(b % CHUNK, b % CHUNK + LANES)
            out_ref = table_part(w, b // CHUNK, first_ref, second_ref, rest_ref)
            out_ref[0, :, at] = c.astype(jnp.bfloat16)
            out_ref[1, :, at] = s.astype(jnp.bfloat16)
            c, s = c * dc + s * ds, s * dc - c * ds


def wave_tables(waves):
    total = waves.shape[0]
    rows = 64
    rest = 2 * pl.cdiv(QUARTER, CHUNK) - 3
    return pl.pallas_call(
        table_kernel,
        out_shape=[
            jax.ShapeDtypeStruct((2, 2, total, CHUNK), jnp.bfloat16),
            jax.ShapeDtypeStruct((2, total, CHUNK), jnp.bfloat16),
            pltpu.HBM((rest, 2, total, CHUNK), jnp.bfloat16),
        ],
        grid=(total // rows,),
        in_specs=[pl.BlockSpec((rows, LANES), lambda i: (i, 0))],
        out_specs=[
            pl.BlockSpec((2, 2, rows, CHUNK), lambda i: (0, 0, i, 0)),
            pl.BlockSpec((2, rows, CHUNK), lambda i: (0, i, 0)),
            pl.BlockSpec((rest, 2, rows, CHUNK), lambda i: (0, 0, i, 0)),
        ],
        compiler_params=pltpu.CompilerParams(vmem_limit_bytes=16 * 1024 * 1024),
        cost_estimate=pl.CostEstimate(
            flops=16 * total * QUARTER, bytes_accessed=8 * total * QUARTER, transcendentals=8 * total * LANES
        ),
        name="tables",
    )(jnp.broadcast_to(waves[:, None], (total, LANES)))


def fourier_kernel(
    arrived_ref, first_ref, second_ref, rest_hbm, sign_hbm, out_hbm,
    left_ref, rest_ref, sign_ref, row_ref, sems, sign_sem, out_sems,
):
    devices, slots, _, _, pairs, width = arrived_ref.shape
    fields = width // 2
    total = devices * pairs
    chunks = (rest_ref.shape[0] + 3) // 2
    rows = 2 * fields

    def load(i):
        return pltpu.make_async_copy(rest_hbm.at[i], rest_ref.at[i], sems.at[i])

    def block(s, i):
        lo, hi = i * CHUNK, min((i + 1) * CHUNK, QUARTER)
        e, o = [
            jnp.dot(
                left_ref[s, w],
                table_part(w, i, first_ref, second_ref, rest_ref)[...].reshape(2 * total, CHUNK),
                preferred_element_type=jnp.float32,
            )[:, : hi - lo]
            for w in range(2)
        ]
        plus, minus = e + o, e - o
        for k, part in enumerate((plus[:rows], plus[rows:], minus[:rows], minus[rows:])):
            at = slice(k * QUARTER + lo, k * QUARTER + hi)
            row_ref[s * rows : (s + 1) * rows, at] = part.astype(jnp.bfloat16)

    sign_copy = pltpu.make_async_copy(sign_hbm, sign_ref, sign_sem)
    sign_copy.start()
    for i in range(rest_ref.shape[0]):
        load(i).start()

    stores = []
    for s in range(slots):
        turned = []
        for h in range(2):
            for w in range(2):
                x = jnp.concatenate([arrived_ref[d, s, h, w] for d in range(devices)], axis=0)
                xt = x.T
                at = slice(h * fields, (h + 1) * fields)
                left_ref[s, w, at, :total] = xt[:fields]
                left_ref[s, w, at, total:] = xt[fields:]
                turned.append((h, w, xt))
        if s == 0:
            sign_copy.wait()
        sign = sign_ref[0:1, :]
        for h, w, xt in turned:
            at = slice(rows + h * fields, rows + (h + 1) * fields)
            signed = (xt.astype(jnp.float32) * sign).astype(jnp.bfloat16)
            re, im = signed[:fields], signed[fields:]
            left_ref[s, w, at, :total] = im if w else re
            left_ref[s, w, at, total:] = -re if w else im
        if s == 0:
            block(s, 0)
    for i in range(rest_ref.shape[0]):
        load(i).wait()
    for s in range(slots):
        for i in range(s == 0, chunks):
            block(s, i)
        base = slice(s * rows, (s + 1) * rows)
        copy = pltpu.make_async_copy(row_ref.at[base], out_hbm.at[base], out_sems.at[s])
        copy.start()
        stores.append(copy)
    for copy in stores:
        copy.wait()


def fourier_stage(arrived, sign, first, second, rest):
    devices, slots, _, _, pairs, width = arrived.shape
    fields = width // 2
    total = devices * pairs
    rows = slots * 2 * fields
    out = pl.pallas_call(
        fourier_kernel,
        out_shape=jax.ShapeDtypeStruct((rows, NLON), jnp.bfloat16),
        in_specs=[pl.BlockSpec(memory_space=pltpu.VMEM)] * 3 + [pl.BlockSpec(memory_space=pl.ANY)] * 2,
        out_specs=pl.BlockSpec(memory_space=pl.ANY),
        scratch_shapes=[
            pltpu.VMEM((slots, 2, 4 * fields, 2 * total), jnp.bfloat16),
            pltpu.VMEM(rest.shape, jnp.bfloat16),
            pltpu.VMEM(sign.shape, jnp.float32),
            pltpu.VMEM((rows, NLON), jnp.bfloat16),
            pltpu.SemaphoreType.DMA((rest.shape[0],)),
            pltpu.SemaphoreType.DMA,
            pltpu.SemaphoreType.DMA((slots,)),
        ],
        compiler_params=pltpu.CompilerParams(vmem_limit_bytes=16 * 1024 * 1024),
        cost_estimate=pl.CostEstimate(
            flops=16 * rows * total * QUARTER, bytes_accessed=8 * total * QUARTER, transcendentals=0
        ),
        name="fourier",
    )(arrived, first, second, in_hbm(rest), in_hbm(sign))
    return out.reshape(slots, 2, fields, NLON)


def on_device(wave_pairs, band_owner, spectra_even, spectra_odd, legendre_even, legendre_odd):
    devices = lax.axis_size("wave")
    pairs = round_up(wave_pairs.shape[0], ROWS)
    extra = pairs - wave_pairs.shape[0]
    slots = band_owner.shape[0]
    width = spectra_even.shape[2]
    if extra:
        wave_pairs = jnp.pad(wave_pairs, (0, extra))
        spectra_even, spectra_odd, legendre_even, legendre_odd = (
            jnp.pad(a, ((0, extra), (0, 0), (0, 0)))
            for a in (spectra_even, spectra_odd, legendre_even, legendre_odd)
        )

    rest = round_up(pairs + slots, LANES) - pairs - slots
    own = jnp.concatenate([wave_pairs, band_owner, jnp.zeros(rest, jnp.int32)])
    own = jnp.broadcast_to(own, (devices, 1) + own.shape)
    index = lax.all_to_all(own, "wave", 0, 0, tiled=True)[:, 0]
    all_bands = index[:, pairs : pairs + slots].reshape(-1)
    rows = legendre_stage(wave_pairs, spectra_even, spectra_odd, legendre_even, legendre_odd)
    picked = pick_latitudes(all_bands, rows, pairs)
    index, picked = lax.optimization_barrier((index, picked))
    arrived = lax.all_to_all(picked.reshape(devices, slots, 2, 2, pairs, width), "wave", 0, 0, tiled=True)
    all_pairs = index[:, :pairs].reshape(-1)
    sign = jnp.where(even_wave(all_pairs) % 4 == 0, 1.0, -1.0).astype(jnp.float32)
    sign, all_pairs = lax.optimization_barrier((jnp.broadcast_to(sign, (ROWS,) + sign.shape), all_pairs))
    return fourier_stage(arrived, sign, *wave_tables(all_pairs))


def solution(mesh):
    return jax.shard_map(
        on_device,
        mesh=mesh,
        in_specs=(
            P("wave"),
            P("wave"),
            P("wave", None, "grp"),
            P("wave", None, "grp"),
            P("wave", None, None),
            P("wave", None, None),
        ),
        out_specs=P("wave", None, "grp", None),
        check_vma=False,
    )
```

```python
import functools
import math

import jax
import jax.numpy as jnp
from jax import lax
from jax.experimental import pallas as pl
from jax.experimental.pallas import tpu as pltpu
from jax.sharding import PartitionSpec as P

M = 1280
NLON = 2688
QUARTER = NLON // 4
CHUNK = 256
ROWS = 8
LANES = 128


def round_up(value, unit):
    return -(-value // unit) * unit


def legendre_kernel(
    waves_hbm, se_hbm, so_hbm, le_hbm, lo_hbm, out_ref,
    waves_ref, se_ref, so_ref, le_ref, lo_ref, columns_ref, anti_ref, sems, wave_sem,
):
    pairs, lats, he = le_ref.shape
    ho = lo_ref.shape[2]
    groups = pairs // ROWS

    def odd_copies(g):
        at = pl.ds(pl.multiple_of(g * ROWS, ROWS), ROWS)
        return (
            pltpu.make_async_copy(lo_hbm.at[at], lo_ref.at[at], sems.at[0, g]),
            pltpu.make_async_copy(so_hbm.at[at], so_ref.at[at], sems.at[1, g]),
        )

    def even_copies(g):
        at = pl.ds(pl.multiple_of(g * ROWS, ROWS), ROWS)
        return (
            pltpu.make_async_copy(le_hbm.at[at], le_ref.at[at], sems.at[2, g]),
            pltpu.make_async_copy(se_hbm.at[:, at], se_ref.at[g], sems.at[3, g]),
        )

    wave_copy = pltpu.make_async_copy(waves_hbm, waves_ref, wave_sem)
    wave_copy.start()
    ahead = 3
    for g in range(min(ahead, groups)):
        for copy in odd_copies(g) + even_copies(g):
            copy.start()
    wave_copy.wait()

    ids_e = lax.broadcasted_iota(jnp.int32, (1, he), 1)
    ids_o = lax.broadcasted_iota(jnp.int32, (1, ho), 1)

    def split(panel, ids, count):
        in_low = jnp.where(ids < count, 1.0, 0.0).astype(jnp.bfloat16)
        lower = panel * in_low
        return jnp.concatenate([lower, panel - lower], axis=0)

    def both(panels, spectra):
        rows, width = panels[0].shape[0], spectra[0].shape[1]
        product = jnp.dot(
            jnp.concatenate(panels, axis=0),
            jnp.concatenate(spectra, axis=1),
            preferred_element_type=jnp.float32,
        )
        return product[:rows, :width], product[rows:, width:]

    @pl.loop(0, groups)
    def _(g):
        base = pl.multiple_of(g * ROWS, ROWS)
        for copy in odd_copies(g) + even_copies(g):
            copy.wait()

        @pl.when(g + ahead < groups)
        def _():
            for copy in odd_copies(g + ahead) + even_copies(g + ahead):
                copy.start()

        for p in range(0, ROWS, 2):
            odd = [split(lo_ref[base + q], ids_o, (M - waves_ref[base + q]) // 2) for q in (p, p + 1)]
            anti_ref[p], anti_ref[p + 1] = both(odd, [so_ref[base + p], so_ref[base + p + 1]])
        columns_ref[...] = se_ref[g].astype(jnp.float32).reshape(columns_ref.shape)
        for p in range(0, ROWS, 2):
            lows = [waves_ref[base + q] for q in (p, p + 1)]
            even = [split(le_ref[base + p + i], ids_e, (M - low + 1) // 2) for i, low in enumerate(lows)]
            xe = [columns_ref[pl.ds(q, he, stride=ROWS), :].astype(jnp.bfloat16) for q in (p, p + 1)]
            for i, (low, sym) in enumerate(zip(lows, both(even, xe))):
                parity = low % 2
                anti = anti_ref[p + i]
                for h, rows in enumerate((sym + anti, sym - anti)):
                    for w in range(2):
                        start = (parity ^ w) * (lats * pairs) + base + p + i
                        out_ref[h, pl.ds(start, lats, stride=pairs), :] = rows[w * lats : (w + 1) * lats]


def in_hbm(x):
    return pltpu.with_memory_space_constraint(x, pltpu.HBM)


def in_vmem(x):
    return pltpu.with_memory_space_constraint(x, pltpu.VMEM)


def legendre_stage(waves, spectra_even, spectra_odd, legendre_even, legendre_odd):
    pairs, he, width = spectra_even.shape
    ho = spectra_odd.shape[1]
    lats = legendre_even.shape[1]
    by_column = jnp.transpose(spectra_even, (1, 0, 2))
    operands = (waves, by_column, spectra_odd, legendre_even, legendre_odd)
    return pl.pallas_call(
        legendre_kernel,
        out_shape=pltpu.VMEM((2, 2 * lats * pairs, width), jnp.float32),
        in_specs=[pl.BlockSpec(memory_space=pl.ANY)] * 5,
        out_specs=pl.BlockSpec(memory_space=pltpu.VMEM),
        scratch_shapes=[
            pltpu.SMEM((pairs,), jnp.int32),
            pltpu.VMEM((pairs // ROWS, he, ROWS, width), jnp.bfloat16),
            pltpu.VMEM((pairs, ho, width), jnp.bfloat16),
            pltpu.VMEM((pairs, lats, he), jnp.bfloat16),
            pltpu.VMEM((pairs, lats, ho), jnp.bfloat16),
            pltpu.VMEM((he * ROWS, width), jnp.float32),
            pltpu.VMEM((ROWS, 2 * lats, width), jnp.float32),
            pltpu.SemaphoreType.DMA((4, pairs // ROWS)),
            pltpu.SemaphoreType.DMA,
        ],
        compiler_params=pltpu.CompilerParams(vmem_limit_bytes=40 * 1024 * 1024),
        cost_estimate=pl.CostEstimate(
            flops=4 * pairs * lats * 2 * (he + ho) * width,
            bytes_accessed=2 * pairs * (he + ho) * (width + lats),
            transcendentals=0,
        ),
        name="legendre",
    )(*(in_hbm(x) for x in operands))


def pick_kernel(column, index_ref, rows_ref, out_hbm, out_ref, sems):
    lats, _, _, pairs, _ = out_ref.shape
    piece = lats // sems.shape[0]
    slots = lats // index_ref.shape[0]

    def store(i):
        at = pl.ds(i * piece, piece)
        return pltpu.make_async_copy(out_ref.at[at], out_hbm.at[at], sems.at[i])

    def emit(slot, carry):
        band = index_ref[slot // slots, column + slot % slots]
        for h in range(2):
            for w in range(2):
                start = pl.multiple_of((w * lats + band) * pairs, ROWS)
                out_ref[slot, h, w] = rows_ref[h, pl.ds(start, pairs), :].astype(jnp.bfloat16)
        return carry

    for i in range(sems.shape[0]):
        lax.fori_loop(i * piece, (i + 1) * piece, emit, 0, unroll=8)
        store(i).start()
    for i in range(sems.shape[0]):
        store(i).wait()


def pick_latitudes(index, rows, lats, pairs):
    width = rows.shape[2]
    shape = (lats, 2, 2, pairs, width)
    return pl.pallas_call(
        functools.partial(pick_kernel, pairs),
        out_shape=pltpu.HBM(shape, jnp.bfloat16),
        grid_spec=pltpu.PrefetchScalarGridSpec(
            num_scalar_prefetch=1,
            grid=(),
            in_specs=[pl.BlockSpec(memory_space=pltpu.VMEM)],
            out_specs=pl.BlockSpec(memory_space=pl.ANY),
            scratch_shapes=[pltpu.VMEM(shape, jnp.bfloat16), pltpu.SemaphoreType.DMA((4,))],
        ),
        compiler_params=pltpu.CompilerParams(vmem_limit_bytes=16 * 1024 * 1024),
        name="pick",
    )(index, in_vmem(rows))


def even_wave(low):
    return jnp.where(low % 2 == 0, low, M - 1 - low)


def table_part(w, i, first_ref, second_ref, rest_ref):
    if i == 0:
        return first_ref.at[w]
    return second_ref if (w, i) == (0, 1) else rest_ref.at[2 * i + w - 3]


def table_kernel(waves_ref, first_ref, second_ref, rest_ref):
    even = even_wave(waves_ref[...])
    odd = M - 1 - even
    lane = lax.broadcasted_iota(jnp.int32, even.shape, 1).astype(jnp.float32)
    unit = 2.0 * math.pi / NLON

    def angle(product):
        turns = jnp.floor(product * (1.0 / NLON))
        return (product - turns * NLON) * unit

    for w, wave in enumerate((even, odd)):
        number = wave.astype(jnp.float32)
        factor = jnp.where(wave == 0, 1.0, 2.0)
        start = angle(number * lane)
        step = angle(number * LANES)
        c, s = factor * jnp.cos(start), -factor * jnp.sin(start)
        dc, ds = jnp.cos(step), jnp.sin(step)
        for b in range(0, QUARTER, LANES):
            at = slice(b % CHUNK, b % CHUNK + LANES)
            out_ref = table_part(w, b // CHUNK, first_ref, second_ref, rest_ref)
            out_ref[0, :, at] = c.astype(jnp.bfloat16)
            out_ref[1, :, at] = s.astype(jnp.bfloat16)
            c, s = c * dc + s * ds, s * dc - c * ds


def wave_tables(waves):
    total = waves.shape[0]
    rows = 64
    rest = 2 * pl.cdiv(QUARTER, CHUNK) - 3
    return pl.pallas_call(
        table_kernel,
        out_shape=[
            jax.ShapeDtypeStruct((2, 2, total, CHUNK), jnp.bfloat16),
            jax.ShapeDtypeStruct((2, total, CHUNK), jnp.bfloat16),
            pltpu.HBM((rest, 2, total, CHUNK), jnp.bfloat16),
        ],
        grid=(total // rows,),
        in_specs=[pl.BlockSpec((rows, LANES), lambda i: (i, 0))],
        out_specs=[
            pl.BlockSpec((2, 2, rows, CHUNK), lambda i: (0, 0, i, 0)),
            pl.BlockSpec((2, rows, CHUNK), lambda i: (0, i, 0)),
            pl.BlockSpec((rest, 2, rows, CHUNK), lambda i: (0, 0, i, 0)),
        ],
        compiler_params=pltpu.CompilerParams(vmem_limit_bytes=16 * 1024 * 1024),
        cost_estimate=pl.CostEstimate(
            flops=16 * total * QUARTER, bytes_accessed=8 * total * QUARTER, transcendentals=8 * total * LANES
        ),
        name="tables",
    )(jnp.broadcast_to(waves[:, None], (total, LANES)))


def fourier_kernel(
    arrived_ref, first_ref, second_ref, rest_hbm, sign_hbm, out_hbm,
    left_ref, rest_ref, sign_ref, row_ref, sems, sign_sem, out_sems,
):
    devices, slots, _, _, pairs, width = arrived_ref.shape
    fields = width // 2
    total = devices * pairs
    chunks = (rest_ref.shape[0] + 3) // 2
    rows = 2 * fields

    def load(i):
        return pltpu.make_async_copy(rest_hbm.at[i], rest_ref.at[i], sems.at[i])

    def block(s, i):
        lo, hi = i * CHUNK, min((i + 1) * CHUNK, QUARTER)
        e, o = [
            jnp.dot(
                left_ref[s, w],
                table_part(w, i, first_ref, second_ref, rest_ref)[...].reshape(2 * total, CHUNK),
                preferred_element_type=jnp.float32,
            )[:, : hi - lo]
            for w in range(2)
        ]
        plus, minus = e + o, e - o
        for k, part in enumerate((plus[:rows], plus[rows:], minus[:rows], minus[rows:])):
            at = slice(k * QUARTER + lo, k * QUARTER + hi)
            row_ref[s * rows : (s + 1) * rows, at] = part.astype(jnp.bfloat16)

    sign_copy = pltpu.make_async_copy(sign_hbm, sign_ref, sign_sem)
    sign_copy.start()
    for i in range(rest_ref.shape[0]):
        load(i).start()

    stores = []
    for s in range(slots):
        turned = []
        for h in range(2):
            for w in range(2):
                x = jnp.concatenate([arrived_ref[d, s, h, w] for d in range(devices)], axis=0)
                xt = x.T
                at = slice(h * fields, (h + 1) * fields)
                left_ref[s, w, at, :total] = xt[:fields]
                left_ref[s, w, at, total:] = xt[fields:]
                turned.append((h, w, xt))
        if s == 0:
            sign_copy.wait()
        sign = sign_ref[0:1, :]
        for h, w, xt in turned:
            at = slice(rows + h * fields, rows + (h + 1) * fields)
            signed = (xt.astype(jnp.float32) * sign).astype(jnp.bfloat16)
            re, im = signed[:fields], signed[fields:]
            left_ref[s, w, at, :total] = im if w else re
            left_ref[s, w, at, total:] = -re if w else im
        if s == 0:
            block(s, 0)
    for i in range(rest_ref.shape[0]):
        load(i).wait()
    for s in range(slots):
        for i in range(s == 0, chunks):
            block(s, i)
        base = slice(s * rows, (s + 1) * rows)
        copy = pltpu.make_async_copy(row_ref.at[base], out_hbm.at[base], out_sems.at[s])
        copy.start()
        stores.append(copy)
    for copy in stores:
        copy.wait()


def fourier_stage(arrived, sign, first, second, rest):
    devices, slots, _, _, pairs, width = arrived.shape
    fields = width // 2
    total = devices * pairs
    rows = slots * 2 * fields
    out = pl.pallas_call(
        fourier_kernel,
        out_shape=jax.ShapeDtypeStruct((rows, NLON), jnp.bfloat16),
        in_specs=[pl.BlockSpec(memory_space=pltpu.VMEM)] * 3 + [pl.BlockSpec(memory_space=pl.ANY)] * 2,
        out_specs=pl.BlockSpec(memory_space=pl.ANY),
        scratch_shapes=[
            pltpu.VMEM((slots, 2, 4 * fields, 2 * total), jnp.bfloat16),
            pltpu.VMEM(rest.shape, jnp.bfloat16),
            pltpu.VMEM(sign.shape, jnp.float32),
            pltpu.VMEM((rows, NLON), jnp.bfloat16),
            pltpu.SemaphoreType.DMA((rest.shape[0],)),
            pltpu.SemaphoreType.DMA,
            pltpu.SemaphoreType.DMA((slots,)),
        ],
        compiler_params=pltpu.CompilerParams(vmem_limit_bytes=16 * 1024 * 1024),
        cost_estimate=pl.CostEstimate(
            flops=16 * rows * total * QUARTER, bytes_accessed=8 * total * QUARTER, transcendentals=0
        ),
        name="fourier",
    )(arrived, first, second, in_hbm(rest), in_hbm(sign))
    return out.reshape(slots, 2, fields, NLON)


def on_device(wave_pairs, band_owner, spectra_even, spectra_odd, legendre_even, legendre_odd):
    devices = lax.axis_size("wave")
    pairs = round_up(wave_pairs.shape[0], ROWS)
    extra = pairs - wave_pairs.shape[0]
    slots = band_owner.shape[0]
    width = spectra_even.shape[2]
    if extra:
        wave_pairs = jnp.pad(wave_pairs, (0, extra))
        spectra_even, spectra_odd, legendre_even, legendre_odd = (
            jnp.pad(a, ((0, extra), (0, 0), (0, 0)))
            for a in (spectra_even, spectra_odd, legendre_even, legendre_odd)
        )

    rest = round_up(pairs + slots, LANES) - pairs - slots
    own = jnp.concatenate([wave_pairs, band_owner, jnp.zeros(rest, jnp.int32)])
    own = jnp.broadcast_to(own, (devices, 1) + own.shape)
    index = lax.all_to_all(own, "wave", 0, 0, tiled=True)[:, 0]
    rows = legendre_stage(wave_pairs, spectra_even, spectra_odd, legendre_even, legendre_odd)
    picked = pick_latitudes(index, rows, devices * slots, pairs)
    index, picked = lax.optimization_barrier((index, picked))
    arrived = lax.all_to_all(picked.reshape(devices, slots, 2, 2, pairs, width), "wave", 0, 0, tiled=True)
    all_pairs = index[:, :pairs].reshape(-1)
    sign = jnp.where(even_wave(all_pairs) % 4 == 0, 1.0, -1.0).astype(jnp.float32)
    sign, all_pairs = lax.optimization_barrier((jnp.broadcast_to(sign, (ROWS,) + sign.shape), all_pairs))
    return fourier_stage(arrived, sign, *wave_tables(all_pairs))


def solution(mesh):
    return jax.shard_map(
        on_device,
        mesh=mesh,
        in_specs=(
            P("wave"),
            P("wave"),
            P("wave", None, "grp"),
            P("wave", None, "grp"),
            P("wave", None, None),
            P("wave", None, None),
        ),
        out_specs=P("wave", None, "grp", None),
        check_vma=False,
    )
```
